512 devices in a mesh: dom: 128 (over x, y, z_lo), edge: 4 (over z_hi, core).
Axes of the slice: x: 4, y: 8, z: 8 (z_hi: 2, z_lo: 4; z = z_hi * 4 + z_lo), core: 2. Of those that a mesh axis runs over, the one named last changes fastest.
Arguments:
- entity: float32 [65536, 400], P('dom'), may hold values from -1.5 to 1.5
- state: float32 [65536], P('dom'), may hold values from 0.01 to 0.5
- relation: float32 [2112, 400], P('edge'), may hold values from 0.5 to 1.5
- edge_head: int32 [2, 128, 4, 512], P(None, 'dom', 'edge'), may hold values from 0 to 511
- edge_rel: int32 [2, 128, 4, 512], P(None, 'dom', 'edge'), may hold values from 0 to 2111
- edge_tail: int32 [2, 128, 4, 512], P(None, 'dom', 'edge'), may hold values from 0 to 511
- negatives: int32 [2, 128, 4, 320], P(None, 'dom', 'edge'), may hold values from 0 to 511
- counts: int32 [2, 128, 4], P(None, 'dom', 'edge'), may hold values from 1 to 512, 1536 in all within a row
- matching: int32 [2, 128], replicated, may hold values from 0 to 127, each once within a row
Outputs:
- updated: float32 [65536, 400], P('dom')
- accum: float32 [65536], P('dom')
The draws below stay inside these ranges and needn't reach their ends.
Inputs may be any that keep to these rules, and one draw needn't show every extreme that they name: `matching`: each row is a permutation of the partitions. The 4 counts of one bucket and partition sum to 1536; the largest is exactly 512.
All inputs are finite; a program needn't handle non-finite values. No bound on the sum of `counts` on one device may be relied on, other than what follows from the above.
Results may differ from the reference program's by a relative error of at most 0.0003.
Values sent between devices are 32-bit elements; how exact they have to be, the bound alone decides.
No kernel may reach another device: no remote copies, remote signals or barrier semaphores. Data moves between devices by JAX's collectives and lax.ppermute only.
A program may use at most 64 MiB of HBM per device.

```python
import math
import jax
import jax.numpy as jnp
import numpy as np
from jax import lax

D = 400
REL = 2112
NEGS = 320
ENT_DEV = 512
SLOTS = 512
ENTITIES = 65536
N_DOM = 128
N_EDGE = 4


def draw_entity(key, part):
    key = jax.random.fold_in(key, 11)
    return 0.3 * jax.random.truncated_normal(key, -5.0, 5.0, (ENTITIES, D), jnp.float32)


def touch_ends(drawn, stream_key, smallest, high):
    longest = drawn.shape.index(max(drawn.shape))
    spots = []
    for shift in (0, 1):
        where = [jax.random.randint(jax.random.fold_in(stream_key, axis), (), 0, length) for axis, length in enumerate(drawn.shape)]
        where[longest] = (where[longest] + shift) % drawn.shape[longest]
        spots.append(tuple(where))
    return drawn.at[spots[0]].set(smallest).at[spots[1]].set(high)


def level_of(own_key, shape, shards, smallest, top_value):
    def one(axis_at, shards_of):
        draws = jax.random.uniform(jax.random.fold_in(jax.random.fold_in(own_key, 6), axis_at), (shards_of,), jnp.float32, smallest / len(shards), top_value / len(shards))
        return jnp.repeat(jnp.exp(draws), shape[axis_at] // shards_of).reshape((-1,) + (1,) * (len(shape) - axis_at - 1))

    gain = one(*shards[0])
    for cut in shards[1:]:
        gain = gain * one(*cut)
    return gain


def cumulative_ranks(count, slope):
    loads = [(1 << 20) // math.isqrt(grade ** slope) + 1 for grade in range(1, count + 1)]
    scale = 1 + sum(loads) // (1 << 30)
    return np.cumsum(np.array([max(1, weight // scale) for weight in loads]))


def ranked(own_key, extent, amount, lean):
    listing = cumulative_ranks(amount, lean)
    lot = jax.random.randint(jax.random.fold_in(own_key, 1), extent, 0, int(listing[amount - 1]))
    standing = jnp.searchsorted(jnp.asarray(listing, jnp.int32), lot, side="right")
    return jax.random.permutation(jax.random.fold_in(own_key, 2), amount)[standing].astype(jnp.int32)


def profile(number_of, total, bound, lean):
    loads = [(1 << 20) // math.isqrt(rank ** lean) + 1 for rank in range(2, number_of + 1)]
    rest, given = total - bound - (number_of - 1), [1] * (number_of - 1)
    while rest > 0:
        movable = [i for i in range(number_of - 1) if given[i] < bound]
        whole, budget = sum([loads[i] for i in movable]), rest
        for i in movable:
            more = min(bound - given[i], max(1, budget * loads[i] // whole), rest)
            given[i] = given[i] + more
            rest = rest - more
    return np.array([bound] + given)


def uneven_parts(own_key, number_of, total, reach, skew):
    if number_of == 2:
        one = jax.random.randint(own_key, (), max(1, total - reach), min(reach, total - 1) + 1)
        return jnp.stack([one, total - one])
    lengths = jnp.asarray(profile(number_of, total, reach, skew), jnp.int32)
    pairs = (number_of - 1) // 2
    donor, sink = lengths[1:1 + 2 * pairs:2], lengths[2:2 + 2 * pairs:2]
    room = jnp.minimum(donor - 1, reach - sink)
    moved = jax.random.randint(jax.random.fold_in(own_key, 1), (pairs,), 0, 1 << 20) % (room + 1)
    lengths = lengths.at[1:1 + 2 * pairs:2].set(donor - moved).at[2:2 + 2 * pairs:2].set(sink + moved)
    return lengths[jax.random.permutation(jax.random.fold_in(own_key, 2), number_of)]


def setup_inputs(seed: int = 0) -> dict:
    streams_of = jax.random.split(jax.random.key(seed), 10)
    return {
        "entity": draw_entity(jax.random.fold_in(streams_of[9], 71), 0),
        "state": jnp.clip(jnp.exp(math.log(0.5) - 3.912023 * jax.random.uniform(streams_of[1], (ENTITIES,), jnp.float32) ** level_of(streams_of[1], (ENTITIES,), ((0, 128),), -0.2, 0.2)), 0.01, 0.5),
        "relation": jnp.clip(0.5 + 1.0 * jax.random.uniform(streams_of[2], (REL, D), jnp.float32) ** level_of(streams_of[2], (REL, D), ((0, 4),), -0.2, 0.2), 0.5, 1.5),
        "edge_head": touch_ends(jax.random.randint(streams_of[3], (2, N_DOM, N_EDGE, SLOTS), 0, ENT_DEV), jax.random.fold_in(streams_of[3], 1), 0, ENT_DEV - 1).astype(jnp.int32),
        "edge_rel": touch_ends(ranked(streams_of[4], (2, N_DOM, N_EDGE, SLOTS), REL, 2), jax.random.fold_in(streams_of[4], 3), 0, REL - 1).astype(jnp.int32),
        "edge_tail": touch_ends(jax.random.randint(streams_of[5], (2, N_DOM, N_EDGE, SLOTS), 0, ENT_DEV), jax.random.fold_in(streams_of[5], 1), 0, ENT_DEV - 1).astype(jnp.int32),
        "negatives": touch_ends(jax.random.randint(streams_of[6], (2, N_DOM, N_EDGE, NEGS), 0, ENT_DEV), jax.random.fold_in(streams_of[6], 1), 0, ENT_DEV - 1).astype(jnp.int32),
        "counts": jax.vmap(lambda own: uneven_parts(own, N_EDGE, 3 * SLOTS, SLOTS, 2))(jax.random.split(streams_of[7], 2 * N_DOM)).reshape((2, N_DOM, N_EDGE)).astype(jnp.int32),
        "matching": jax.vmap(lambda own: jax.random.permutation(own, N_DOM))(jax.random.split(streams_of[8], 2)).reshape((2, N_DOM)).astype(jnp.int32),
    }


learn_rate = 0.1
highest_prec = lax.Precision.HIGHEST

def edge_terms(heads, rel_rows, tails, negs, live_mask):
    left_side = heads * rel_rows
    pos_score = lax.optimization_barrier(jnp.sum(left_side * tails, axis=1))
    neg_scores = jnp.dot(left_side, negs.T, precision=highest_prec)
    row_top = jnp.maximum(pos_score, lax.optimization_barrier(jnp.max(neg_scores, axis=1)))
    weight_pos = jnp.exp(pos_score - row_top)
    weight_neg = jnp.exp(neg_scores - row_top[:, None])
    partition_sum = weight_pos + lax.optimization_barrier(jnp.sum(weight_neg, axis=1))
    grad_pos = jnp.where(live_mask, weight_pos / partition_sum - 1.0, 0.0)
    grad_neg = jnp.where(live_mask[:, None], weight_neg / partition_sum[:, None], 0.0)
    grad_left = grad_pos[:, None] * tails + jnp.dot(grad_neg, negs, precision=highest_prec)
    return (grad_left * rel_rows, grad_pos[:, None] * left_side, jnp.dot(grad_neg.T, left_side, precision=highest_prec))

def reference(entity, state, relation, edge_head, edge_rel, edge_tail, negatives, counts, matching):
    gradient = jnp.zeros(entity.shape, jnp.float32)
    slot_index = jnp.arange(SLOTS, dtype=jnp.int32)
    for bucket in range(2):

        def one_partition(carry, owner):
            partner = matching[bucket, owner]
            head_rows = owner * ENT_DEV + edge_head[bucket, owner]
            tail_rows = partner * ENT_DEV + edge_tail[bucket, owner]
            neg_rows = partner * ENT_DEV + negatives[bucket, owner]
            live_mask = slot_index[None, :] < counts[bucket, owner][:, None]
            grad_heads, grad_tails, grad_negs = jax.vmap(edge_terms)(entity[head_rows], relation[edge_rel[bucket, owner]], entity[tail_rows], entity[neg_rows], live_mask)
            carry = carry.at[head_rows.reshape(-1)].add(grad_heads.reshape(-1, D))
            carry = carry.at[tail_rows.reshape(-1)].add(grad_tails.reshape(-1, D))
            carry = carry.at[neg_rows.reshape(-1)].add(grad_negs.reshape(-1, D))
            return (carry, None)
        gradient, _ = lax.scan(one_partition, gradient, jnp.arange(N_DOM, dtype=jnp.int32))
    accum = state + lax.optimization_barrier(jnp.mean(gradient * gradient, axis=1))
    updated = entity - learn_rate * gradient / jnp.sqrt(accum)[:, None]
    return (updated, accum)
```

```python
import functools

import jax
import jax.numpy as jnp
from jax import lax
from jax.experimental import pallas as pl
from jax.experimental.pallas import tpu as pltpu
from jax.sharding import PartitionSpec as P


LEARN_RATE = 0.1
D = 400
ROWS = 512
HALF = 256
SLOTS = 512
REL_DEV = 528
PIECES = 4
PIECE = 144
PIECE_STEP = 144
PIECE_LAST = REL_DEV - PIECE
TABLE = 2 * REL_DEV + 2 * PIECES * PIECE
LIST = 16
LEG1 = 896
LEG2 = 1664
TAIL0 = 1536
F32 = jnp.float32
BF16 = jnp.bfloat16
VMEM_LIMIT = 40 * 1024 * 1024


def split2(x):
    hi = x.astype(BF16)
    return hi, (x - hi.astype(F32)).astype(BF16)


def split3(x):
    hi = x.astype(BF16)
    rest = x - hi.astype(F32)
    mid = rest.astype(BF16)
    return hi, mid, (rest - mid.astype(F32)).astype(BF16)


def dot_nn(a, b):
    return lax.dot_general(a, b, (((1,), (0,)), ((), ())), preferred_element_type=F32)


def dot_nt(a, b):
    return lax.dot_general(a, b, (((1,), (1,)), ((), ())), preferred_element_type=F32)


def iota(shape, dim):
    return lax.broadcasted_iota(jnp.int32, shape, dim)


def place():
    edge = lax.axis_index("edge")
    return edge // 2, lax.rem(edge, 2)


def onehot_cols(lists, first, count, columns):
    blocks = [(lists[:, first + j : first + j + 1] == columns) for j in range(count)]
    return jnp.concatenate([jnp.where(b, 1.0, 0.0) for b in blocks], axis=0).astype(BF16)


def pack_kernel(entity_ref, head_ref, rel_ref, tail_ref, neg_ref, count_ref, out_ref, lists_ref, rows_ref):
    zh, core = place()
    rows_ref[...] = jnp.full((128, 128), -1.0, F32)
    lane = iota((1, 128), 1)
    for bucket in range(2):
        at = bucket * LIST
        live = count_ref[bucket, 0, 0]
        for j in range(4):
            span = pl.ds(128 * j, 128)
            head = jnp.where(lane + 128 * j < live, head_ref[bucket, 0, 0:1, span], -1)
            rows_ref[at + j : at + j + 1, :] = head.astype(F32)
            rows_ref[at + 4 + j : at + 5 + j, :] = rel_ref[bucket, 0, 0:1, span].astype(F32)
            rows_ref[at + 8 + j : at + 9 + j, :] = tail_ref[bucket, 0, 0:1, span].astype(F32)
        rows_ref[at + 12 : at + 13, :] = neg_ref[bucket, 0, 0:1, 0:128].astype(F32)
        rows_ref[at + 13 : at + 14, :] = neg_ref[bucket, 0, 0:1, 128:256].astype(F32)
        rows_ref[at + 14 : at + 15, 0:64] = neg_ref[bucket, 0, 0:1, 256:320].astype(F32)
    one, two = rows_ref[0:LIST, :], rows_ref[LIST : 2 * LIST, :]
    keep = jnp.where(zh == 0, one, two)
    give = jnp.where(zh == 0, two, one)
    both = jnp.concatenate([keep, give, rows_ref[2 * LIST :, :]], axis=0).T
    lists_ref[...] = both
    start = pl.multiple_of(core * HALF, HALF)
    out_ref[...] = jnp.concatenate(
        [entity_ref[pl.ds(start, 128), :], entity_ref[pl.ds(start + 128, 128), :], both[:, 0 : LEG1 - 2 * D]], axis=1
    )


def route_kernel(x_ref, matching_ref, out_ref):
    zh, _ = place()
    x = x_ref[...]
    parts = split3(x)
    rows = iota((128, 128), 0)
    marks = [jnp.where(matching_ref[b : b + 1, :] == rows, 1.0, 0.0) for b in range(2)]
    back_keep = jnp.where(zh == 0, marks[0], marks[1])
    back_give = jnp.where(zh == 0, marks[1], marks[0])
    fore = back_keep.T.astype(BF16)
    back_keep, back_give = back_keep.astype(BF16), back_give.astype(BF16)
    partner = sum(dot_nn(fore, p) for p in reversed(parts))
    source = sum(dot_nn(back_keep, p) for p in reversed(parts))
    given = sum(dot_nn(back_give, p[:, 768:LEG1]) for p in reversed(parts))
    out_ref[...] = jnp.concatenate(
        [partner[:, 0 : 2 * D], source[:, 0 : 2 * D + LIST], given[:, 48:64], jnp.zeros((128, LEG2 - 4 * D - 2 * LIST), F32)],
        axis=1,
    )


def table_row(rel, zh, core, spot):
    owner = (rel >= REL_DEV).astype(jnp.int32) + (rel >= 2 * REL_DEV).astype(jnp.int32)
    owner = owner + (rel >= 3 * REL_DEV).astype(jnp.int32)
    off = rel - REL_DEV * owner
    owner_zh = (owner >= 2).astype(jnp.int32)
    other_core = (owner - 2 * owner_zh) != core
    piece = (off >= PIECE_STEP).astype(jnp.int32) + (off >= 2 * PIECE_STEP).astype(jnp.int32)
    piece = piece + (off >= 3 * PIECE_STEP).astype(jnp.int32)
    start = jnp.minimum(PIECE_STEP * piece, PIECE_LAST)
    slot = spot - piece
    slot = jnp.where(slot < 0, slot + PIECES, slot)
    near = jnp.where(other_core, REL_DEV, 0) + off
    far = 2 * REL_DEV + jnp.where(other_core, PIECES * PIECE, 0) + slot * PIECE + off - start
    return jnp.where(owner_zh == zh, near, far)


def spot_of_device():
    return lax.axis_index("dom") // 32


def left_kernel(
    entity_ref, mine_ref, theirs_ref, near_ref, near2_ref, far_ref, far2_ref, rel_out, left_hi, left_lo, table_hi, table_lo
):
    zh, core = place()
    spot = spot_of_device()
    at = 0
    for ref in (near_ref, near2_ref, far_ref, far2_ref):
        count = ref.shape[0]
        hi, lo = split2(ref[...])
        table_hi[at : at + count, :] = hi
        table_lo[at : at + count, :] = lo
        at += count
    entity_hi, entity_lo = split2(entity_ref[...])
    own = iota((128, ROWS), 1).astype(F32)
    table_at = iota((128, TABLE), 1)
    for k in range(2):
        lists = (mine_ref[:, 0:LIST], theirs_ref[:, LIST : 2 * LIST])[k]
        heads = onehot_cols(lists, 0, 4, own)
        head_rows = dot_nn(heads, entity_hi) + dot_nn(heads, entity_lo)
        rel_at = table_row(lists[:, 4:8].astype(jnp.int32), zh, core, spot)
        rels = onehot_cols(rel_at, 0, 4, table_at)
        rel_rows = dot_nn(rels, table_hi[...]) + dot_nn(rels, table_lo[...])
        hi, lo = split2(head_rows * rel_rows)
        span = pl.ds(k * SLOTS, SLOTS)
        rel_out[span, :] = rel_rows
        left_hi[span, :] = hi
        left_lo[span, :] = lo


def fill_block(hi_ref, lo_ref, mine_ref, theirs_ref, first):
    for k, (ref, lane) in enumerate(((mine_ref, 0), (mine_ref, D), (theirs_ref, 0), (theirs_ref, D))):
        hi, lo = split2(ref[:, first + lane : first + lane + D])
        hi_ref[128 * k : 128 * (k + 1), :] = hi
        lo_ref[128 * k : 128 * (k + 1), :] = lo


def lists_rows(lists):
    return jnp.concatenate([lists, jnp.zeros((128, 128 - LIST), F32)], axis=1).T


def head_kernel(mine_ref, theirs_ref, lists_mine, lists_theirs, rel_ref, left_hi, left_lo, grad_ref, block_hi, block_lo):
    _, core = place()
    fill_block(block_hi, block_lo, mine_ref, theirs_ref, 0)
    numbers = jnp.bitwise_xor(iota((128, ROWS), 1), core * HALF).astype(F32)
    heads_at = iota((ROWS, 128), 0).astype(F32)
    total = None
    for k in range(2):
        lists = (lists_mine[:, 0:LIST], lists_theirs[:, LIST : 2 * LIST])[k]
        span = pl.ds(k * SLOTS, SLOTS)
        hi, lo = left_hi[span, :], left_lo[span, :]
        b_hi, b_lo = block_hi[...], block_lo[...]
        scores = dot_nt(hi, b_lo) + dot_nt(lo, b_hi) + dot_nt(hi, b_hi)
        tails = jnp.concatenate(
            [jnp.where(lists[:, 8 + j : 9 + j] == numbers, 1.0, 0.0) for j in range(4)], axis=0
        )
        drawn = sum(jnp.where(lists[:, 12 + j : 13 + j] == numbers, 1.0, 0.0) for j in range(3))
        times = jnp.sum(drawn, axis=0, keepdims=True) + tails
        scores = jnp.where(times > 0.0, scores, -3.0e38)
        weights = times * jnp.exp(scores - jnp.max(scores, axis=1, keepdims=True))
        weights = weights / jnp.sum(weights, axis=1, keepdims=True) - tails
        w_hi, w_lo = split2(weights)
        grad_left = dot_nn(w_hi, b_lo) + dot_nn(w_lo, b_hi) + dot_nn(w_hi, b_hi)
        g_hi, g_lo = split2(grad_left * rel_ref[span, :])
        rows = lists_rows(lists)
        marks = jnp.concatenate(
            [jnp.where(rows[j : j + 1, :] == heads_at, 1.0, 0.0) for j in range(4)], axis=1
        ).astype(BF16)
        part = dot_nn(marks, g_lo) + dot_nn(marks, g_hi)
        total = part if total is None else total + part
    grad_ref[...] = total


def tail_kernel(
    mine_ref, theirs_ref, given_ref, entity_ref, table_hi, table_lo, head_grad, keep_ref, send_ref, block_hi, block_lo, sum_ref
):
    zh, core = place()
    spot = spot_of_device()
    fill_block(block_hi, block_lo, mine_ref, theirs_ref, 2 * D)
    e_hi, e_lo = split2(entity_ref[...])
    numbers = jnp.bitwise_xor(iota((128, ROWS), 1), core * HALF).astype(F32)
    rows_at = iota((ROWS, 128), 0).astype(F32)
    table_at = iota((128, TABLE), 1)
    total = head_grad[...]
    for k in range(2):
        if k == 0:
            lists = mine_ref[:, 4 * D : 4 * D + LIST]
        else:
            lists = given_ref[:, 4 * D + LIST - TAIL0 : 4 * D + 2 * LIST - TAIL0]
        heads = onehot_cols(lists, 0, 4, numbers)
        head_rows = dot_nn(heads, block_hi[...]) + dot_nn(heads, block_lo[...])
        rel_at = table_row(lists[:, 4:8].astype(jnp.int32), zh, core, spot)
        rels = onehot_cols(rel_at, 0, 4, table_at)
        rel_rows = dot_nn(rels, table_hi[...]) + dot_nn(rels, table_lo[...])
        l_hi, l_lo = split2(head_rows * rel_rows)
        scores = dot_nt(e_lo, l_hi) + dot_nt(e_hi, l_lo) + dot_nt(e_hi, l_hi)
        rows = lists_rows(lists)
        tails = jnp.concatenate(
            [jnp.where(rows[8 + j : 9 + j, :] == rows_at, 1.0, 0.0) for j in range(4)], axis=1
        )
        drawn = sum(jnp.where(rows[12 + j : 13 + j, :] == rows_at, 1.0, 0.0) for j in range(3))
        times = jnp.sum(drawn, axis=1, keepdims=True) + tails
        scores = jnp.where(times > 0.0, scores, -3.0e38)
        weights = times * jnp.exp(scores - jnp.max(scores, axis=0, keepdims=True))
        weights = weights / jnp.sum(weights, axis=0, keepdims=True) - tails
        w_hi, w_lo = split2(weights)
        total = total + (dot_nn(w_lo, l_hi) + dot_nn(w_hi, l_lo) + dot_nn(w_hi, l_hi))
    sum_ref[...] = total
    keep_ref[...] = sum_ref[pl.ds(pl.multiple_of(core * HALF, HALF), HALF), :]
    send_ref[...] = sum_ref[pl.ds(pl.multiple_of((1 - core) * HALF, HALF), HALF), :]


def update_kernel(mine_ref, theirs_ref, entity_ref, state_ref, updated_ref, accum_ref):
    _, core = place()
    lane = iota((128, 128), 1)
    state = jnp.concatenate([state_ref[...], jnp.zeros((124, 128), F32)], axis=0).T
    accums = jnp.zeros((128, 128), F32)
    for j in range(4):
        a = mine_ref[128 * (j % 2) : 128 * (j % 2) + 128, :]
        b = theirs_ref[128 * (j % 2) : 128 * (j % 2) + 128, :]
        gradient = jnp.where(core == j // 2, a, b)
        accum = state[:, j : j + 1] + jnp.sum(gradient * gradient, axis=1, keepdims=True) / float(D)
        accums = jnp.where(lane == j, accum, accums)
        span = slice(128 * j, 128 * j + 128)
        updated_ref[span, :] = entity_ref[span, :] - LEARN_RATE * gradient / jnp.sqrt(accum)
    accum_ref[...] = accums.T[0:4, :]


def call(kernel, out_shape, args, scratch=(), cost=None, smem=()):
    out_shape = jax.tree.map(lambda s: jax.ShapeDtypeStruct(*s), out_shape, is_leaf=lambda s: isinstance(s, tuple))
    specs = [
        pl.BlockSpec(memory_space=pltpu.SMEM if i in smem else pltpu.VMEM) for i in range(len(args))
    ]
    return pl.pallas_call(
        kernel,
        out_shape=out_shape,
        in_specs=specs,
        out_specs=jax.tree.map(lambda _: pl.BlockSpec(memory_space=pltpu.VMEM), out_shape),
        scratch_shapes=list(scratch),
        compiler_params=pltpu.CompilerParams(vmem_limit_bytes=VMEM_LIMIT),
        cost_estimate=cost,
        name=kernel.__name__,
    )(*args)


def flops(us):
    return pl.CostEstimate(flops=int(us * 1.0e9), bytes_accessed=4_000_000, transcendentals=0)


def shards(entity, state, relation, edge_head, edge_rel, edge_tail, negatives, counts, matching):
    edge = lax.axis_index("edge")
    doms = lax.axis_size("dom")
    spot = spot_of_device()
    swap_core = functools.partial(lax.ppermute, axis_name="edge", perm=[(0, 1), (1, 0), (2, 3), (3, 2)])
    swap_zh = functools.partial(lax.ppermute, axis_name="edge", perm=[(0, 2), (2, 0), (1, 3), (3, 1)])

    payload, lists = call(
        pack_kernel,
        [((128, LEG1), F32), ((128, 128), F32)],
        (entity, edge_head, edge_rel, edge_tail, negatives, counts),
        scratch=[pltpu.VMEM((128, 128), F32)],
        smem=(5,),
    )
    spread = lax.all_to_all(payload, "dom", split_axis=0, concat_axis=0, tiled=True)
    lists_other = swap_zh(lists)

    start = jnp.minimum(PIECE_STEP * spot, PIECE_LAST)
    piece = swap_zh(lax.dynamic_slice_in_dim(relation, start, PIECE, axis=0))
    far = [piece]
    for shift in range(1, PIECES):
        far.append(lax.ppermute(piece, "dom", perm=[(d, (d + 32 * shift) % doms) for d in range(doms)]))
    far = jnp.concatenate(far, axis=0)
    near2 = swap_core(relation)
    far2 = swap_core(far)

    routed = call(route_kernel, ((128, LEG2), F32), (spread, matching))
    fetched = lax.all_to_all(routed, "dom", split_axis=0, concat_axis=0, tiled=True)
    rel_rows, left_hi, left_lo, table_hi, table_lo = call(
        left_kernel,
        [
            ((2 * SLOTS, D), F32),
            ((2 * SLOTS, D), BF16),
            ((2 * SLOTS, D), BF16),
            ((TABLE, D), BF16),
            ((TABLE, D), BF16),
        ],
        (entity, lists, lists_other, relation, near2, far, far2),
        cost=flops(15),
    )
    fetched_other = swap_core(fetched)
    given = swap_zh(fetched[:, TAIL0:LEG2])
    block = [pltpu.VMEM((ROWS, D), BF16), pltpu.VMEM((ROWS, D), BF16)]
    head_grad = call(
        head_kernel,
        ((ROWS, D), F32),
        (fetched, fetched_other, lists, lists_other, rel_rows, left_hi, left_lo),
        scratch=block,
        cost=flops(8),
    )
    keep, send = call(
        tail_kernel,
        [((HALF, D), F32), ((HALF, D), F32)],
        (fetched, fetched_other, given, entity, table_hi, table_lo, head_grad),
        scratch=block + [pltpu.VMEM((ROWS, D), F32)],
        cost=flops(10),
    )
    half = keep + swap_core(send)
    half = half + swap_zh(half)
    other = swap_core(half)
    updated, accum = call(
        update_kernel,
        [((ROWS, D), F32), ((4, 128), F32)],
        (half, other, entity, state.reshape(4, 128)),
    )
    return updated, accum.reshape(ROWS)


def solution(mesh):
    return jax.shard_map(
        shards,
        mesh=mesh,
        in_specs=(
            P("dom", None),
            P("dom"),
            P("edge", None),
            P(None, "dom", "edge", None),
            P(None, "dom", "edge", None),
            P(None, "dom", "edge", None),
            P(None, "dom", "edge", None),
            P(None, "dom", "edge"),
            P(),
        ),
        out_specs=(P("dom", None), P("dom")),
        check_vma=False,
    )
```

```python
import functools

import jax
import jax.numpy as jnp
from jax import lax
from jax.experimental import pallas as pl
from jax.experimental.pallas import tpu as pltpu
from jax.sharding import PartitionSpec as P


LEARN_RATE = 0.1
D = 400
ROWS = 512
HALF = 256
SLOTS = 512
REL_DEV = 528
PIECES = 4
PIECE = 112
TABLE = 4 * REL_DEV
FAR = 640
LIST = 16
LEG1 = 896
LEG2 = 1664
TAIL0 = 1536
F32 = jnp.float32
BF16 = jnp.bfloat16
VMEM_LIMIT = 40 * 1024 * 1024


def split2(x):
    hi = x.astype(BF16)
    return hi, (x - hi.astype(F32)).astype(BF16)


def split3(x):
    hi = x.astype(BF16)
    rest = x - hi.astype(F32)
    mid = rest.astype(BF16)
    return hi, mid, (rest - mid.astype(F32)).astype(BF16)


def dot_nn(a, b):
    return lax.dot_general(a, b, (((1,), (0,)), ((), ())), preferred_element_type=F32)


def dot_nt(a, b):
    return lax.dot_general(a, b, (((1,), (1,)), ((), ())), preferred_element_type=F32)


def iota(shape, dim):
    return lax.broadcasted_iota(jnp.int32, shape, dim)


def place():
    edge = lax.axis_index("edge")
    return edge // 2, lax.rem(edge, 2)


def onehot_cols(lists, first, count, columns):
    blocks = [(lists[:, first + j : first + j + 1] == columns) for j in range(count)]
    return jnp.concatenate([jnp.where(b, 1.0, 0.0) for b in blocks], axis=0).astype(BF16)


def pack_kernel(entity_ref, head_ref, rel_ref, tail_ref, neg_ref, count_ref, out_ref, cols_ref, give_ref, rows_ref):
    zh, core = place()
    rows_ref[...] = jnp.full((128, 128), -1.0, F32)
    lane = iota((1, 128), 1)
    for bucket in range(2):
        at = bucket * LIST
        live = count_ref[bucket, 0, 0]
        for j in range(4):
            span = pl.ds(128 * j, 128)
            head = jnp.where(lane + 128 * j < live, head_ref[bucket, 0, 0:1, span], -1)
            rows_ref[at + j : at + j + 1, :] = head.astype(F32)
            rows_ref[at + 4 + j : at + 5 + j, :] = rel_ref[bucket, 0, 0:1, span].astype(F32)
            rows_ref[at + 8 + j : at + 9 + j, :] = tail_ref[bucket, 0, 0:1, span].astype(F32)
        rows_ref[at + 12 : at + 13, :] = neg_ref[bucket, 0, 0:1, 0:128].astype(F32)
        rows_ref[at + 13 : at + 14, :] = neg_ref[bucket, 0, 0:1, 128:256].astype(F32)
        rows_ref[at + 14 : at + 15, 0:64] = neg_ref[bucket, 0, 0:1, 256:320].astype(F32)
    one, two = rows_ref[0:LIST, :], rows_ref[LIST : 2 * LIST, :]
    keep = jnp.where(zh == 0, one, two)
    give = jnp.where(zh == 0, two, one)
    both = jnp.concatenate([keep, give, rows_ref[2 * LIST :, :]], axis=0).T
    cols_ref[...] = both
    give_ref[...] = give
    half = jnp.where(core == 0, entity_ref[:, 0:HALF], entity_ref[:, HALF:ROWS]).T
    out_ref[:, 0, :] = jnp.concatenate([half[0:128, :], half[128:HALF, :], both[:, 0 : LEG1 - 2 * D]], axis=1)


def route_kernel(x_ref, matching_ref, out_ref):
    zh, _ = place()
    parts = split3(x_ref[:, 0, :])
    rows = iota((128, 128), 0)
    marks = [jnp.where(matching_ref[b : b + 1, :] == rows, 1.0, 0.0) for b in range(2)]
    back_keep = jnp.where(zh == 0, marks[0], marks[1])
    back_give = jnp.where(zh == 0, marks[1], marks[0])
    fore = back_keep.T.astype(BF16)
    back_keep, back_give = back_keep.astype(BF16), back_give.astype(BF16)
    partner = sum(dot_nn(fore, p) for p in reversed(parts))
    source = sum(dot_nn(back_keep, p) for p in reversed(parts))
    given = sum(dot_nn(back_give, p[:, 768:LEG1]) for p in reversed(parts))
    out_ref[:, 0, :] = jnp.concatenate(
        [partner[:, 0 : 2 * D], source[:, 0 : 2 * D + LIST], given[:, 48:64], jnp.zeros((128, LEG2 - 4 * D - 2 * LIST), F32)],
        axis=1,
    )


def table_row(rel, zh, core):
    owner = (rel >= REL_DEV).astype(jnp.int32) + (rel >= 2 * REL_DEV).astype(jnp.int32)
    owner = owner + (rel >= 3 * REL_DEV).astype(jnp.int32)
    off = rel - REL_DEV * owner
    owner_zh = (owner >= 2).astype(jnp.int32)
    other_core = (owner - 2 * owner_zh) != core
    return jnp.where(owner_zh == zh, 0, 2 * REL_DEV) + jnp.where(other_core, REL_DEV, 0) + off


def piece_start(spot):
    return pl.multiple_of(jnp.minimum(PIECE * spot, D - PIECE), 16)


def spot_of_device():
    return lax.axis_index("dom") // 32


def bundle_kernel(relation_ref, give_ref, out_ref):
    out_ref[0:PIECE, :] = relation_ref[pl.ds(piece_start(spot_of_device()), PIECE), :]
    out_ref[PIECE : PIECE + LIST, :] = jnp.zeros((LIST, REL_DEV), F32)
    out_ref[PIECE : PIECE + LIST, 0:128] = give_ref[...]


def table_kernel(relation_ref, piece0_ref, piece1_ref, piece2_ref, piece3_ref, out_ref):
    spot = spot_of_device()
    out_ref[:, 0:REL_DEV] = relation_ref[...]
    out_ref[:, REL_DEV:FAR] = jnp.zeros((D, FAR - REL_DEV), F32)
    for shift, ref in enumerate((piece0_ref, piece1_ref, piece2_ref, piece3_ref)):
        origin = jnp.where(spot < shift, spot - shift + PIECES, spot - shift)
        out_ref[pl.ds(piece_start(origin), PIECE), FAR : FAR + REL_DEV] = ref[0:PIECE, :]


def gather_relations(lists, zh, core, table_hi, table_lo):
    rel_at = table_row(lists[:, 4:8].astype(jnp.int32), zh, core)
    rels = onehot_cols(rel_at, 0, 4, iota((128, TABLE), 1))
    return dot_nn(rels, table_hi[...]) + dot_nn(rels, table_lo[...])


def left_kernel(
    entity_ref, cols_ref, bundle_ref, mine_ref, theirs_ref,
    rel_out, left_hi, left_lo, table_hi, table_lo, entity_hi, entity_lo, cols_out,
):
    zh, core = place()
    for k, (ref, first) in enumerate(((mine_ref, 0), (theirs_ref, 0), (mine_ref, FAR), (theirs_ref, FAR))):
        hi, lo = split2(ref[:, first : first + REL_DEV].T)
        table_hi[k * REL_DEV : (k + 1) * REL_DEV, :] = hi
        table_lo[k * REL_DEV : (k + 1) * REL_DEV, :] = lo
    hi, lo = split2(entity_ref[...].T)
    entity_hi[...] = hi
    entity_lo[...] = lo
    own = iota((128, ROWS), 1).astype(F32)
    theirs = jnp.concatenate([bundle_ref[PIECE : PIECE + LIST, 0:128], jnp.zeros((128 - LIST, 128), F32)], axis=0).T
    cols_out[...] = theirs
    for k, lists in enumerate((cols_ref[:, 0:LIST], theirs[:, 0:LIST])):
        heads = onehot_cols(lists, 0, 4, own)
        head_rows = dot_nn(heads, hi) + dot_nn(heads, lo)
        rel_rows = gather_relations(lists, zh, core, table_hi, table_lo)
        l_hi, l_lo = split2(head_rows * rel_rows)
        span = pl.ds(k * SLOTS, SLOTS)
        rel_out[span, :] = rel_rows
        left_hi[span, :] = l_hi
        left_lo[span, :] = l_lo


def fill_block(hi_ref, lo_ref, mine_ref, theirs_ref, first):
    for k, (ref, lane) in enumerate(((mine_ref, 0), (mine_ref, D), (theirs_ref, 0), (theirs_ref, D))):
        hi, lo = split2(ref[:, 0, first + lane : first + lane + D])
        hi_ref[128 * k : 128 * (k + 1), :] = hi
        lo_ref[128 * k : 128 * (k + 1), :] = lo


def lists_rows(lists):
    return jnp.concatenate([lists, jnp.zeros((128, 128 - LIST), F32)], axis=1).T


def head_kernel(mine_ref, theirs_ref, lists_mine, lists_theirs, rel_ref, left_hi, left_lo, grad_ref, block_hi, block_lo):
    _, core = place()
    fill_block(block_hi, block_lo, mine_ref, theirs_ref, 0)
    numbers = jnp.bitwise_xor(iota((128, ROWS), 1), core * HALF).astype(F32)
    heads_at = iota((ROWS, 128), 0).astype(F32)
    total = None
    for k in range(2):
        lists = (lists_mine, lists_theirs)[k][:, 0:LIST]
        span = pl.ds(k * SLOTS, SLOTS)
        hi, lo = left_hi[span, :], left_lo[span, :]
        b_hi, b_lo = block_hi[...], block_lo[...]
        scores = dot_nt(hi, b_lo) + dot_nt(lo, b_hi) + dot_nt(hi, b_hi)
        tails = jnp.concatenate(
            [jnp.where(lists[:, 8 + j : 9 + j] == numbers, 1.0, 0.0) for j in range(4)], axis=0
        )
        drawn = sum(jnp.where(lists[:, 12 + j : 13 + j] == numbers, 1.0, 0.0) for j in range(3))
        times = jnp.sum(drawn, axis=0, keepdims=True) + tails
        scores = jnp.where(times > 0.0, scores, -3.0e38)
        weights = times * jnp.exp(scores - jnp.max(scores, axis=1, keepdims=True))
        weights = weights / jnp.sum(weights, axis=1, keepdims=True) - tails
        w_hi, w_lo = split2(weights)
        grad_left = dot_nn(w_hi, b_lo) + dot_nn(w_lo, b_hi) + dot_nn(w_hi, b_hi)
        g_hi, g_lo = split2(grad_left * rel_ref[span, :])
        rows = lists_rows(lists)
        marks = jnp.concatenate(
            [jnp.where(rows[j : j + 1, :] == heads_at, 1.0, 0.0) for j in range(4)], axis=1
        ).astype(BF16)
        part = dot_nn(marks, g_lo) + dot_nn(marks, g_hi)
        total = part if total is None else total + part
    grad_ref[...] = total


def first_relations_kernel(mine_ref, table_hi, table_lo, rel_ref):
    zh, core = place()
    rel_ref[...] = gather_relations(mine_ref[:, 0, 4 * D : 4 * D + LIST], zh, core, table_hi, table_lo)


def tail_kernel(
    mine_ref, theirs_ref, given_ref, rel_ref, entity_hi, entity_lo, table_hi, table_lo, head_grad,
    keep_ref, send_ref, block_hi, block_lo,
):
    zh, core = place()
    fill_block(block_hi, block_lo, mine_ref, theirs_ref, 2 * D)
    e_hi, e_lo = entity_hi[...], entity_lo[...]
    numbers = jnp.bitwise_xor(iota((128, ROWS), 1), core * HALF).astype(F32)
    rows_at = iota((ROWS, 128), 0).astype(F32)
    total = head_grad[...]
    for k in range(2):
        if k == 0:
            lists = mine_ref[:, 0, 4 * D : 4 * D + LIST]
            rel_rows = rel_ref[...]
        else:
            lists = given_ref[:, 0, 4 * D + LIST - TAIL0 : 4 * D + 2 * LIST - TAIL0]
            rel_rows = gather_relations(lists, zh, core, table_hi, table_lo)
        heads = onehot_cols(lists, 0, 4, numbers)
        head_rows = dot_nn(heads, block_hi[...]) + dot_nn(heads, block_lo[...])
        l_hi, l_lo = split2(head_rows * rel_rows)
        scores = dot_nt(e_lo, l_hi) + dot_nt(e_hi, l_lo) + dot_nt(e_hi, l_hi)
        rows = lists_rows(lists)
        tails = jnp.concatenate(
            [jnp.where(rows[8 + j : 9 + j, :] == rows_at, 1.0, 0.0) for j in range(4)], axis=1
        )
        drawn = sum(jnp.where(rows[12 + j : 13 + j, :] == rows_at, 1.0, 0.0) for j in range(3))
        times = jnp.sum(drawn, axis=1, keepdims=True) + tails
        scores = jnp.where(times > 0.0, scores, -3.0e38)
        weights = times * jnp.exp(scores - jnp.max(scores, axis=0, keepdims=True))
        weights = weights / jnp.sum(weights, axis=0, keepdims=True) - tails
        w_hi, w_lo = split2(weights)
        total = total + (dot_nn(w_lo, l_hi) + dot_nn(w_hi, l_lo) + dot_nn(w_hi, l_hi))
    first, second = total[0:HALF, :].T, total[HALF:ROWS, :].T
    keep_ref[...] = jnp.where(core == 0, first, second)
    send_ref[...] = jnp.where(core == 0, second, first)


def update_kernel(mine_ref, theirs_ref, entity_ref, state_ref, updated_ref, accum_ref):
    _, core = place()
    mine, theirs = mine_ref[...], theirs_ref[...]
    for j, gradient in enumerate((jnp.where(core == 0, mine, theirs), jnp.where(core == 0, theirs, mine))):
        span = slice(HALF * j, HALF * (j + 1))
        accum = state_ref[:, span] + jnp.sum(gradient * gradient, axis=0, keepdims=True) / float(D)
        accum_ref[:, span] = accum
        updated_ref[:, span] = entity_ref[:, span] - LEARN_RATE * gradient / jnp.sqrt(accum)


def call(kernel, out_shape, args, scratch=(), cost=None, smem=()):
    out_shape = jax.tree.map(lambda s: jax.ShapeDtypeStruct(*s), out_shape, is_leaf=lambda s: isinstance(s, tuple))
    specs = [
        pl.BlockSpec(memory_space=pltpu.SMEM if i in smem else pltpu.VMEM) for i in range(len(args))
    ]
    return pl.pallas_call(
        kernel,
        out_shape=out_shape,
        in_specs=specs,
        out_specs=jax.tree.map(lambda _: pl.BlockSpec(memory_space=pltpu.VMEM), out_shape),
        scratch_shapes=list(scratch),
        compiler_params=pltpu.CompilerParams(vmem_limit_bytes=VMEM_LIMIT),
        cost_estimate=cost,
        name=kernel.__name__,
    )(*args)


def flops(us):
    return pl.CostEstimate(flops=int(us * 1.0e9), bytes_accessed=4_000_000, transcendentals=0)


def shards(entity, state, relation, edge_head, edge_rel, edge_tail, negatives, counts, matching):
    doms = lax.axis_size("dom")
    swap_core = functools.partial(lax.ppermute, axis_name="edge", perm=[(0, 1), (1, 0), (2, 3), (3, 2)])
    swap_zh = functools.partial(lax.ppermute, axis_name="edge", perm=[(0, 2), (2, 0), (1, 3), (3, 1)])
    entity_t, relation_t = entity.T, relation.T

    payload, cols, give = call(
        pack_kernel,
        [((128, 1, LEG1), F32), ((128, 128), F32), ((LIST, 128), F32)],
        (entity_t, edge_head, edge_rel, edge_tail, negatives, counts),
        scratch=[pltpu.VMEM((128, 128), F32)],
        smem=(5,),
    )
    spread = lax.all_to_all(payload, "dom", split_axis=0, concat_axis=0, tiled=True)

    bundle = call(bundle_kernel, ((PIECE + LIST, REL_DEV), F32), (relation_t, give))
    bundle = swap_zh(bundle)
    pieces = [bundle]
    for shift in range(1, PIECES):
        pieces.append(lax.ppermute(bundle, "dom", perm=[(d, (d + 32 * shift) % doms) for d in range(doms)]))
    spread, bundle = lax.optimization_barrier((spread, bundle))

    routed = call(route_kernel, ((128, 1, LEG2), F32), (spread, matching))
    fetched = lax.all_to_all(routed, "dom", split_axis=0, concat_axis=0, tiled=True)
    table = call(table_kernel, ((D, FAR + REL_DEV), F32), (relation_t, *pieces))
    table_other = swap_core(table)
    prepared = call(
        left_kernel,
        [
            ((2 * SLOTS, D), F32),
            ((2 * SLOTS, D), BF16),
            ((2 * SLOTS, D), BF16),
            ((TABLE, D), BF16),
            ((TABLE, D), BF16),
            ((ROWS, D), BF16),
            ((ROWS, D), BF16),
            ((128, 128), F32),
        ],
        (entity_t, cols, bundle, table, table_other),
        cost=flops(8),
    )
    fetched, prepared = lax.optimization_barrier((fetched, prepared))
    rel_rows, left_hi, left_lo, table_hi, table_lo, entity_hi, entity_lo, cols_other = prepared
    fetched_other = swap_core(fetched)
    given = swap_zh(fetched[:, :, TAIL0:LEG2])
    first_rel = call(first_relations_kernel, ((SLOTS, D), F32), (fetched, table_hi, table_lo), cost=flops(3))
    fetched_other, first_rel = lax.optimization_barrier((fetched_other, first_rel))
    block = [pltpu.VMEM((ROWS, D), BF16), pltpu.VMEM((ROWS, D), BF16)]
    head_grad = call(
        head_kernel,
        ((ROWS, D), F32),
        (fetched, fetched_other, cols, cols_other, rel_rows, left_hi, left_lo),
        scratch=block,
        cost=flops(6),
    )
    keep, send = call(
        tail_kernel,
        [((D, HALF), F32), ((D, HALF), F32)],
        (fetched, fetched_other, given, first_rel, entity_hi, entity_lo, table_hi, table_lo, head_grad),
        scratch=block,
        cost=flops(9),
    )
    half = keep + swap_core(send)
    half = half + swap_zh(half)
    other = swap_core(half)
    updated, accum = call(
        update_kernel,
        [((D, ROWS), F32), ((1, ROWS), F32)],
        (half, other, entity_t, state.reshape(1, ROWS)),
    )
    return updated.T, accum.reshape(ROWS)


def solution(mesh):
    return jax.shard_map(
        shards,
        mesh=mesh,
        in_specs=(
            P("dom", None),
            P("dom"),
            P("edge", None),
            P(None, "dom", "edge", None),
            P(None, "dom", "edge", None),
            P(None, "dom", "edge", None),
            P(None, "dom", "edge", None),
            P(None, "dom", "edge"),
            P(),
        ),
        out_specs=(P("dom", None), P("dom")),
        check_vma=False,
    )
```

```python
import functools

import jax
import jax.numpy as jnp
from jax import lax
from jax.experimental import pallas as pl
from jax.experimental.pallas import tpu as pltpu
from jax.sharding import PartitionSpec as P


LEARN_RATE = 0.1
D = 400
ROWS = 512
HALF = 256
SLOTS = 512
NEGS = 320
REL_DEV = 528
PIECES = 4
PIECE = 112
REL_LANES = 640
TABLE = 4 * REL_DEV
LIST = 16
CHUNK1 = 7
CHUNK2 = 13
GIVEN_CHUNK = 12
FIRST = 4 * D - 128 * GIVEN_CHUNK
F32 = jnp.float32
BF16 = jnp.bfloat16
MIB = 1024 * 1024


def split2(x):
    hi = x.astype(BF16)
    return hi, (x - hi.astype(F32)).astype(BF16)


def split3(x):
    hi = x.astype(BF16)
    rest = x - hi.astype(F32)
    mid = rest.astype(BF16)
    return hi, mid, (rest - mid.astype(F32)).astype(BF16)


def dot_nn(a, b):
    return lax.dot_general(a, b, (((1,), (0,)), ((), ())), preferred_element_type=F32)


def dot_nt(a, b):
    return lax.dot_general(a, b, (((1,), (1,)), ((), ())), preferred_element_type=F32)


def iota(shape, dim):
    return lax.broadcasted_iota(jnp.int32, shape, dim)


def place():
    return lax.axis_index("zh"), lax.axis_index("core")


def read_rows(ref, chunks):
    return jnp.concatenate([ref[pl.ds(k, 128, stride=chunks), :] for k in range(chunks)], axis=1)


def write_rows(ref, value, chunks):
    for k in range(chunks):
        ref[pl.ds(k, 128, stride=chunks), :] = value[:, 128 * k : 128 * (k + 1)]


def onehot_cols(lists, first, count, columns):
    blocks = [(lists[:, first + j : first + j + 1] == columns) for j in range(count)]
    return jnp.concatenate([jnp.where(b, 1.0, 0.0) for b in blocks], axis=0).astype(BF16)


def pack_kernel(
    entity_hbm, head_hbm, rel_hbm, tail_hbm, neg_hbm, count_hbm, out_ref, cols_ref, give_ref,
    rows_ref, entity_ref, head_ref, rel_ref, tail_ref, neg_ref, count_ref, sems,
):
    zh, core = place()
    pairs = (
        (head_hbm, head_ref), (rel_hbm, rel_ref), (tail_hbm, tail_ref), (neg_hbm, neg_ref), (count_hbm, count_ref),
        (entity_hbm, entity_ref),
    )
    copies = [pltpu.make_async_copy(a, b, sems.at[i]) for i, (a, b) in enumerate(pairs)]
    for copy in copies:
        copy.start()
    rows_ref[...] = jnp.full((128, 128), -1.0, F32)
    lane = iota((1, 128), 1)
    for copy in copies[:-1]:
        copy.wait()
    for bucket in range(2):
        at = bucket * LIST
        live = count_ref[bucket]
        for j in range(4):
            span = pl.ds(128 * j, 128)
            head = jnp.where(lane + 128 * j < live, head_ref[bucket, 0, 0:1, span], -1)
            rows_ref[at + j : at + j + 1, :] = head.astype(F32)
            rows_ref[at + 4 + j : at + 5 + j, :] = rel_ref[bucket, 0, 0:1, span].astype(F32)
            rows_ref[at + 8 + j : at + 9 + j, :] = tail_ref[bucket, 0, 0:1, span].astype(F32)
        rows_ref[at + 12 : at + 13, :] = neg_ref[bucket, 0, 0:1, 0:128].astype(F32)
        rows_ref[at + 13 : at + 14, :] = neg_ref[bucket, 0, 0:1, 128:256].astype(F32)
        rows_ref[at + 14 : at + 15, 0:64] = neg_ref[bucket, 0, 0:1, 256:320].astype(F32)
    one, two = rows_ref[0:LIST, :], rows_ref[LIST : 2 * LIST, :]
    keep = jnp.where(zh == 0, one, two)
    give = jnp.where(zh == 0, two, one)
    both = jnp.concatenate([keep, give, rows_ref[2 * LIST :, :]], axis=0).T
    cols_ref[...] = both
    give_ref[...] = give
    copies[-1].wait()
    half = jnp.where(core == 0, entity_ref[:, 0:HALF], entity_ref[:, HALF:ROWS]).T
    payload = jnp.concatenate([half[0:128, :], half[128:HALF, :], both[:, 0 : 128 * CHUNK1 - 2 * D]], axis=1)
    write_rows(out_ref, payload, CHUNK1)


def route_kernel(x_ref, matching_ref, out_ref):
    zh, _ = place()
    parts = split3(read_rows(x_ref, CHUNK1))
    rows = iota((128, 128), 0)
    marks = [jnp.where(matching_ref[b : b + 1, :] == rows, 1.0, 0.0) for b in range(2)]
    back_keep = jnp.where(zh == 0, marks[0], marks[1])
    back_give = jnp.where(zh == 0, marks[1], marks[0])
    fore = back_keep.T.astype(BF16)
    back_keep, back_give = back_keep.astype(BF16), back_give.astype(BF16)
    partner = sum(dot_nn(fore, p) for p in reversed(parts))
    source = sum(dot_nn(back_keep, p) for p in reversed(parts))
    given = sum(dot_nn(back_give, p[:, 768 : 128 * CHUNK1]) for p in reversed(parts))
    fill = jnp.zeros((128, 128 * CHUNK2 - 4 * D - 2 * LIST), F32)
    routed = jnp.concatenate([partner[:, 0 : 2 * D], source[:, 0 : 2 * D + LIST], given[:, 48:64], fill], axis=1)
    write_rows(out_ref, routed, CHUNK2)


def table_row(rel, zh, core):
    owner = (rel >= REL_DEV).astype(jnp.int32) + (rel >= 2 * REL_DEV).astype(jnp.int32)
    owner = owner + (rel >= 3 * REL_DEV).astype(jnp.int32)
    off = rel - REL_DEV * owner
    owner_zh = (owner >= 2).astype(jnp.int32)
    other_core = (owner - 2 * owner_zh) != core
    return jnp.where(owner_zh == zh, 0, 2 * REL_DEV) + jnp.where(other_core, REL_DEV, 0) + off


def piece_start(spot):
    return min(PIECE * spot, D - PIECE)


def bundle_kernel(relation_ref, give_ref, out_ref):
    spot = lax.axis_index("x")
    start = pl.multiple_of(jnp.minimum(PIECE * spot, D - PIECE), 16)
    out_ref[:, 512:REL_LANES] = jnp.zeros((PIECE + LIST, REL_LANES - 512), F32)
    out_ref[0:PIECE, 0:REL_DEV] = relation_ref[pl.ds(start, PIECE), :]
    out_ref[PIECE : PIECE + LIST, 128:512] = jnp.zeros((LIST, 384), F32)
    out_ref[PIECE : PIECE + LIST, 0:128] = give_ref[...]


def gather_relations(lists, zh, core, table_hi, table_lo):
    rel_at = table_row(lists[:, 4:8].astype(jnp.int32), zh, core)
    rels = onehot_cols(rel_at, 0, 4, iota((128, TABLE), 1))
    return dot_nn(rels, table_hi[...]) + dot_nn(rels, table_lo[...])


def left_kernel(
    entity_ref, cols_ref, bundle_ref, near_ref, near2_ref, far_ref,
    rel_out, left_hi, left_lo, table_hi, table_lo, entity_hi, entity_lo, cols_out, far_table,
):
    zh, core = place()
    for c in range(2):
        for spot in range(PIECES):
            far_table[c, piece_start(spot) : piece_start(spot) + PIECE, :] = far_ref[2 * spot + c, :, 0:REL_DEV]
    parts = (near_ref[...], near2_ref[...], far_table[core], far_table[1 - core])
    for k, part in enumerate(parts):
        hi, lo = split2(part.T)
        table_hi[k * REL_DEV : (k + 1) * REL_DEV, :] = hi
        table_lo[k * REL_DEV : (k + 1) * REL_DEV, :] = lo
    hi, lo = split2(entity_ref[...].T)
    entity_hi[...] = hi
    entity_lo[...] = lo
    own = iota((128, ROWS), 1).astype(F32)
    theirs = jnp.concatenate([bundle_ref[PIECE : PIECE + LIST, 0:128], jnp.zeros((128 - LIST, 128), F32)], axis=0).T
    cols_out[...] = theirs
    for k, lists in enumerate((cols_ref[:, 0:LIST], theirs[:, 0:LIST])):
        heads = onehot_cols(lists, 0, 4, own)
        head_rows = dot_nn(heads, hi) + dot_nn(heads, lo)
        rel_rows = gather_relations(lists, zh, core, table_hi, table_lo)
        l_hi, l_lo = split2(head_rows * rel_rows)
        span = pl.ds(k * SLOTS, SLOTS)
        rel_out[span, :] = rel_rows
        left_hi[span, :] = l_hi
        left_lo[span, :] = l_lo


def fill_block(hi_ref, lo_ref, mine, theirs, first):
    for k, (rows, lane) in enumerate(((mine, 0), (mine, D), (theirs, 0), (theirs, D))):
        hi, lo = split2(rows[:, first + lane : first + lane + D])
        hi_ref[128 * k : 128 * (k + 1), :] = hi
        lo_ref[128 * k : 128 * (k + 1), :] = lo


def lists_rows(lists):
    return jnp.concatenate([lists, jnp.zeros((128, 128 - LIST), F32)], axis=1).T


def head_kernel(mine_ref, theirs_ref, lists_mine, lists_theirs, rel_ref, left_hi, left_lo, grad_ref, block_hi, block_lo):
    _, core = place()
    fill_block(block_hi, block_lo, read_rows(mine_ref, CHUNK2), read_rows(theirs_ref, CHUNK2), 0)
    numbers = jnp.bitwise_xor(iota((128, ROWS), 1), core * HALF).astype(F32)
    heads_at = iota((ROWS, 128), 0).astype(F32)
    total = None
    for k in range(2):
        lists = (lists_mine, lists_theirs)[k][:, 0:LIST]
        span = pl.ds(k * SLOTS, SLOTS)
        hi, lo = left_hi[span, :], left_lo[span, :]
        b_hi, b_lo = block_hi[...], block_lo[...]
        scores = dot_nt(hi, b_lo) + dot_nt(lo, b_hi) + dot_nt(hi, b_hi)
        tails = jnp.concatenate(
            [jnp.where(lists[:, 8 + j : 9 + j] == numbers, 1.0, 0.0) for j in range(4)], axis=0
        )
        drawn = sum(jnp.where(lists[:, 12 + j : 13 + j] == numbers, 1.0, 0.0) for j in range(3))
        times = jnp.sum(drawn, axis=0, keepdims=True) + tails
        scores = jnp.where(times > 0.0, scores, -3.0e38)
        weights = times * jnp.exp(scores - jnp.max(scores, axis=1, keepdims=True))
        weights = weights / jnp.sum(weights, axis=1, keepdims=True) - tails
        w_hi, w_lo = split2(weights)
        grad_left = dot_nn(w_hi, b_lo) + dot_nn(w_lo, b_hi) + dot_nn(w_hi, b_hi)
        g_hi, g_lo = split2(grad_left * rel_ref[span, :])
        rows = lists_rows(lists)
        marks = jnp.concatenate(
            [jnp.where(rows[j : j + 1, :] == heads_at, 1.0, 0.0) for j in range(4)], axis=1
        ).astype(BF16)
        part = dot_nn(marks, g_lo) + dot_nn(marks, g_hi)
        total = part if total is None else total + part
    grad_ref[...] = total


def first_relations_kernel(mine_ref, table_hi, table_lo, rel_ref):
    zh, core = place()
    chunk = mine_ref[pl.ds(GIVEN_CHUNK, 128, stride=CHUNK2), :]
    rel_ref[...] = gather_relations(chunk[:, FIRST : FIRST + LIST], zh, core, table_hi, table_lo)


def tail_kernel(
    mine_ref, theirs_ref, given_ref, rel_ref, entity_hi, entity_lo, table_hi, table_lo, head_grad,
    keep_ref, send_ref, block_hi, block_lo,
):
    zh, core = place()
    mine = read_rows(mine_ref, CHUNK2)
    fill_block(block_hi, block_lo, mine, read_rows(theirs_ref, CHUNK2), 2 * D)
    e_hi, e_lo = entity_hi[...], entity_lo[...]
    numbers = jnp.bitwise_xor(iota((128, ROWS), 1), core * HALF).astype(F32)
    rows_at = iota((ROWS, 128), 0).astype(F32)
    total = head_grad[...]
    for k in range(2):
        if k == 0:
            lists = mine[:, 4 * D : 4 * D + LIST]
            rel_rows = rel_ref[...]
        else:
            lists = given_ref[:, FIRST + LIST : FIRST + 2 * LIST]
            rel_rows = gather_relations(lists, zh, core, table_hi, table_lo)
        heads = onehot_cols(lists, 0, 4, numbers)
        head_rows = dot_nn(heads, block_hi[...]) + dot_nn(heads, block_lo[...])
        l_hi, l_lo = split2(head_rows * rel_rows)
        scores = dot_nt(e_lo, l_hi) + dot_nt(e_hi, l_lo) + dot_nt(e_hi, l_hi)
        rows = lists_rows(lists)
        tails = jnp.concatenate(
            [jnp.where(rows[8 + j : 9 + j, :] == rows_at, 1.0, 0.0) for j in range(4)], axis=1
        )
        drawn = sum(jnp.where(rows[12 + j : 13 + j, :] == rows_at, 1.0, 0.0) for j in range(3))
        times = jnp.sum(drawn, axis=1, keepdims=True) + tails
        scores = jnp.where(times > 0.0, scores, -3.0e38)
        weights = times * jnp.exp(scores - jnp.max(scores, axis=0, keepdims=True))
        weights = weights / jnp.sum(weights, axis=0, keepdims=True) - tails
        w_hi, w_lo = split2(weights)
        total = total + (dot_nn(w_lo, l_hi) + dot_nn(w_hi, l_lo) + dot_nn(w_hi, l_hi))
    first, second = total[0:HALF, :].T, total[HALF:ROWS, :].T
    keep_ref[...] = jnp.where(core == 0, first, second)
    send_ref[...] = jnp.where(core == 0, second, first)


def update_kernel(mine_ref, theirs_ref, entity_ref, state_ref, updated_ref, accum_ref):
    _, core = place()
    mine, theirs = mine_ref[...], theirs_ref[...]
    for j, gradient in enumerate((jnp.where(core == 0, mine, theirs), jnp.where(core == 0, theirs, mine))):
        span = slice(HALF * j, HALF * (j + 1))
        accum = state_ref[:, span] + jnp.sum(gradient * gradient, axis=0, keepdims=True) / float(D)
        accum_ref[:, span] = accum
        updated_ref[:, span] = entity_ref[:, span] - LEARN_RATE * gradient / jnp.sqrt(accum)


def call(kernel, out_shape, args, vmem, scratch=(), cost=None, space=pltpu.VMEM):
    out_shape = jax.tree.map(lambda s: jax.ShapeDtypeStruct(*s), out_shape, is_leaf=lambda s: isinstance(s, tuple))
    return pl.pallas_call(
        kernel,
        out_shape=out_shape,
        in_specs=[pl.BlockSpec(memory_space=space) for _ in args],
        out_specs=jax.tree.map(lambda _: pl.BlockSpec(memory_space=pltpu.VMEM), out_shape),
        scratch_shapes=list(scratch),
        compiler_params=pltpu.CompilerParams(vmem_limit_bytes=vmem * MIB),
        cost_estimate=cost,
        name=kernel.__name__,
    )(*args)


def flops(us):
    return pl.CostEstimate(flops=int(us * 1.0e9), bytes_accessed=4_000_000, transcendentals=0)


def shards(entity, state, relation, edge_head, edge_rel, edge_tail, negatives, counts, matching):
    swap_core = functools.partial(lax.ppermute, axis_name="core", perm=[(0, 1), (1, 0)])
    swap_zh = functools.partial(lax.ppermute, axis_name="zh", perm=[(0, 1), (1, 0)])
    exchange = functools.partial(lax.all_to_all, axis_name=("x", "yz"), split_axis=0, concat_axis=0, tiled=True)
    entity_t, relation_t = entity.T, relation.T

    payload, cols, give = call(
        pack_kernel,
        [((128 * CHUNK1, 128), F32), ((128, 128), F32), ((LIST, 128), F32)],
        (entity_t, edge_head, edge_rel, edge_tail, negatives, counts),
        vmem=60,
        scratch=[pltpu.VMEM((128, 128), F32), pltpu.VMEM((D, ROWS), F32)]
        + [pltpu.VMEM((2, 1, 1, n), jnp.int32) for n in (SLOTS, SLOTS, SLOTS, NEGS)]
        + [pltpu.VMEM((2, 1, 1), jnp.int32), pltpu.SemaphoreType.DMA((6,))],
        space=pltpu.HBM,
    )
    spread = exchange(payload.reshape(128, 1, 128 * CHUNK1)).reshape(128 * CHUNK1, 128)

    bundle = swap_zh(call(bundle_kernel, ((PIECE + LIST, REL_LANES), F32), (relation_t, give), vmem=8))
    near2 = swap_core(relation_t)
    spread, bundle = lax.optimization_barrier((spread, bundle))
    far = lax.all_gather(bundle[0:PIECE], ("x", "core"), axis=0)

    routed = call(route_kernel, ((128 * CHUNK2, 128), F32), (spread, matching), vmem=16)
    fetched = exchange(routed.reshape(128, 1, 128 * CHUNK2)).reshape(128 * CHUNK2, 128)
    prepared = call(
        left_kernel,
        [
            ((2 * SLOTS, D), F32),
            ((2 * SLOTS, D), BF16),
            ((2 * SLOTS, D), BF16),
            ((TABLE, D), BF16),
            ((TABLE, D), BF16),
            ((ROWS, D), BF16),
            ((ROWS, D), BF16),
            ((128, 128), F32),
        ],
        (entity_t, cols, bundle, relation_t, near2, far),
        vmem=36,
        scratch=[pltpu.VMEM((2, D, REL_DEV), F32)],
        cost=flops(8),
    )
    rel_rows, left_hi, left_lo, table_hi, table_lo, entity_hi, entity_lo, cols_other = prepared
    fetched, cols_other = lax.optimization_barrier((fetched, cols_other))
    fetched_other = swap_core(fetched)
    given = swap_zh(lax.slice(fetched, (GIVEN_CHUNK, 0), fetched.shape, (CHUNK2, 1)))
    first_rel = call(first_relations_kernel, ((SLOTS, D), F32), (fetched, table_hi, table_lo), vmem=24, cost=flops(3))
    fetched_other, first_rel = lax.optimization_barrier((fetched_other, first_rel))
    block = [pltpu.VMEM((ROWS, D), BF16), pltpu.VMEM((ROWS, D), BF16)]
    head_grad = call(
        head_kernel,
        ((ROWS, D), F32),
        (fetched, fetched_other, cols, cols_other, rel_rows, left_hi, left_lo),
        vmem=24,
        scratch=block,
        cost=flops(6),
    )
    keep, send = call(
        tail_kernel,
        [((D, HALF), F32), ((D, HALF), F32)],
        (fetched, fetched_other, given, first_rel, entity_hi, entity_lo, table_hi, table_lo, head_grad),
        vmem=32,
        scratch=block,
        cost=flops(9),
    )
    half = keep + swap_core(send)
    half = half + swap_zh(half)
    other = swap_core(half)
    updated, accum = call(
        update_kernel,
        [((D, ROWS), F32), ((1, ROWS), F32)],
        (half, other, entity_t, state.reshape(1, ROWS)),
        vmem=8,
    )
    return updated.T, accum.reshape(ROWS)


def solution(mesh):
    parts = (PIECES, mesh.shape["dom"] // PIECES, 2, 2)
    fine = jax.sharding.Mesh(mesh.devices.reshape(parts), ("x", "yz", "zh", "core"))
    dom, edge = ("x", "yz"), ("zh", "core")
    return jax.shard_map(
        shards,
        mesh=fine,
        in_specs=(
            P(dom, None),
            P(dom),
            P(edge, None),
            P(None, dom, edge, None),
            P(None, dom, edge, None),
            P(None, dom, edge, None),
            P(None, dom, edge, None),
            P(None, dom, edge),
            P(),
        ),
        out_specs=(P(dom, None), P(dom)),
        check_vma=False,
    )
```

```python
import functools

import jax
import jax.numpy as jnp
from jax import lax
from jax.experimental import pallas as pl
from jax.experimental.pallas import tpu as pltpu
from jax.sharding import PartitionSpec as P


LEARN_RATE = 0.1
D = 400
ROWS = 512
HALF = 256
SLOTS = 512
NEGS = 320
REL_DEV = 528
PIECES = 4
PIECE = 112
REL_LANES = 576
TABLE = 4 * REL_DEV
LIST = 16
CHUNK1 = 7
CHUNK2 = 13
GIVEN_CHUNK = 12
FIRST = 4 * D - 128 * GIVEN_CHUNK
F32 = jnp.float32
BF16 = jnp.bfloat16
MIB = 1024 * 1024


def split2(x):
    hi = x.astype(BF16)
    return hi, (x - hi.astype(F32)).astype(BF16)


def split3(x):
    hi = x.astype(BF16)
    rest = x - hi.astype(F32)
    mid = rest.astype(BF16)
    return hi, mid, (rest - mid.astype(F32)).astype(BF16)


def dot_nn(a, b):
    return lax.dot_general(a, b, (((1,), (0,)), ((), ())), preferred_element_type=F32)


def dot_nt(a, b):
    return lax.dot_general(a, b, (((1,), (1,)), ((), ())), preferred_element_type=F32)


def iota(shape, dim):
    return lax.broadcasted_iota(jnp.int32, shape, dim)


def place():
    return lax.axis_index("zh"), lax.axis_index("core")


def read_rows(ref, chunks):
    return jnp.concatenate([ref[pl.ds(k, 128, stride=chunks), :] for k in range(chunks)], axis=1)


def write_rows(ref, value, chunks):
    for k in range(chunks):
        ref[pl.ds(k, 128, stride=chunks), :] = value[:, 128 * k : 128 * (k + 1)]


def onehot_cols(lists, first, count, columns):
    blocks = [(lists[:, first + j : first + j + 1] == columns) for j in range(count)]
    return jnp.concatenate([jnp.where(b, 1.0, 0.0).astype(BF16) for b in blocks], axis=0)


def pack_kernel(
    entity_hbm, head_hbm, rel_hbm, tail_hbm, neg_hbm, count_hbm, out_ref, cols_ref, give_ref,
    rows_ref, entity_ref, head_ref, rel_ref, tail_ref, neg_ref, count_ref, sems,
):
    zh, core = place()
    pairs = (
        (head_hbm, head_ref), (rel_hbm, rel_ref), (tail_hbm, tail_ref), (neg_hbm, neg_ref), (count_hbm, count_ref),
        (entity_hbm, entity_ref),
    )
    copies = [pltpu.make_async_copy(a, b, sems.at[i]) for i, (a, b) in enumerate(pairs)]
    for copy in copies:
        copy.start()
    rows_ref[...] = jnp.full((128, 128), -1.0, F32)
    lane = iota((1, 128), 1)
    for copy in copies[:-1]:
        copy.wait()
    for bucket in range(2):
        at = bucket * LIST
        live = count_ref[0, :, bucket : bucket + 1]
        for j in range(4):
            span = pl.ds(128 * j, 128)
            head = jnp.where(lane + 128 * j < live, head_ref[bucket, 0, 0:1, span], -1)
            rows_ref[at + j : at + j + 1, :] = head.astype(F32)
            rows_ref[at + 4 + j : at + 5 + j, :] = rel_ref[bucket, 0, 0:1, span].astype(F32)
            rows_ref[at + 8 + j : at + 9 + j, :] = tail_ref[bucket, 0, 0:1, span].astype(F32)
        rows_ref[at + 12 : at + 13, :] = neg_ref[bucket, 0, 0:1, 0:128].astype(F32)
        rows_ref[at + 13 : at + 14, :] = neg_ref[bucket, 0, 0:1, 128:256].astype(F32)
        rows_ref[at + 14 : at + 15, 0:64] = neg_ref[bucket, 0, 0:1, 256:320].astype(F32)
    one, two = rows_ref[0:LIST, :], rows_ref[LIST : 2 * LIST, :]
    keep = jnp.where(zh == 0, one, two)
    give = jnp.where(zh == 0, two, one)
    both = jnp.concatenate([keep, give, rows_ref[2 * LIST :, :]], axis=0).T
    cols_ref[...] = both
    give_ref[...] = give
    copies[-1].wait()
    half = jnp.where(core == 0, entity_ref[:, 0:HALF], entity_ref[:, HALF:ROWS]).T
    payload = jnp.concatenate([half[0:128, :], half[128:HALF, :], both[:, 0 : 128 * CHUNK1 - 2 * D]], axis=1)
    write_rows(out_ref, payload, CHUNK1)


def route_kernel(x_ref, matching_ref, out_ref):
    zh, _ = place()
    parts = split3(read_rows(x_ref, CHUNK1))
    rows = iota((128, 128), 0)
    marks = [jnp.where(matching_ref[b : b + 1, :] == rows, 1.0, 0.0) for b in range(2)]
    back_keep = jnp.where(zh == 0, marks[0], marks[1])
    back_give = jnp.where(zh == 0, marks[1], marks[0])
    fore = back_keep.T.astype(BF16)
    back_keep, back_give = back_keep.astype(BF16), back_give.astype(BF16)
    partner = sum(dot_nn(fore, p) for p in reversed(parts))
    source = sum(dot_nn(back_keep, p) for p in reversed(parts))
    given = sum(dot_nn(back_give, p[:, 768 : 128 * CHUNK1]) for p in reversed(parts))
    fill = jnp.zeros((128, 128 * CHUNK2 - 4 * D - 2 * LIST), F32)
    routed = jnp.concatenate([partner[:, 0 : 2 * D], source[:, 0 : 2 * D + LIST], given[:, 48:64], fill], axis=1)
    write_rows(out_ref, routed, CHUNK2)


def table_row(rel, zh, core):
    owner = (rel >= REL_DEV).astype(jnp.int32) + (rel >= 2 * REL_DEV).astype(jnp.int32)
    owner = owner + (rel >= 3 * REL_DEV).astype(jnp.int32)
    off = rel - REL_DEV * owner
    owner_zh = (owner >= 2).astype(jnp.int32)
    other_core = (owner - 2 * owner_zh) != core
    return jnp.where(owner_zh == zh, 0, 2 * REL_DEV) + jnp.where(other_core, REL_DEV, 0) + off


def piece_start(spot):
    return min(PIECE * spot, D - PIECE)


def bundle_kernel(relation_ref, give_ref, out_ref):
    spot = lax.axis_index("x")
    start = pl.multiple_of(jnp.minimum(PIECE * spot, D - PIECE), 16)
    out_ref[:, 512:REL_LANES] = jnp.zeros((PIECE + LIST, REL_LANES - 512), F32)
    out_ref[0:PIECE, 0:REL_DEV] = relation_ref[pl.ds(start, PIECE), :]
    out_ref[PIECE : PIECE + LIST, 128:512] = jnp.zeros((LIST, 384), F32)
    out_ref[PIECE : PIECE + LIST, 0:128] = give_ref[...]


def gather_relations(lists, zh, core, table_hi, table_lo):
    rel_at = table_row(lists[:, 4:8].astype(jnp.int32), zh, core)
    rels = onehot_cols(rel_at, 0, 4, iota((128, TABLE), 1))
    return dot_nn(rels, table_hi[...]) + dot_nn(rels, table_lo[...])


def left_kernel(
    entity_ref, cols_ref, bundle_ref, near_ref, near2_ref, far_ref, far2_ref,
    rel_out, left_hi, left_lo, table_hi, table_lo, entity_hi, entity_lo, cols_out, far_table,
):
    zh, core = place()
    for c, ref in enumerate((far_ref, far2_ref)):
        for spot in range(PIECES):
            far_table[c, piece_start(spot) : piece_start(spot) + PIECE, :] = ref[spot, :, 0:REL_DEV]
    parts = (near_ref[...], near2_ref[...], far_table[0], far_table[1])
    for k, part in enumerate(parts):
        hi, lo = split2(part.T)
        table_hi[k * REL_DEV : (k + 1) * REL_DEV, :] = hi
        table_lo[k * REL_DEV : (k + 1) * REL_DEV, :] = lo
    hi, lo = split2(entity_ref[...].T)
    entity_hi[...] = hi
    entity_lo[...] = lo
    own = iota((128, ROWS), 1).astype(F32)
    theirs = jnp.concatenate([bundle_ref[PIECE : PIECE + LIST, 0:128], jnp.zeros((128 - LIST, 128), F32)], axis=0).T
    cols_out[...] = theirs
    for k, lists in enumerate((cols_ref[:, 0:LIST], theirs[:, 0:LIST])):
        heads = onehot_cols(lists, 0, 4, own)
        head_rows = dot_nn(heads, hi) + dot_nn(heads, lo)
        rel_rows = gather_relations(lists, zh, core, table_hi, table_lo)
        l_hi, l_lo = split2(head_rows * rel_rows)
        span = pl.ds(k * SLOTS, SLOTS)
        rel_out[span, :] = rel_rows
        left_hi[span, :] = l_hi
        left_lo[span, :] = l_lo


def fill_block(hi_ref, lo_ref, mine, theirs, first):
    for k, (rows, lane) in enumerate(((mine, 0), (mine, D), (theirs, 0), (theirs, D))):
        hi, lo = split2(rows[:, first + lane : first + lane + D])
        hi_ref[128 * k : 128 * (k + 1), :] = hi
        lo_ref[128 * k : 128 * (k + 1), :] = lo


def lists_rows(lists):
    return jnp.concatenate([lists, jnp.zeros((128, 128 - LIST), F32)], axis=1).T


def head_kernel(mine_ref, theirs_ref, lists_mine, lists_theirs, rel_ref, left_hi, left_lo, grad_ref, block_hi, block_lo):
    _, core = place()
    fill_block(block_hi, block_lo, read_rows(mine_ref, CHUNK2), read_rows(theirs_ref, CHUNK2), 0)
    numbers = jnp.bitwise_xor(iota((128, ROWS), 1), core * HALF).astype(F32)
    heads_at = iota((ROWS, 128), 0).astype(F32)
    total = None
    for k in range(2):
        lists = (lists_mine, lists_theirs)[k][:, 0:LIST]
        span = pl.ds(k * SLOTS, SLOTS)
        hi, lo = left_hi[span, :], left_lo[span, :]
        b_hi, b_lo = block_hi[...], block_lo[...]
        scores = dot_nt(hi, b_lo) + dot_nt(lo, b_hi) + dot_nt(hi, b_hi)
        tails = jnp.concatenate(
            [jnp.where(lists[:, 8 + j : 9 + j] == numbers, 1.0, 0.0) for j in range(4)], axis=0
        )
        drawn = sum(jnp.where(lists[:, 12 + j : 13 + j] == numbers, 1.0, 0.0) for j in range(3))
        times = jnp.sum(drawn, axis=0, keepdims=True) + tails
        scores = jnp.where(times > 0.0, scores, -3.0e38)
        weights = times * jnp.exp(scores - jnp.max(scores, axis=1, keepdims=True))
        weights = weights / jnp.sum(weights, axis=1, keepdims=True) - tails
        w_hi, w_lo = split2(weights)
        grad_left = dot_nn(w_hi, b_lo) + dot_nn(w_lo, b_hi) + dot_nn(w_hi, b_hi)
        g_hi, g_lo = split2(grad_left * rel_ref[span, :])
        rows = lists_rows(lists)
        marks = jnp.concatenate(
            [jnp.where(rows[j : j + 1, :] == heads_at, 1.0, 0.0) for j in range(4)], axis=1
        ).astype(BF16)
        part = dot_nn(marks, g_lo) + dot_nn(marks, g_hi)
        total = part if total is None else total + part
    grad_ref[...] = total


def first_relations_kernel(mine_ref, table_hi, table_lo, rel_ref):
    zh, core = place()
    chunk = mine_ref[pl.ds(GIVEN_CHUNK, 128, stride=CHUNK2), :]
    rel_ref[...] = gather_relations(chunk[:, FIRST : FIRST + LIST], zh, core, table_hi, table_lo)


def tail_kernel(
    mine_ref, theirs_ref, given_ref, rel_ref, entity_hi, entity_lo, table_hi, table_lo, head_grad,
    keep_ref, send_ref, block_hi, block_lo,
):
    zh, core = place()
    mine = read_rows(mine_ref, CHUNK2)
    fill_block(block_hi, block_lo, mine, read_rows(theirs_ref, CHUNK2), 2 * D)
    e_hi, e_lo = entity_hi[...], entity_lo[...]
    numbers = jnp.bitwise_xor(iota((128, ROWS), 1), core * HALF).astype(F32)
    rows_at = iota((ROWS, 128), 0).astype(F32)
    total = head_grad[...]
    for k in range(2):
        if k == 0:
            lists = mine[:, 4 * D : 4 * D + LIST]
            rel_rows = rel_ref[...]
        else:
            lists = given_ref[:, FIRST + LIST : FIRST + 2 * LIST]
            rel_rows = gather_relations(lists, zh, core, table_hi, table_lo)
        heads = onehot_cols(lists, 0, 4, numbers)
        head_rows = dot_nn(heads, block_hi[...]) + dot_nn(heads, block_lo[...])
        l_hi, l_lo = split2(head_rows * rel_rows)
        scores = dot_nt(e_lo, l_hi) + dot_nt(e_hi, l_lo) + dot_nt(e_hi, l_hi)
        rows = lists_rows(lists)
        tails = jnp.concatenate(
            [jnp.where(rows[8 + j : 9 + j, :] == rows_at, 1.0, 0.0) for j in range(4)], axis=1
        )
        drawn = sum(jnp.where(rows[12 + j : 13 + j, :] == rows_at, 1.0, 0.0) for j in range(3))
        times = jnp.sum(drawn, axis=1, keepdims=True) + tails
        scores = jnp.where(times > 0.0, scores, -3.0e38)
        weights = times * jnp.exp(scores - jnp.max(scores, axis=0, keepdims=True))
        weights = weights / jnp.sum(weights, axis=0, keepdims=True) - tails
        w_hi, w_lo = split2(weights)
        total = total + (dot_nn(w_lo, l_hi) + dot_nn(w_hi, l_lo) + dot_nn(w_hi, l_hi))
    first, second = total[0:HALF, :].T, total[HALF:ROWS, :].T
    keep_ref[...] = jnp.where(core == 0, first, second)
    send_ref[...] = jnp.where(core == 0, second, first)


def update_kernel(mine_ref, theirs_ref, entity_ref, state_ref, updated_ref, accum_ref):
    _, core = place()
    mine, theirs = mine_ref[...], theirs_ref[...]
    for j, gradient in enumerate((jnp.where(core == 0, mine, theirs), jnp.where(core == 0, theirs, mine))):
        span = slice(HALF * j, HALF * (j + 1))
        accum = state_ref[:, span] + jnp.sum(gradient * gradient, axis=0, keepdims=True) / float(D)
        accum_ref[:, span] = accum
        updated_ref[:, span] = entity_ref[:, span] - LEARN_RATE * gradient / jnp.sqrt(accum)


def call(kernel, out_shape, args, vmem, scratch=(), cost=None, space=pltpu.VMEM):
    out_shape = jax.tree.map(lambda s: jax.ShapeDtypeStruct(*s), out_shape, is_leaf=lambda s: isinstance(s, tuple))
    return pl.pallas_call(
        kernel,
        out_shape=out_shape,
        in_specs=[pl.BlockSpec(memory_space=space) for _ in args],
        out_specs=jax.tree.map(lambda _: pl.BlockSpec(memory_space=pltpu.VMEM), out_shape),
        scratch_shapes=list(scratch),
        compiler_params=pltpu.CompilerParams(vmem_limit_bytes=vmem * MIB),
        cost_estimate=cost,
        name=kernel.__name__,
    )(*args)


def flops(us):
    return pl.CostEstimate(flops=int(us * 1.0e9), bytes_accessed=4_000_000, transcendentals=0)


def shards(entity, state, relation, edge_head, edge_rel, edge_tail, negatives, counts, matching):
    swap_core = functools.partial(lax.ppermute, axis_name="core", perm=[(0, 1), (1, 0)])
    swap_zh = functools.partial(lax.ppermute, axis_name="zh", perm=[(0, 1), (1, 0)])
    exchange = functools.partial(lax.all_to_all, axis_name=("x", "yz"), split_axis=0, concat_axis=0, tiled=True)
    entity_t, relation_t = entity.T, relation.T

    payload, cols, give = call(
        pack_kernel,
        [((128 * CHUNK1, 128), F32), ((128, 128), F32), ((LIST, 128), F32)],
        (entity_t, edge_head, edge_rel, edge_tail, negatives, counts.transpose(1, 2, 0)),
        vmem=60,
        scratch=[pltpu.VMEM((128, 128), F32), pltpu.VMEM((D, ROWS), F32)]
        + [pltpu.VMEM((2, 1, 1, n), jnp.int32) for n in (SLOTS, SLOTS, SLOTS, NEGS)]
        + [pltpu.VMEM((1, 1, 2), jnp.int32), pltpu.SemaphoreType.DMA((6,))],
        space=pltpu.HBM,
    )
    spread = exchange(payload.reshape(128, 1, 128 * CHUNK1)).reshape(128 * CHUNK1, 128)

    bundle = swap_zh(call(bundle_kernel, ((PIECE + LIST, REL_LANES), F32), (relation_t, give), vmem=8))
    near2 = swap_core(relation_t)

    routed = call(route_kernel, ((128 * CHUNK2, 128), F32), (spread, matching), vmem=16)
    fetched = exchange(routed.reshape(128, 1, 128 * CHUNK2)).reshape(128 * CHUNK2, 128)
    bundle, _ = lax.optimization_barrier((bundle, routed))
    far = lax.all_gather(bundle[0:PIECE], "x", axis=0)
    far2 = swap_core(far)
    prepared = call(
        left_kernel,
        [
            ((2 * SLOTS, D), F32),
            ((2 * SLOTS, D), BF16),
            ((2 * SLOTS, D), BF16),
            ((TABLE, D), BF16),
            ((TABLE, D), BF16),
            ((ROWS, D), BF16),
            ((ROWS, D), BF16),
            ((128, 128), F32),
        ],
        (entity_t, cols, bundle, relation_t, near2, far, far2),
        vmem=36,
        scratch=[pltpu.VMEM((2, D, REL_DEV), F32)],
        cost=flops(8),
    )
    rel_rows, left_hi, left_lo, table_hi, table_lo, entity_hi, entity_lo, cols_other = prepared
    fetched_other = swap_core(fetched)
    given = swap_zh(lax.slice(fetched, (GIVEN_CHUNK, 0), fetched.shape, (CHUNK2, 1)))
    first_rel = call(first_relations_kernel, ((SLOTS, D), F32), (fetched, table_hi, table_lo), vmem=24, cost=flops(3))
    fetched_other, first_rel = lax.optimization_barrier((fetched_other, first_rel))
    block = [pltpu.VMEM((ROWS, D), BF16), pltpu.VMEM((ROWS, D), BF16)]
    head_grad = call(
        head_kernel,
        ((ROWS, D), F32),
        (fetched, fetched_other, cols, cols_other, rel_rows, left_hi, left_lo),
        vmem=24,
        scratch=block,
        cost=flops(6),
    )
    keep, send = call(
        tail_kernel,
        [((D, HALF), F32), ((D, HALF), F32)],
        (fetched, fetched_other, given, first_rel, entity_hi, entity_lo, table_hi, table_lo, head_grad),
        vmem=32,
        scratch=block,
        cost=flops(9),
    )
    half = keep + swap_core(send)
    half = half + swap_zh(half)
    other = swap_core(half)
    updated, accum = call(
        update_kernel,
        [((D, ROWS), F32), ((1, ROWS), F32)],
        (half, other, entity_t, state.reshape(1, ROWS)),
        vmem=8,
    )
    return updated.T, accum.reshape(ROWS)


def solution(mesh):
    parts = (PIECES, mesh.shape["dom"] // PIECES, 2, 2)
    fine = jax.sharding.Mesh(mesh.devices.reshape(parts), ("x", "yz", "zh", "core"))
    dom, edge = ("x", "yz"), ("zh", "core")
    return jax.shard_map(
        shards,
        mesh=fine,
        in_specs=(
            P(dom, None),
            P(dom),
            P(edge, None),
            P(None, dom, edge, None),
            P(None, dom, edge, None),
            P(None, dom, edge, None),
            P(None, dom, edge, None),
            P(None, dom, edge),
            P(),
        ),
        out_specs=(P(dom, None), P(dom)),
        check_vma=False,
    )
```

```python
import functools

import jax
import jax.numpy as jnp
from jax import lax
from jax.experimental import pallas as pl
from jax.experimental.pallas import tpu as pltpu
from jax.sharding import PartitionSpec as P


LEARN_RATE = 0.1
D = 400
ROWS = 512
HALF = 256
SLOTS = 512
NEGS = 320
REL_DEV = 528
PIECES = 4
PIECE = 104
MAIN = 512
REST = REL_DEV - MAIN
TABLE = 4 * REL_DEV
LIST = 16
CHUNK1 = 7
CHUNK2 = 13
GIVEN_CHUNK = 12
FIRST = 4 * D - 128 * GIVEN_CHUNK
F32 = jnp.float32
BF16 = jnp.bfloat16
MIB = 1024 * 1024


def split2(x):
    hi = x.astype(BF16)
    return hi, (x - hi.astype(F32)).astype(BF16)


def split3(x):
    hi = x.astype(BF16)
    rest = x - hi.astype(F32)
    mid = rest.astype(BF16)
    return hi, mid, (rest - mid.astype(F32)).astype(BF16)


def dot_nn(a, b):
    return lax.dot_general(a, b, (((1,), (0,)), ((), ())), preferred_element_type=F32)


def dot_nt(a, b):
    return lax.dot_general(a, b, (((1,), (1,)), ((), ())), preferred_element_type=F32)


def iota(shape, dim):
    return lax.broadcasted_iota(jnp.int32, shape, dim)


def place():
    return lax.axis_index("zh"), lax.axis_index("core")


def read_rows(ref, chunks):
    return jnp.concatenate([ref[pl.ds(k, 128, stride=chunks), :] for k in range(chunks)], axis=1)


def write_rows(ref, value, chunks):
    for k in range(chunks):
        ref[pl.ds(k, 128, stride=chunks), :] = value[:, 128 * k : 128 * (k + 1)]


def onehot_cols(lists, first, count, columns):
    blocks = [(lists[:, first + j : first + j + 1] == columns) for j in range(count)]
    return jnp.concatenate([jnp.where(b, 1.0, 0.0).astype(BF16) for b in blocks], axis=0)


def pack_kernel(
    entity_hbm, head_hbm, rel_hbm, tail_hbm, neg_hbm, count_hbm, out_ref, cols_ref, give_ref,
    rows_ref, entity_ref, head_ref, rel_ref, tail_ref, neg_ref, count_ref, sems,
):
    zh, core = place()
    pairs = (
        (head_hbm, head_ref), (rel_hbm, rel_ref), (tail_hbm, tail_ref), (neg_hbm, neg_ref), (count_hbm, count_ref),
        (entity_hbm, entity_ref),
    )
    copies = [pltpu.make_async_copy(a, b, sems.at[i]) for i, (a, b) in enumerate(pairs)]
    for copy in copies:
        copy.start()
    rows_ref[...] = jnp.full((128, 128), -1.0, F32)
    lane = iota((1, 128), 1)
    for copy in copies[:-1]:
        copy.wait()
    for bucket in range(2):
        at = bucket * LIST
        live = count_ref[0, :, bucket : bucket + 1]
        for j in range(4):
            span = pl.ds(128 * j, 128)
            head = jnp.where(lane + 128 * j < live, head_ref[bucket, 0, 0:1, span], -1)
            rows_ref[at + j : at + j + 1, :] = head.astype(F32)
            rows_ref[at + 4 + j : at + 5 + j, :] = rel_ref[bucket, 0, 0:1, span].astype(F32)
            rows_ref[at + 8 + j : at + 9 + j, :] = tail_ref[bucket, 0, 0:1, span].astype(F32)
        rows_ref[at + 12 : at + 13, :] = neg_ref[bucket, 0, 0:1, 0:128].astype(F32)
        rows_ref[at + 13 : at + 14, :] = neg_ref[bucket, 0, 0:1, 128:256].astype(F32)
        rows_ref[at + 14 : at + 15, 0:64] = neg_ref[bucket, 0, 0:1, 256:320].astype(F32)
    one, two = rows_ref[0:LIST, :], rows_ref[LIST : 2 * LIST, :]
    keep = jnp.where(zh == 0, one, two)
    give = jnp.where(zh == 0, two, one)
    both = jnp.concatenate([keep, give, rows_ref[2 * LIST :, :]], axis=0).T
    cols_ref[...] = both
    give_ref[...] = give
    copies[-1].wait()
    half = jnp.where(core == 0, entity_ref[:, 0:HALF], entity_ref[:, HALF:ROWS]).T
    payload = jnp.concatenate([half[0:128, :], half[128:HALF, :], both[:, 0 : 128 * CHUNK1 - 2 * D]], axis=1)
    write_rows(out_ref, payload, CHUNK1)


def route_kernel(x_ref, matching_ref, out_ref):
    zh, _ = place()
    parts = split3(read_rows(x_ref, CHUNK1))
    rows = iota((128, 128), 0)
    marks = [jnp.where(matching_ref[b : b + 1, :] == rows, 1.0, 0.0) for b in range(2)]
    back_keep = jnp.where(zh == 0, marks[0], marks[1])
    back_give = jnp.where(zh == 0, marks[1], marks[0])
    fore = back_keep.T.astype(BF16)
    back_keep, back_give = back_keep.astype(BF16), back_give.astype(BF16)
    partner = sum(dot_nn(fore, p) for p in reversed(parts))
    source = sum(dot_nn(back_keep, p) for p in reversed(parts))
    given = sum(dot_nn(back_give, p[:, 768 : 128 * CHUNK1]) for p in reversed(parts))
    fill = jnp.zeros((128, 128 * CHUNK2 - 4 * D - 2 * LIST), F32)
    routed = jnp.concatenate([partner[:, 0 : 2 * D], source[:, 0 : 2 * D + LIST], given[:, 48:64], fill], axis=1)
    write_rows(out_ref, routed, CHUNK2)


def table_row(rel, zh, core):
    owner = (rel >= REL_DEV).astype(jnp.int32) + (rel >= 2 * REL_DEV).astype(jnp.int32)
    owner = owner + (rel >= 3 * REL_DEV).astype(jnp.int32)
    off = rel - REL_DEV * owner
    owner_zh = (owner >= 2).astype(jnp.int32)
    other_core = (owner - 2 * owner_zh) != core
    return jnp.where(owner_zh == zh, 0, 2 * REL_DEV) + jnp.where(other_core, REL_DEV, 0) + off


def piece_start(spot):
    return min(PIECE * spot, D - PIECE)


def bundle_kernel(relation_ref, give_ref, out_ref):
    spot = lax.axis_index("x")
    start = pl.multiple_of(jnp.minimum(PIECE * spot, D - PIECE), 8)
    piece = relation_ref[pl.ds(start, PIECE), :]
    out_ref[0:PIECE, :] = piece[:, 0:MAIN]
    rest = jnp.concatenate([piece[:, MAIN:REL_DEV], jnp.zeros((PIECE, 128 - REST), F32)], axis=1)
    rest = jnp.concatenate([rest, jnp.zeros((128 - PIECE, 128), F32)], axis=0).T
    for g in range(4):
        out_ref[PIECE : PIECE + 4, 128 * g : 128 * (g + 1)] = rest[4 * g : 4 * g + 4, :]
        out_ref[PIECE + 4 : PIECE + 8, 128 * g : 128 * (g + 1)] = give_ref[4 * g : 4 * g + 4, :]


def unfold(rows):
    return jnp.concatenate([rows[:, 128 * g : 128 * (g + 1)] for g in range(4)], axis=0)


def gather_relations(lists, zh, core, table_hi, table_lo):
    rel_at = table_row(lists[:, 4:8].astype(jnp.int32), zh, core)
    rels = onehot_cols(rel_at, 0, 4, iota((128, TABLE), 1))
    return dot_nn(rels, table_hi[...]) + dot_nn(rels, table_lo[...])


def relations_kernel(
    entity_ref, cols_ref, bundle_ref, near_ref, near2_ref, far_ref, far2_ref, fetched_ref,
    rel_out, left_hi, left_lo, first_out, table_hi, table_lo, entity_hi, entity_lo, cols_out, far_table,
):
    zh, core = place()
    for k, ref in enumerate((near_ref, near2_ref)):
        hi, lo = split2(ref[...].T)
        table_hi[k * REL_DEV : (k + 1) * REL_DEV, :] = hi
        table_lo[k * REL_DEV : (k + 1) * REL_DEV, :] = lo
    for k, ref in enumerate((far_ref, far2_ref)):
        for spot in range(PIECES):
            far_table[k, piece_start(spot) : piece_start(spot) + PIECE, :] = ref[spot, 0:PIECE, :]
        at = (2 + k) * REL_DEV
        hi, lo = split2(far_table[k].T)
        table_hi[at : at + MAIN, :] = hi
        table_lo[at : at + MAIN, :] = lo
        rest = [unfold(ref[spot, PIECE : PIECE + 4, :]) for spot in range(PIECES)]
        rest = [rest[spot][:, 0:PIECE] for spot in range(PIECES - 1)] + [rest[-1][:, PIECES * PIECE - D : PIECE]]
        hi, lo = split2(jnp.concatenate(rest, axis=1))
        table_hi[at + MAIN : at + REL_DEV, :] = hi
        table_lo[at + MAIN : at + REL_DEV, :] = lo
    hi, lo = split2(entity_ref[...].T)
    entity_hi[...] = hi
    entity_lo[...] = lo
    own = iota((128, ROWS), 1).astype(F32)
    theirs = jnp.concatenate([unfold(bundle_ref[PIECE + 4 : PIECE + 8, :]), jnp.zeros((128 - LIST, 128), F32)], axis=0).T
    cols_out[...] = theirs
    for k, lists in enumerate((cols_ref[:, 0:LIST], theirs[:, 0:LIST])):
        heads = onehot_cols(lists, 0, 4, own)
        head_rows = dot_nn(heads, hi) + dot_nn(heads, lo)
        rel_rows = gather_relations(lists, zh, core, table_hi, table_lo)
        l_hi, l_lo = split2(head_rows * rel_rows)
        span = pl.ds(k * SLOTS, SLOTS)
        rel_out[span, :] = rel_rows
        left_hi[span, :] = l_hi
        left_lo[span, :] = l_lo
    chunk = fetched_ref[pl.ds(GIVEN_CHUNK, 128, stride=CHUNK2), :]
    first_out[...] = gather_relations(chunk[:, FIRST : FIRST + LIST], zh, core, table_hi, table_lo)


def fill_block(hi_ref, lo_ref, mine, theirs, first):
    for k, (rows, lane) in enumerate(((mine, 0), (mine, D), (theirs, 0), (theirs, D))):
        hi, lo = split2(rows[:, first + lane : first + lane + D])
        hi_ref[128 * k : 128 * (k + 1), :] = hi
        lo_ref[128 * k : 128 * (k + 1), :] = lo


def lists_rows(lists):
    return jnp.concatenate([lists, jnp.zeros((128, 128 - LIST), F32)], axis=1).T


def head_kernel(mine_ref, theirs_ref, lists_mine, lists_theirs, rel_ref, left_hi, left_lo, grad_ref, block_hi, block_lo):
    _, core = place()
    fill_block(block_hi, block_lo, read_rows(mine_ref, CHUNK2), read_rows(theirs_ref, CHUNK2), 0)
    numbers = jnp.bitwise_xor(iota((128, ROWS), 1), core * HALF).astype(F32)
    heads_at = iota((ROWS, 128), 0).astype(F32)
    total = None
    for k in range(2):
        lists = (lists_mine, lists_theirs)[k][:, 0:LIST]
        span = pl.ds(k * SLOTS, SLOTS)
        hi, lo = left_hi[span, :], left_lo[span, :]
        b_hi, b_lo = block_hi[...], block_lo[...]
        scores = dot_nt(hi, b_lo) + dot_nt(lo, b_hi) + dot_nt(hi, b_hi)
        tails = jnp.concatenate(
            [jnp.where(lists[:, 8 + j : 9 + j] == numbers, 1.0, 0.0) for j in range(4)], axis=0
        )
        drawn = sum(jnp.where(lists[:, 12 + j : 13 + j] == numbers, 1.0, 0.0) for j in range(3))
        times = jnp.sum(drawn, axis=0, keepdims=True) + tails
        scores = jnp.where(times > 0.0, scores, -3.0e38)
        weights = times * jnp.exp(scores - jnp.max(scores, axis=1, keepdims=True))
        weights = weights / jnp.sum(weights, axis=1, keepdims=True) - tails
        w_hi, w_lo = split2(weights)
        grad_left = dot_nn(w_hi, b_lo) + dot_nn(w_lo, b_hi) + dot_nn(w_hi, b_hi)
        g_hi, g_lo = split2(grad_left * rel_ref[span, :])
        rows = lists_rows(lists)
        marks = jnp.concatenate(
            [jnp.where(rows[j : j + 1, :] == heads_at, 1.0, 0.0) for j in range(4)], axis=1
        ).astype(BF16)
        part = dot_nn(marks, g_lo) + dot_nn(marks, g_hi)
        total = part if total is None else total + part
    grad_ref[...] = total


def given_kernel(fetched_ref, out_ref):
    out_ref[...] = fetched_ref[pl.ds(GIVEN_CHUNK, 128, stride=CHUNK2), :].T[FIRST + LIST : FIRST + 2 * LIST, :]


def tail_kernel(
    mine_ref, theirs_ref, given_ref, rel_ref, entity_hi, entity_lo, table_hi, table_lo, head_grad,
    keep_ref, send_ref, block_hi, block_lo,
):
    zh, core = place()
    mine = read_rows(mine_ref, CHUNK2)
    fill_block(block_hi, block_lo, mine, read_rows(theirs_ref, CHUNK2), 2 * D)
    e_hi, e_lo = entity_hi[...], entity_lo[...]
    numbers = jnp.bitwise_xor(iota((128, ROWS), 1), core * HALF).astype(F32)
    rows_at = iota((ROWS, 128), 0).astype(F32)
    total = head_grad[...]
    for k in range(2):
        if k == 0:
            lists = mine[:, 4 * D : 4 * D + LIST]
            rel_rows = rel_ref[...]
        else:
            lists = jnp.concatenate([given_ref[...], jnp.zeros((128 - LIST, 128), F32)], axis=0).T[:, 0:LIST]
            rel_rows = gather_relations(lists, zh, core, table_hi, table_lo)
        heads = onehot_cols(lists, 0, 4, numbers)
        head_rows = dot_nn(heads, block_hi[...]) + dot_nn(heads, block_lo[...])
        l_hi, l_lo = split2(head_rows * rel_rows)
        scores = dot_nt(e_lo, l_hi) + dot_nt(e_hi, l_lo) + dot_nt(e_hi, l_hi)
        rows = lists_rows(lists)
        tails = jnp.concatenate(
            [jnp.where(rows[8 + j : 9 + j, :] == rows_at, 1.0, 0.0) for j in range(4)], axis=1
        )
        drawn = sum(jnp.where(rows[12 + j : 13 + j, :] == rows_at, 1.0, 0.0) for j in range(3))
        times = jnp.sum(drawn, axis=1, keepdims=True) + tails
        scores = jnp.where(times > 0.0, scores, -3.0e38)
        weights = times * jnp.exp(scores - jnp.max(scores, axis=0, keepdims=True))
        weights = weights / jnp.sum(weights, axis=0, keepdims=True) - tails
        w_hi, w_lo = split2(weights)
        total = total + (dot_nn(w_lo, l_hi) + dot_nn(w_hi, l_lo) + dot_nn(w_hi, l_hi))
    first, second = total[0:HALF, :].T, total[HALF:ROWS, :].T
    keep_ref[...] = jnp.where(core == 0, first, second)
    send_ref[...] = jnp.where(core == 0, second, first)


def update_kernel(mine_ref, theirs_ref, entity_ref, state_ref, updated_ref, accum_ref):
    _, core = place()
    mine, theirs = mine_ref[...], theirs_ref[...]
    for j, gradient in enumerate((jnp.where(core == 0, mine, theirs), jnp.where(core == 0, theirs, mine))):
        span = slice(HALF * j, HALF * (j + 1))
        accum = state_ref[:, span] + jnp.sum(gradient * gradient, axis=0, keepdims=True) / float(D)
        accum_ref[:, span] = accum
        updated_ref[:, span] = entity_ref[:, span] - LEARN_RATE * gradient / jnp.sqrt(accum)


def call(kernel, out_shape, args, vmem, scratch=(), cost=None, space=pltpu.VMEM):
    out_shape = jax.tree.map(lambda s: jax.ShapeDtypeStruct(*s), out_shape, is_leaf=lambda s: isinstance(s, tuple))
    return pl.pallas_call(
        kernel,
        out_shape=out_shape,
        in_specs=[pl.BlockSpec(memory_space=space) for _ in args],
        out_specs=jax.tree.map(lambda _: pl.BlockSpec(memory_space=pltpu.VMEM), out_shape),
        scratch_shapes=list(scratch),
        compiler_params=pltpu.CompilerParams(vmem_limit_bytes=vmem * MIB),
        cost_estimate=cost,
        name=kernel.__name__,
    )(*args)


def flops(us):
    return pl.CostEstimate(flops=int(us * 1.0e9), bytes_accessed=4_000_000, transcendentals=0)


def shards(entity, state, relation, edge_head, edge_rel, edge_tail, negatives, counts, matching):
    swap_core = functools.partial(lax.ppermute, axis_name="core", perm=[(0, 1), (1, 0)])
    swap_zh = functools.partial(lax.ppermute, axis_name="zh", perm=[(0, 1), (1, 0)])
    exchange = functools.partial(lax.all_to_all, axis_name=("x", "yz"), split_axis=0, concat_axis=0, tiled=True)
    entity_t, relation_t = entity.T, relation.T

    payload, cols, give = call(
        pack_kernel,
        [((128 * CHUNK1, 128), F32), ((128, 128), F32), ((LIST, 128), F32)],
        (entity_t, edge_head, edge_rel, edge_tail, negatives, counts.transpose(1, 2, 0)),
        vmem=60,
        scratch=[pltpu.VMEM((128, 128), F32), pltpu.VMEM((D, ROWS), F32)]
        + [pltpu.VMEM((2, 1, 1, n), jnp.int32) for n in (SLOTS, SLOTS, SLOTS, NEGS)]
        + [pltpu.VMEM((1, 1, 2), jnp.int32), pltpu.SemaphoreType.DMA((6,))],
        space=pltpu.HBM,
    )
    spread = exchange(payload.reshape(128, 1, 128 * CHUNK1)).reshape(128 * CHUNK1, 128)

    bundle = swap_zh(call(bundle_kernel, ((PIECE + 8, MAIN), F32), (relation_t, give), vmem=8))
    near2 = swap_core(relation_t)

    routed = call(route_kernel, ((128 * CHUNK2, 128), F32), (spread, matching), vmem=16)
    fetched = exchange(routed.reshape(128, 1, 128 * CHUNK2)).reshape(128 * CHUNK2, 128)
    bundle, _ = lax.optimization_barrier((bundle, routed))
    far = lax.all_gather(bundle, "x", axis=0)
    far2 = swap_core(far)
    fetched_other = swap_core(fetched)
    given = swap_zh(call(given_kernel, ((LIST, 128), F32), (fetched,), vmem=4))
    rel_rows, left_hi, left_lo, first_rel, table_hi, table_lo, entity_hi, entity_lo, cols_other = call(
        relations_kernel,
        [
            ((2 * SLOTS, D), F32),
            ((2 * SLOTS, D), BF16),
            ((2 * SLOTS, D), BF16),
            ((SLOTS, D), F32),
            ((TABLE, D), BF16),
            ((TABLE, D), BF16),
            ((ROWS, D), BF16),
            ((ROWS, D), BF16),
            ((128, 128), F32),
        ],
        (entity_t, cols, bundle, relation_t, near2, far, far2, fetched),
        vmem=32,
        scratch=[pltpu.VMEM((2, D, MAIN), F32)],
        cost=flops(10),
    )
    block = [pltpu.VMEM((ROWS, D), BF16), pltpu.VMEM((ROWS, D), BF16)]
    head_grad = call(
        head_kernel,
        ((ROWS, D), F32),
        (fetched, fetched_other, cols, cols_other, rel_rows, left_hi, left_lo),
        vmem=20,
        scratch=block,
        cost=flops(6),
    )
    keep, send = call(
        tail_kernel,
        [((D, HALF), F32), ((D, HALF), F32)],
        (fetched, fetched_other, given, first_rel, entity_hi, entity_lo, table_hi, table_lo, head_grad),
        vmem=28,
        scratch=block,
        cost=flops(9),
    )
    half = keep + swap_core(send)
    half = half + swap_zh(half)
    other = swap_core(half)
    updated, accum = call(
        update_kernel,
        [((D, ROWS), F32), ((1, ROWS), F32)],
        (half, other, entity_t, state.reshape(1, ROWS)),
        vmem=8,
    )
    return updated.T, accum.reshape(ROWS)


def solution(mesh):
    parts = (PIECES, mesh.shape["dom"] // PIECES, 2, 2)
    fine = jax.sharding.Mesh(mesh.devices.reshape(parts), ("x", "yz", "zh", "core"))
    dom, edge = ("x", "yz"), ("zh", "core")
    return jax.shard_map(
        shards,
        mesh=fine,
        in_specs=(
            P(dom, None),
            P(dom),
            P(edge, None),
            P(None, dom, edge, None),
            P(None, dom, edge, None),
            P(None, dom, edge, None),
            P(None, dom, edge, None),
            P(None, dom, edge),
            P(),
        ),
        out_specs=(P(dom, None), P(dom)),
        check_vma=False,
    )
```

```python
import functools

import jax
import jax.numpy as jnp
from jax import lax
from jax.experimental import pallas as pl
from jax.experimental.pallas import tpu as pltpu
from jax.sharding import PartitionSpec as P


LEARN_RATE = 0.1
D = 400
ROWS = 512
HALF = 256
SLOTS = 512
NEGS = 320
REL_DEV = 528
PIECES = 4
PIECE = 104
MAIN = 512
REST = REL_DEV - MAIN
TABLE = 4 * REL_DEV
LIST = 16
CHUNK1 = 7
CHUNK2 = 13
GIVEN_CHUNK = 12
FIRST = 4 * D - 128 * GIVEN_CHUNK
F32 = jnp.float32
BF16 = jnp.bfloat16
MIB = 1024 * 1024


def split2(x):
    hi = x.astype(BF16)
    return hi, (x - hi.astype(F32)).astype(BF16)


def split3(x):
    hi = x.astype(BF16)
    rest = x - hi.astype(F32)
    mid = rest.astype(BF16)
    return hi, mid, (rest - mid.astype(F32)).astype(BF16)


def dot_nn(a, b):
    return lax.dot_general(a, b, (((1,), (0,)), ((), ())), preferred_element_type=F32)


def dot_nt(a, b):
    return lax.dot_general(a, b, (((1,), (1,)), ((), ())), preferred_element_type=F32)


def iota(shape, dim):
    return lax.broadcasted_iota(jnp.int32, shape, dim)


def place():
    return lax.axis_index("zh"), lax.axis_index("core")


def read_rows(ref, chunks):
    return jnp.concatenate([ref[pl.ds(k, 128, stride=chunks), :] for k in range(chunks)], axis=1)


def write_rows(ref, value, chunks):
    for k in range(chunks):
        ref[pl.ds(k, 128, stride=chunks), :] = value[:, 128 * k : 128 * (k + 1)]


def onehot_cols(lists, first, count, columns):
    blocks = [(lists[:, first + j : first + j + 1] == columns) for j in range(count)]
    return jnp.concatenate([jnp.where(b, 1.0, 0.0).astype(BF16) for b in blocks], axis=0)


def pack_kernel(
    entity_hbm, head_hbm, rel_hbm, tail_hbm, neg_hbm, count_hbm, out_ref, cols_ref, give_ref,
    rows_ref, entity_ref, head_ref, rel_ref, tail_ref, neg_ref, count_ref, sems,
):
    zh, core = place()
    pairs = (
        (head_hbm, head_ref), (rel_hbm, rel_ref), (tail_hbm, tail_ref), (neg_hbm, neg_ref), (count_hbm, count_ref),
        (entity_hbm, entity_ref),
    )
    copies = [pltpu.make_async_copy(a, b, sems.at[i]) for i, (a, b) in enumerate(pairs)]
    for copy in copies:
        copy.start()
    rows_ref[...] = jnp.full((128, 128), -1.0, F32)
    lane = iota((1, 128), 1)
    for copy in copies[:-1]:
        copy.wait()
    for bucket in range(2):
        at = bucket * LIST
        live = count_ref[0, :, bucket : bucket + 1]
        for j in range(4):
            span = pl.ds(128 * j, 128)
            head = jnp.where(lane + 128 * j < live, head_ref[bucket, 0, 0:1, span], -1)
            rows_ref[at + j : at + j + 1, :] = head.astype(F32)
            rows_ref[at + 4 + j : at + 5 + j, :] = rel_ref[bucket, 0, 0:1, span].astype(F32)
            rows_ref[at + 8 + j : at + 9 + j, :] = tail_ref[bucket, 0, 0:1, span].astype(F32)
        rows_ref[at + 12 : at + 13, :] = neg_ref[bucket, 0, 0:1, 0:128].astype(F32)
        rows_ref[at + 13 : at + 14, :] = neg_ref[bucket, 0, 0:1, 128:256].astype(F32)
        rows_ref[at + 14 : at + 15, 0:64] = neg_ref[bucket, 0, 0:1, 256:320].astype(F32)
    one, two = rows_ref[0:LIST, :], rows_ref[LIST : 2 * LIST, :]
    keep = jnp.where(zh == 0, one, two)
    give = jnp.where(zh == 0, two, one)
    both = jnp.concatenate([keep, give, rows_ref[2 * LIST :, :]], axis=0).T
    cols_ref[...] = both
    give_ref[...] = give
    copies[-1].wait()
    half = jnp.where(core == 0, entity_ref[:, 0:HALF], entity_ref[:, HALF:ROWS]).T
    payload = jnp.concatenate([half[0:128, :], half[128:HALF, :], both[:, 0 : 128 * CHUNK1 - 2 * D]], axis=1)
    write_rows(out_ref, payload, CHUNK1)


def route_kernel(x_ref, matching_ref, out_ref):
    zh, _ = place()
    parts = split3(read_rows(x_ref, CHUNK1))
    rows = iota((128, 128), 0)
    marks = [jnp.where(matching_ref[b : b + 1, :] == rows, 1.0, 0.0) for b in range(2)]
    back_keep = jnp.where(zh == 0, marks[0], marks[1])
    back_give = jnp.where(zh == 0, marks[1], marks[0])
    fore = back_keep.T.astype(BF16)
    back_keep, back_give = back_keep.astype(BF16), back_give.astype(BF16)
    partner = sum(dot_nn(fore, p) for p in reversed(parts))
    source = sum(dot_nn(back_keep, p) for p in reversed(parts))
    given = sum(dot_nn(back_give, p[:, 768 : 128 * CHUNK1]) for p in reversed(parts))
    fill = jnp.zeros((128, 128 * CHUNK2 - 4 * D - 2 * LIST), F32)
    routed = jnp.concatenate([partner[:, 0 : 2 * D], source[:, 0 : 2 * D + LIST], given[:, 48:64], fill], axis=1)
    write_rows(out_ref, routed, CHUNK2)


def table_row(rel, zh, core):
    owner = (rel >= REL_DEV).astype(jnp.int32) + (rel >= 2 * REL_DEV).astype(jnp.int32)
    owner = owner + (rel >= 3 * REL_DEV).astype(jnp.int32)
    off = rel - REL_DEV * owner
    owner_zh = (owner >= 2).astype(jnp.int32)
    other_core = (owner - 2 * owner_zh) != core
    return jnp.where(owner_zh == zh, 0, 2 * REL_DEV) + jnp.where(other_core, REL_DEV, 0) + off


def piece_start(spot):
    return min(PIECE * spot, D - PIECE)


def bundle_kernel(relation_ref, give_ref, out_ref):
    spot = lax.axis_index("x")
    start = pl.multiple_of(jnp.minimum(PIECE * spot, D - PIECE), 8)
    piece = relation_ref[pl.ds(start, PIECE), :]
    out_ref[0:PIECE, :] = piece[:, 0:MAIN]
    rest = jnp.concatenate([piece[:, MAIN:REL_DEV], jnp.zeros((PIECE, 128 - REST), F32)], axis=1)
    rest = jnp.concatenate([rest, jnp.zeros((128 - PIECE, 128), F32)], axis=0).T
    for g in range(4):
        out_ref[PIECE : PIECE + 4, 128 * g : 128 * (g + 1)] = rest[4 * g : 4 * g + 4, :]
        out_ref[PIECE + 4 : PIECE + 8, 128 * g : 128 * (g + 1)] = give_ref[4 * g : 4 * g + 4, :]


def unfold(rows):
    return jnp.concatenate([rows[:, 128 * g : 128 * (g + 1)] for g in range(4)], axis=0)


def gather_relations(lists, zh, core, table_hi, table_lo):
    rel_at = table_row(lists[:, 4:8].astype(jnp.int32), zh, core)
    rels = onehot_cols(rel_at, 0, 4, iota((128, TABLE), 1))
    return dot_nn(rels, table_hi[...]) + dot_nn(rels, table_lo[...])


def relations_kernel(
    entity_ref, cols_ref, bundle_ref, near_ref, near2_ref, far_ref, far2_ref, fetched_ref,
    rel_out, left_hi, left_lo, first_out, table_hi, table_lo, entity_hi, entity_lo, cols_out, far_table,
):
    zh, core = place()
    for k, ref in enumerate((near_ref, near2_ref)):
        hi, lo = split2(ref[...].T)
        table_hi[k * REL_DEV : (k + 1) * REL_DEV, :] = hi
        table_lo[k * REL_DEV : (k + 1) * REL_DEV, :] = lo
    for k, ref in enumerate((far_ref, far2_ref)):
        for spot in range(PIECES):
            far_table[k, piece_start(spot) : piece_start(spot) + PIECE, :] = ref[spot, 0:PIECE, :]
        at = (2 + k) * REL_DEV
        hi, lo = split2(far_table[k].T)
        table_hi[at : at + MAIN, :] = hi
        table_lo[at : at + MAIN, :] = lo
        rest = [unfold(ref[spot, PIECE : PIECE + 4, :]) for spot in range(PIECES)]
        rest = [rest[spot][:, 0:PIECE] for spot in range(PIECES - 1)] + [rest[-1][:, PIECES * PIECE - D : PIECE]]
        hi, lo = split2(jnp.concatenate(rest, axis=1))
        table_hi[at + MAIN : at + REL_DEV, :] = hi
        table_lo[at + MAIN : at + REL_DEV, :] = lo
    hi, lo = split2(entity_ref[...].T)
    entity_hi[...] = hi
    entity_lo[...] = lo
    own = iota((128, ROWS), 1).astype(F32)
    theirs = jnp.concatenate([unfold(bundle_ref[PIECE + 4 : PIECE + 8, :]), jnp.zeros((128 - LIST, 128), F32)], axis=0).T
    cols_out[...] = theirs
    for k, lists in enumerate((cols_ref[:, 0:LIST], theirs[:, 0:LIST])):
        heads = onehot_cols(lists, 0, 4, own)
        head_rows = dot_nn(heads, hi) + dot_nn(heads, lo)
        rel_rows = gather_relations(lists, zh, core, table_hi, table_lo)
        l_hi, l_lo = split2(head_rows * rel_rows)
        span = pl.ds(k * SLOTS, SLOTS)
        rel_out[span, :] = rel_rows
        left_hi[span, :] = l_hi
        left_lo[span, :] = l_lo
    chunk = fetched_ref[pl.ds(GIVEN_CHUNK, 128, stride=CHUNK2), :]
    first_out[...] = gather_relations(chunk[:, FIRST : FIRST + LIST], zh, core, table_hi, table_lo)


def fill_block(hi_ref, lo_ref, mine, theirs, first):
    for k, (rows, lane) in enumerate(((mine, 0), (mine, D), (theirs, 0), (theirs, D))):
        hi, lo = split2(rows[:, first + lane : first + lane + D])
        hi_ref[128 * k : 128 * (k + 1), :] = hi
        lo_ref[128 * k : 128 * (k + 1), :] = lo


def lists_rows(lists):
    return jnp.concatenate([lists, jnp.zeros((128, 128 - LIST), F32)], axis=1).T


def head_kernel(mine_ref, theirs_ref, lists_mine, lists_theirs, rel_ref, left_hi, left_lo, grad_ref, block_hi, block_lo):
    _, core = place()
    fill_block(block_hi, block_lo, read_rows(mine_ref, CHUNK2), read_rows(theirs_ref, CHUNK2), 0)
    numbers = jnp.bitwise_xor(iota((128, ROWS), 1), core * HALF).astype(F32)
    heads_at = iota((ROWS, 128), 0).astype(F32)
    total = None
    for k in range(2):
        lists = (lists_mine, lists_theirs)[k][:, 0:LIST]
        span = pl.ds(k * SLOTS, SLOTS)
        hi, lo = left_hi[span, :], left_lo[span, :]
        b_hi, b_lo = block_hi[...], block_lo[...]
        scores = dot_nt(hi, b_lo) + dot_nt(lo, b_hi) + dot_nt(hi, b_hi)
        tails = jnp.concatenate(
            [jnp.where(lists[:, 8 + j : 9 + j] == numbers, 1.0, 0.0) for j in range(4)], axis=0
        )
        drawn = sum(jnp.where(lists[:, 12 + j : 13 + j] == numbers, 1.0, 0.0) for j in range(3))
        times = jnp.sum(drawn, axis=0, keepdims=True) + tails
        scores = jnp.where(times > 0.0, scores, -3.0e38)
        weights = times * jnp.exp(scores - jnp.max(scores, axis=1, keepdims=True))
        weights = weights / jnp.sum(weights, axis=1, keepdims=True) - tails
        w_hi, w_lo = split2(weights)
        grad_left = dot_nn(w_hi, b_lo) + dot_nn(w_lo, b_hi) + dot_nn(w_hi, b_hi)
        g_hi, g_lo = split2(grad_left * rel_ref[span, :])
        rows = lists_rows(lists)
        marks = jnp.concatenate(
            [jnp.where(rows[j : j + 1, :] == heads_at, 1.0, 0.0) for j in range(4)], axis=1
        ).astype(BF16)
        part = dot_nn(marks, g_lo) + dot_nn(marks, g_hi)
        total = part if total is None else total + part
    grad_ref[...] = total


def given_kernel(fetched_ref, out_ref):
    out_ref[...] = fetched_ref[pl.ds(GIVEN_CHUNK, 128, stride=CHUNK2), :].T[FIRST + LIST : FIRST + 2 * LIST, :]


def tail_kernel(
    mine_ref, theirs_ref, given_ref, rel_ref, entity_hi, entity_lo, table_hi, table_lo, head_grad,
    keep0_ref, keep1_ref, send0_ref, send1_ref, block_hi, block_lo,
):
    zh, core = place()
    mine = read_rows(mine_ref, CHUNK2)
    fill_block(block_hi, block_lo, mine, read_rows(theirs_ref, CHUNK2), 2 * D)
    keep_refs, send_refs = (keep0_ref, keep1_ref), (send0_ref, send1_ref)
    e_hi, e_lo = entity_hi[...], entity_lo[...]
    numbers = jnp.bitwise_xor(iota((128, ROWS), 1), core * HALF).astype(F32)
    rows_at = iota((ROWS, 128), 0).astype(F32)
    total = head_grad[...]
    for k in range(2):
        if k == 0:
            lists = mine[:, 4 * D : 4 * D + LIST]
            rel_rows = rel_ref[...]
        else:
            lists = jnp.concatenate([given_ref[...], jnp.zeros((128 - LIST, 128), F32)], axis=0).T[:, 0:LIST]
            rel_rows = gather_relations(lists, zh, core, table_hi, table_lo)
        heads = onehot_cols(lists, 0, 4, numbers)
        head_rows = dot_nn(heads, block_hi[...]) + dot_nn(heads, block_lo[...])
        l_hi, l_lo = split2(head_rows * rel_rows)
        scores = dot_nt(e_lo, l_hi) + dot_nt(e_hi, l_lo) + dot_nt(e_hi, l_hi)
        rows = lists_rows(lists)
        tails = jnp.concatenate(
            [jnp.where(rows[8 + j : 9 + j, :] == rows_at, 1.0, 0.0) for j in range(4)], axis=1
        )
        drawn = sum(jnp.where(rows[12 + j : 13 + j, :] == rows_at, 1.0, 0.0) for j in range(3))
        times = jnp.sum(drawn, axis=1, keepdims=True) + tails
        scores = jnp.where(times > 0.0, scores, -3.0e38)
        weights = times * jnp.exp(scores - jnp.max(scores, axis=0, keepdims=True))
        weights = weights / jnp.sum(weights, axis=0, keepdims=True) - tails
        w_hi, w_lo = split2(weights)
        total = total + (dot_nn(w_lo, l_hi) + dot_nn(w_hi, l_lo) + dot_nn(w_hi, l_hi))
    first, second = total[0:HALF, :].T, total[HALF:ROWS, :].T
    keep, send = jnp.where(core == 0, first, second), jnp.where(core == 0, second, first)
    for k in range(2):
        keep_refs[k][...] = keep[k * D // 2 : (k + 1) * D // 2, :]
        send_refs[k][...] = send[k * D // 2 : (k + 1) * D // 2, :]


def update_kernel(mine0_ref, mine1_ref, theirs0_ref, theirs1_ref, entity_ref, state_ref, updated_ref, accum_ref):
    _, core = place()
    mine = jnp.concatenate([mine0_ref[...], mine1_ref[...]], axis=0)
    theirs = jnp.concatenate([theirs0_ref[...], theirs1_ref[...]], axis=0)
    for j, gradient in enumerate((jnp.where(core == 0, mine, theirs), jnp.where(core == 0, theirs, mine))):
        span = slice(HALF * j, HALF * (j + 1))
        accum = state_ref[:, span] + jnp.sum(gradient * gradient, axis=0, keepdims=True) / float(D)
        accum_ref[:, span] = accum
        updated_ref[:, span] = entity_ref[:, span] - LEARN_RATE * gradient / jnp.sqrt(accum)


def call(kernel, out_shape, args, vmem, scratch=(), cost=None, space=pltpu.VMEM):
    out_shape = jax.tree.map(lambda s: jax.ShapeDtypeStruct(*s), out_shape, is_leaf=lambda s: isinstance(s, tuple))
    return pl.pallas_call(
        kernel,
        out_shape=out_shape,
        in_specs=[pl.BlockSpec(memory_space=space) for _ in args],
        out_specs=jax.tree.map(lambda _: pl.BlockSpec(memory_space=pltpu.VMEM), out_shape),
        scratch_shapes=list(scratch),
        compiler_params=pltpu.CompilerParams(vmem_limit_bytes=vmem * MIB),
        cost_estimate=cost,
        name=kernel.__name__,
    )(*args)


def flops(us):
    return pl.CostEstimate(flops=int(us * 1.0e9), bytes_accessed=4_000_000, transcendentals=0)


def shards(entity, state, relation, edge_head, edge_rel, edge_tail, negatives, counts, matching):
    swap_core = functools.partial(lax.ppermute, axis_name="core", perm=[(0, 1), (1, 0)])
    swap_zh = functools.partial(lax.ppermute, axis_name="zh", perm=[(0, 1), (1, 0)])
    exchange = functools.partial(lax.all_to_all, axis_name=("x", "yz"), split_axis=0, concat_axis=0, tiled=True)
    entity_t, relation_t = entity.T, relation.T

    payload, cols, give = call(
        pack_kernel,
        [((128 * CHUNK1, 128), F32), ((128, 128), F32), ((LIST, 128), F32)],
        (entity_t, edge_head, edge_rel, edge_tail, negatives, counts.transpose(1, 2, 0)),
        vmem=60,
        scratch=[pltpu.VMEM((128, 128), F32), pltpu.VMEM((D, ROWS), F32)]
        + [pltpu.VMEM((2, 1, 1, n), jnp.int32) for n in (SLOTS, SLOTS, SLOTS, NEGS)]
        + [pltpu.VMEM((1, 1, 2), jnp.int32), pltpu.SemaphoreType.DMA((6,))],
        space=pltpu.HBM,
    )
    spread = exchange(payload.reshape(128, 1, 128 * CHUNK1)).reshape(128 * CHUNK1, 128)

    bundle = swap_zh(call(bundle_kernel, ((PIECE + 8, MAIN), F32), (relation_t, give), vmem=8))
    near2 = swap_core(relation_t)
    spread, bundle = lax.optimization_barrier((spread, bundle))

    routed = call(route_kernel, ((128 * CHUNK2, 128), F32), (spread, matching), vmem=16)
    fetched = exchange(routed.reshape(128, 1, 128 * CHUNK2)).reshape(128 * CHUNK2, 128)
    bundle, _ = lax.optimization_barrier((bundle, routed))
    far = lax.all_gather(bundle, "x", axis=0)
    far2 = swap_core(far)
    fetched_other = swap_core(fetched)
    given = swap_zh(call(given_kernel, ((LIST, 128), F32), (fetched,), vmem=4))
    rel_rows, left_hi, left_lo, first_rel, table_hi, table_lo, entity_hi, entity_lo, cols_other = call(
        relations_kernel,
        [
            ((2 * SLOTS, D), F32),
            ((2 * SLOTS, D), BF16),
            ((2 * SLOTS, D), BF16),
            ((SLOTS, D), F32),
            ((TABLE, D), BF16),
            ((TABLE, D), BF16),
            ((ROWS, D), BF16),
            ((ROWS, D), BF16),
            ((128, 128), F32),
        ],
        (entity_t, cols, bundle, relation_t, near2, far, far2, fetched),
        vmem=32,
        scratch=[pltpu.VMEM((2, D, MAIN), F32)],
        cost=flops(10),
    )
    block = [pltpu.VMEM((ROWS, D), BF16), pltpu.VMEM((ROWS, D), BF16)]
    head_grad = call(
        head_kernel,
        ((ROWS, D), F32),
        (fetched, fetched_other, cols, cols_other, rel_rows, left_hi, left_lo),
        vmem=20,
        scratch=block,
        cost=flops(6),
    )
    parts = call(
        tail_kernel,
        [((D // 2, HALF), F32)] * 4,
        (fetched, fetched_other, given, first_rel, entity_hi, entity_lo, table_hi, table_lo, head_grad),
        vmem=28,
        scratch=block,
        cost=flops(9),
    )
    halves = [keep + swap_core(send) for keep, send in zip(parts[:2], parts[2:])]
    halves = [half + swap_zh(half) for half in halves]
    others = [swap_core(half) for half in halves]
    updated, accum = call(
        update_kernel,
        [((D, ROWS), F32), ((1, ROWS), F32)],
        (*halves, *others, entity_t, state.reshape(1, ROWS)),
        vmem=8,
    )
    return updated.T, accum.reshape(ROWS)


def solution(mesh):
    parts = (PIECES, mesh.shape["dom"] // PIECES, 2, 2)
    fine = jax.sharding.Mesh(mesh.devices.reshape(parts), ("x", "yz", "zh", "core"))
    dom, edge = ("x", "yz"), ("zh", "core")
    return jax.shard_map(
        shards,
        mesh=fine,
        in_specs=(
            P(dom, None),
            P(dom),
            P(edge, None),
            P(None, dom, edge, None),
            P(None, dom, edge, None),
            P(None, dom, edge, None),
            P(None, dom, edge, None),
            P(None, dom, edge),
            P(),
        ),
        out_specs=(P(dom, None), P(dom)),
        check_vma=False,
    )
```

```python
import functools

import jax
import jax.numpy as jnp
from jax import lax
from jax.experimental import pallas as pl
from jax.experimental.pallas import tpu as pltpu
from jax.sharding import PartitionSpec as P


LEARN_RATE = 0.1
D = 400
ROWS = 512
HALF = 256
SLOTS = 512
NEGS = 320
REL_DEV = 528
PIECES = 4
PIECE = 104
MAIN = 512
REST = REL_DEV - MAIN
TABLE = 4 * REL_DEV
LIST = 16
CHUNK1 = 7
CHUNK2 = 13
GIVEN_CHUNK = 12
FIRST = 4 * D - 128 * GIVEN_CHUNK
F32 = jnp.float32
BF16 = jnp.bfloat16
MIB = 1024 * 1024


def split2(x):
    hi = x.astype(BF16)
    return hi, (x - hi.astype(F32)).astype(BF16)


def split3(x):
    hi = x.astype(BF16)
    rest = x - hi.astype(F32)
    mid = rest.astype(BF16)
    return hi, mid, (rest - mid.astype(F32)).astype(BF16)


def dot_nn(a, b):
    return lax.dot_general(a, b, (((1,), (0,)), ((), ())), preferred_element_type=F32)


def dot_nt(a, b):
    return lax.dot_general(a, b, (((1,), (1,)), ((), ())), preferred_element_type=F32)


def iota(shape, dim):
    return lax.broadcasted_iota(jnp.int32, shape, dim)


def place():
    return lax.axis_index("zh"), lax.axis_index("core")


def read_rows(ref, chunks):
    return jnp.concatenate([ref[pl.ds(k, 128, stride=chunks), :] for k in range(chunks)], axis=1)


def write_rows(ref, value, chunks):
    for k in range(chunks):
        ref[pl.ds(k, 128, stride=chunks), :] = value[:, 128 * k : 128 * (k + 1)]


def onehot_cols(lists, first, count, columns):
    blocks = [(lists[:, first + j : first + j + 1] == columns) for j in range(count)]
    return jnp.concatenate([jnp.where(b, 1.0, 0.0).astype(BF16) for b in blocks], axis=0)


def pack_kernel(
    entity_hbm, head_hbm, rel_hbm, tail_hbm, neg_hbm, count_hbm, out_ref, cols_ref, give_ref,
    rows_ref, entity_ref, head_ref, rel_ref, tail_ref, neg_ref, count_ref, sems,
):
    zh, core = place()
    pairs = (
        (head_hbm, head_ref), (rel_hbm, rel_ref), (tail_hbm, tail_ref), (neg_hbm, neg_ref), (count_hbm, count_ref),
        (entity_hbm, entity_ref),
    )
    copies = [pltpu.make_async_copy(a, b, sems.at[i]) for i, (a, b) in enumerate(pairs)]
    for copy in copies:
        copy.start()
    rows_ref[...] = jnp.full((128, 128), -1.0, F32)
    lane = iota((1, 128), 1)
    for copy in copies[:-1]:
        copy.wait()
    for bucket in range(2):
        at = bucket * LIST
        live = count_ref[0, :, bucket : bucket + 1]
        for j in range(4):
            span = pl.ds(128 * j, 128)
            head = jnp.where(lane + 128 * j < live, head_ref[bucket, 0, 0:1, span], -1)
            rows_ref[at + j : at + j + 1, :] = head.astype(F32)
            rows_ref[at + 4 + j : at + 5 + j, :] = rel_ref[bucket, 0, 0:1, span].astype(F32)
            rows_ref[at + 8 + j : at + 9 + j, :] = tail_ref[bucket, 0, 0:1, span].astype(F32)
        rows_ref[at + 12 : at + 13, :] = neg_ref[bucket, 0, 0:1, 0:128].astype(F32)
        rows_ref[at + 13 : at + 14, :] = neg_ref[bucket, 0, 0:1, 128:256].astype(F32)
        rows_ref[at + 14 : at + 15, 0:64] = neg_ref[bucket, 0, 0:1, 256:320].astype(F32)
    one, two = rows_ref[0:LIST, :], rows_ref[LIST : 2 * LIST, :]
    keep = jnp.where(zh == 0, one, two)
    give = jnp.where(zh == 0, two, one)
    both = jnp.concatenate([keep, give, rows_ref[2 * LIST :, :]], axis=0).T
    cols_ref[...] = both
    give_ref[...] = give
    copies[-1].wait()
    half = jnp.where(core == 0, entity_ref[:, 0:HALF], entity_ref[:, HALF:ROWS]).T
    payload = jnp.concatenate([half[0:128, :], half[128:HALF, :], both[:, 0 : 128 * CHUNK1 - 2 * D]], axis=1)
    write_rows(out_ref, payload, CHUNK1)


def route_kernel(x_ref, matching_ref, out_ref):
    zh, _ = place()
    parts = split3(read_rows(x_ref, CHUNK1))
    rows = iota((128, 128), 0)
    marks = [jnp.where(matching_ref[b : b + 1, :] == rows, 1.0, 0.0) for b in range(2)]
    back_keep = jnp.where(zh == 0, marks[0], marks[1])
    back_give = jnp.where(zh == 0, marks[1], marks[0])
    fore = back_keep.T.astype(BF16)
    back_keep, back_give = back_keep.astype(BF16), back_give.astype(BF16)
    partner = sum(dot_nn(fore, p) for p in reversed(parts))
    source = sum(dot_nn(back_keep, p) for p in reversed(parts))
    given = sum(dot_nn(back_give, p[:, 768 : 128 * CHUNK1]) for p in reversed(parts))
    fill = jnp.zeros((128, 128 * CHUNK2 - 4 * D - 2 * LIST), F32)
    routed = jnp.concatenate([partner[:, 0 : 2 * D], source[:, 0 : 2 * D + LIST], given[:, 48:64], fill], axis=1)
    write_rows(out_ref, routed, CHUNK2)


def table_row(rel, zh, core):
    owner = (rel >= REL_DEV).astype(jnp.int32) + (rel >= 2 * REL_DEV).astype(jnp.int32)
    owner = owner + (rel >= 3 * REL_DEV).astype(jnp.int32)
    off = rel - REL_DEV * owner
    owner_zh = (owner >= 2).astype(jnp.int32)
    other_core = (owner - 2 * owner_zh) != core
    return jnp.where(owner_zh == zh, 0, 2 * REL_DEV) + jnp.where(other_core, REL_DEV, 0) + off


def piece_start(spot):
    return min(PIECE * spot, D - PIECE)


def bundle_kernel(relation_ref, give_ref, out_ref):
    spot = lax.axis_index("x")
    start = pl.multiple_of(jnp.minimum(PIECE * spot, D - PIECE), 8)
    piece = relation_ref[pl.ds(start, PIECE), :]
    out_ref[0:PIECE, :] = piece[:, 0:MAIN]
    rest = jnp.concatenate([piece[:, MAIN:REL_DEV], jnp.zeros((PIECE, 128 - REST), F32)], axis=1)
    rest = jnp.concatenate([rest, jnp.zeros((128 - PIECE, 128), F32)], axis=0).T
    for g in range(4):
        out_ref[PIECE : PIECE + 4, 128 * g : 128 * (g + 1)] = rest[4 * g : 4 * g + 4, :]
        out_ref[PIECE + 4 : PIECE + 8, 128 * g : 128 * (g + 1)] = give_ref[4 * g : 4 * g + 4, :]


def unfold(rows):
    return jnp.concatenate([rows[:, 128 * g : 128 * (g + 1)] for g in range(4)], axis=0)


def store_relations(table_ref, first, rows):
    padded = jnp.concatenate([rows, jnp.zeros((rows.shape[0], 512 - D), F32)], axis=1)
    for k in range(4):
        table_ref[pl.ds(4 * first + k, rows.shape[0], stride=4), :] = padded[:, 128 * k : 128 * (k + 1)]


def load_indices(rels, zh, core, index_vmem, index_smem, sem):
    rels = jnp.concatenate([rels, jnp.zeros((16 - rels.shape[0], 128), F32)], axis=0)
    index_vmem[...] = table_row(rels.astype(jnp.int32), zh, core)
    copy = pltpu.make_async_copy(index_vmem, index_smem, sem)
    copy.start()
    copy.wait()


def gather_relations(table_ref, index_smem, first, out_ref):
    def body(step, _):
        for j in range(4):
            for u in range(8):
                lane = step * 8 + u
                at = pl.multiple_of(4 * index_smem[first + j, lane], 4)
                to = pl.multiple_of(512 * j + 4 * lane, 4)
                out_ref[pl.ds(to, 4), :] = table_ref[pl.ds(at, 4), :]
        return 0

    lax.fori_loop(0, 16, body, 0)
    return jnp.concatenate([out_ref[pl.ds(k, SLOTS, stride=4), :] for k in range(4)], axis=1)[:, 0:D]


def gather_heads(lists, hi, lo):
    heads = onehot_cols(lists, 0, 4, iota((128, ROWS), 1).astype(F32))
    return dot_nn(heads, hi) + dot_nn(heads, lo)


def relations_kernel(
    entity_ref, cols_ref, bundle_ref, near_ref, near2_ref, far_ref, far2_ref, fetched_ref,
    rel_out, left_hi, left_lo, first_out, table_ref, entity_hi, entity_lo, cols_out,
    far_table, gathered, index_vmem, index_smem, sem,
):
    zh, core = place()
    theirs = unfold(bundle_ref[PIECE + 4 : PIECE + 8, :])
    chunk = fetched_ref[pl.ds(GIVEN_CHUNK, 128, stride=CHUNK2), :].T
    rels = jnp.concatenate([cols_ref[...].T[4:8, :], theirs[4:8, :], chunk[FIRST + 4 : FIRST + 8, :]], axis=0)
    load_indices(rels, zh, core, index_vmem, index_smem, sem)
    for k, ref in enumerate((near_ref, near2_ref)):
        store_relations(table_ref, k * REL_DEV, ref[...].T)
    for k, ref in enumerate((far_ref, far2_ref)):
        for spot in range(PIECES):
            far_table[k, piece_start(spot) : piece_start(spot) + PIECE, :] = ref[spot, 0:PIECE, :]
        store_relations(table_ref, (2 + k) * REL_DEV, far_table[k].T)
        rest = [unfold(ref[spot, PIECE : PIECE + 4, :]) for spot in range(PIECES)]
        rest = [rest[spot][:, 0:PIECE] for spot in range(PIECES - 1)] + [rest[-1][:, PIECES * PIECE - D : PIECE]]
        store_relations(table_ref, (2 + k) * REL_DEV + MAIN, jnp.concatenate(rest, axis=1))
    theirs = jnp.concatenate([theirs, jnp.zeros((128 - LIST, 128), F32)], axis=0).T
    cols_out[...] = theirs
    hi, lo = split2(entity_ref[...].T)
    entity_hi[...] = hi
    entity_lo[...] = lo
    for k in range(2):
        head_rows = gather_heads((cols_ref, theirs)[k][:, 0:LIST], hi, lo)
        rel_rows = gather_relations(table_ref, index_smem, 4 * k, gathered)
        l_hi, l_lo = split2(head_rows * rel_rows)
        span = pl.ds(k * SLOTS, SLOTS)
        rel_out[span, :] = rel_rows
        left_hi[span, :] = l_hi
        left_lo[span, :] = l_lo
    first_out[...] = gather_relations(table_ref, index_smem, 8, gathered)


def fill_block(hi_ref, lo_ref, mine, theirs, first):
    for k, (rows, lane) in enumerate(((mine, 0), (mine, D), (theirs, 0), (theirs, D))):
        hi, lo = split2(rows[:, first + lane : first + lane + D])
        hi_ref[128 * k : 128 * (k + 1), :] = hi
        lo_ref[128 * k : 128 * (k + 1), :] = lo


def lists_rows(lists):
    return jnp.concatenate([lists, jnp.zeros((128, 128 - LIST), F32)], axis=1).T


def head_kernel(mine_ref, theirs_ref, lists_mine, lists_theirs, rel_ref, left_hi, left_lo, grad_ref, block_hi, block_lo):
    _, core = place()
    fill_block(block_hi, block_lo, read_rows(mine_ref, CHUNK2), read_rows(theirs_ref, CHUNK2), 0)
    numbers = jnp.bitwise_xor(iota((128, ROWS), 1), core * HALF).astype(F32)
    heads_at = iota((ROWS, 128), 0).astype(F32)
    total = None
    for k in range(2):
        lists = (lists_mine, lists_theirs)[k][:, 0:LIST]
        span = pl.ds(k * SLOTS, SLOTS)
        hi, lo = left_hi[span, :], left_lo[span, :]
        b_hi, b_lo = block_hi[...], block_lo[...]
        scores = dot_nt(hi, b_lo) + dot_nt(lo, b_hi) + dot_nt(hi, b_hi)
        tails = jnp.concatenate(
            [jnp.where(lists[:, 8 + j : 9 + j] == numbers, 1.0, 0.0) for j in range(4)], axis=0
        )
        drawn = sum(jnp.where(lists[:, 12 + j : 13 + j] == numbers, 1.0, 0.0) for j in range(3))
        times = jnp.sum(drawn, axis=0, keepdims=True) + tails
        scores = jnp.where(times > 0.0, scores, -3.0e38)
        weights = times * jnp.exp(scores - jnp.max(scores, axis=1, keepdims=True))
        weights = weights / jnp.sum(weights, axis=1, keepdims=True) - tails
        w_hi, w_lo = split2(weights)
        grad_left = dot_nn(w_hi, b_lo) + dot_nn(w_lo, b_hi) + dot_nn(w_hi, b_hi)
        g_hi, g_lo = split2(grad_left * rel_ref[span, :])
        rows = lists_rows(lists)
        marks = jnp.concatenate(
            [jnp.where(rows[j : j + 1, :] == heads_at, 1.0, 0.0) for j in range(4)], axis=1
        ).astype(BF16)
        part = dot_nn(marks, g_lo) + dot_nn(marks, g_hi)
        total = part if total is None else total + part
    grad_ref[...] = total


def given_kernel(fetched_ref, out_ref):
    out_ref[...] = fetched_ref[pl.ds(GIVEN_CHUNK, 128, stride=CHUNK2), :].T[FIRST + LIST : FIRST + 2 * LIST, :]


def tail_kernel(
    mine_ref, theirs_ref, given_ref, rel_ref, entity_hi, entity_lo, table_ref, head_grad,
    keep0_ref, keep1_ref, send0_ref, send1_ref, block_hi, block_lo, gathered, index_vmem, index_smem, sem,
):
    zh, core = place()
    mine = read_rows(mine_ref, CHUNK2)
    fill_block(block_hi, block_lo, mine, read_rows(theirs_ref, CHUNK2), 2 * D)
    keep_refs, send_refs = (keep0_ref, keep1_ref), (send0_ref, send1_ref)
    e_hi, e_lo = entity_hi[...], entity_lo[...]
    numbers = jnp.bitwise_xor(iota((128, ROWS), 1), core * HALF).astype(F32)
    rows_at = iota((ROWS, 128), 0).astype(F32)
    total = head_grad[...]
    for k in range(2):
        if k == 0:
            lists = mine[:, 4 * D : 4 * D + LIST]
            rel_rows = rel_ref[...]
        else:
            lists = jnp.concatenate([given_ref[...], jnp.zeros((128 - LIST, 128), F32)], axis=0).T[:, 0:LIST]
            load_indices(given_ref[4:8, :], zh, core, index_vmem, index_smem, sem)
            rel_rows = gather_relations(table_ref, index_smem, 0, gathered)
        heads = onehot_cols(lists, 0, 4, numbers)
        head_rows = dot_nn(heads, block_hi[...]) + dot_nn(heads, block_lo[...])
        l_hi, l_lo = split2(head_rows * rel_rows)
        scores = dot_nt(e_lo, l_hi) + dot_nt(e_hi, l_lo) + dot_nt(e_hi, l_hi)
        rows = lists_rows(lists)
        tails = jnp.concatenate(
            [jnp.where(rows[8 + j : 9 + j, :] == rows_at, 1.0, 0.0) for j in range(4)], axis=1
        )
        drawn = sum(jnp.where(rows[12 + j : 13 + j, :] == rows_at, 1.0, 0.0) for j in range(3))
        times = jnp.sum(drawn, axis=1, keepdims=True) + tails
        scores = jnp.where(times > 0.0, scores, -3.0e38)
        weights = times * jnp.exp(scores - jnp.max(scores, axis=0, keepdims=True))
        weights = weights / jnp.sum(weights, axis=0, keepdims=True) - tails
        w_hi, w_lo = split2(weights)
        total = total + (dot_nn(w_lo, l_hi) + dot_nn(w_hi, l_lo) + dot_nn(w_hi, l_hi))
    first, second = total[0:HALF, :].T, total[HALF:ROWS, :].T
    keep, send = jnp.where(core == 0, first, second), jnp.where(core == 0, second, first)
    for k in range(2):
        keep_refs[k][...] = keep[k * D // 2 : (k + 1) * D // 2, :]
        send_refs[k][...] = send[k * D // 2 : (k + 1) * D // 2, :]


def update_kernel(mine0_ref, mine1_ref, theirs0_ref, theirs1_ref, entity_ref, state_ref, updated_ref, accum_ref):
    _, core = place()
    mine = jnp.concatenate([mine0_ref[...], mine1_ref[...]], axis=0)
    theirs = jnp.concatenate([theirs0_ref[...], theirs1_ref[...]], axis=0)
    for j, gradient in enumerate((jnp.where(core == 0, mine, theirs), jnp.where(core == 0, theirs, mine))):
        span = slice(HALF * j, HALF * (j + 1))
        accum = state_ref[:, span] + jnp.sum(gradient * gradient, axis=0, keepdims=True) / float(D)
        accum_ref[:, span] = accum
        updated_ref[:, span] = entity_ref[:, span] - LEARN_RATE * gradient / jnp.sqrt(accum)


def call(kernel, out_shape, args, vmem, scratch=(), cost=None, space=pltpu.VMEM):
    out_shape = jax.tree.map(lambda s: jax.ShapeDtypeStruct(*s), out_shape, is_leaf=lambda s: isinstance(s, tuple))
    return pl.pallas_call(
        kernel,
        out_shape=out_shape,
        in_specs=[pl.BlockSpec(memory_space=space) for _ in args],
        out_specs=jax.tree.map(lambda _: pl.BlockSpec(memory_space=pltpu.VMEM), out_shape),
        scratch_shapes=list(scratch),
        compiler_params=pltpu.CompilerParams(vmem_limit_bytes=vmem * MIB),
        cost_estimate=cost,
        name=kernel.__name__,
    )(*args)


def flops(us):
    return pl.CostEstimate(flops=int(us * 1.0e9), bytes_accessed=4_000_000, transcendentals=0)


def shards(entity, state, relation, edge_head, edge_rel, edge_tail, negatives, counts, matching):
    swap_core = functools.partial(lax.ppermute, axis_name="core", perm=[(0, 1), (1, 0)])
    swap_zh = functools.partial(lax.ppermute, axis_name="zh", perm=[(0, 1), (1, 0)])
    exchange = functools.partial(lax.all_to_all, axis_name=("x", "yz"), split_axis=0, concat_axis=0, tiled=True)
    entity_t, relation_t = entity.T, relation.T

    payload, cols, give = call(
        pack_kernel,
        [((128 * CHUNK1, 128), F32), ((128, 128), F32), ((LIST, 128), F32)],
        (entity_t, edge_head, edge_rel, edge_tail, negatives, counts.transpose(1, 2, 0)),
        vmem=60,
        scratch=[pltpu.VMEM((128, 128), F32), pltpu.VMEM((D, ROWS), F32)]
        + [pltpu.VMEM((2, 1, 1, n), jnp.int32) for n in (SLOTS, SLOTS, SLOTS, NEGS)]
        + [pltpu.VMEM((1, 1, 2), jnp.int32), pltpu.SemaphoreType.DMA((6,))],
        space=pltpu.HBM,
    )
    spread = exchange(payload.reshape(128, 1, 128 * CHUNK1)).reshape(128 * CHUNK1, 128)

    bundle = swap_zh(call(bundle_kernel, ((PIECE + 8, MAIN), F32), (relation_t, give), vmem=8))
    near2 = swap_core(relation_t)
    spread, bundle = lax.optimization_barrier((spread, bundle))

    routed = call(route_kernel, ((128 * CHUNK2, 128), F32), (spread, matching), vmem=16)
    fetched = exchange(routed.reshape(128, 1, 128 * CHUNK2)).reshape(128 * CHUNK2, 128)
    bundle, _ = lax.optimization_barrier((bundle, routed))
    far = lax.all_gather(bundle, "x", axis=0)
    far2 = swap_core(far)
    fetched_other = swap_core(fetched)
    given = swap_zh(call(given_kernel, ((LIST, 128), F32), (fetched,), vmem=4))
    gather = [
        pltpu.VMEM((4 * SLOTS, 128), F32),
        pltpu.VMEM((16, 128), jnp.int32),
        pltpu.SMEM((16, 128), jnp.int32),
        pltpu.SemaphoreType.DMA,
    ]
    rel_rows, left_hi, left_lo, first_rel, table, entity_hi, entity_lo, cols_other = call(
        relations_kernel,
        [
            ((2 * SLOTS, D), F32),
            ((2 * SLOTS, D), BF16),
            ((2 * SLOTS, D), BF16),
            ((SLOTS, D), F32),
            ((4 * TABLE, 128), F32),
            ((ROWS, D), BF16),
            ((ROWS, D), BF16),
            ((128, 128), F32),
        ],
        (entity_t, cols, bundle, relation_t, near2, far, far2, fetched),
        vmem=32,
        scratch=[pltpu.VMEM((2, D, MAIN), F32)] + gather,
        cost=flops(6),
    )
    block = [pltpu.VMEM((ROWS, D), BF16), pltpu.VMEM((ROWS, D), BF16)]
    head_grad = call(
        head_kernel,
        ((ROWS, D), F32),
        (fetched, fetched_other, cols, cols_other, rel_rows, left_hi, left_lo),
        vmem=20,
        scratch=block,
        cost=flops(6),
    )
    parts = call(
        tail_kernel,
        [((D // 2, HALF), F32)] * 4,
        (fetched, fetched_other, given, first_rel, entity_hi, entity_lo, table, head_grad),
        vmem=28,
        scratch=block + gather,
        cost=flops(9),
    )
    halves = [keep + swap_core(send) for keep, send in zip(parts[:2], parts[2:])]
    halves = [half + swap_zh(half) for half in halves]
    others = [swap_core(half) for half in halves]
    updated, accum = call(
        update_kernel,
        [((D, ROWS), F32), ((1, ROWS), F32)],
        (*halves, *others, entity_t, state.reshape(1, ROWS)),
        vmem=8,
    )
    return updated.T, accum.reshape(ROWS)


def solution(mesh):
    parts = (PIECES, mesh.shape["dom"] // PIECES, 2, 2)
    fine = jax.sharding.Mesh(mesh.devices.reshape(parts), ("x", "yz", "zh", "core"))
    dom, edge = ("x", "yz"), ("zh", "core")
    return jax.shard_map(
        shards,
        mesh=fine,
        in_specs=(
            P(dom, None),
            P(dom),
            P(edge, None),
            P(None, dom, edge, None),
            P(None, dom, edge, None),
            P(None, dom, edge, None),
            P(None, dom, edge, None),
            P(None, dom, edge),
            P(),
        ),
        out_specs=(P(dom, None), P(dom)),
        check_vma=False,
    )
```

```python
import functools

import jax
import jax.numpy as jnp
from jax import lax
from jax.experimental import pallas as pl
from jax.experimental.pallas import tpu as pltpu
from jax.sharding import PartitionSpec as P


LEARN_RATE = 0.1
D = 400
ROWS = 512
HALF = 256
SLOTS = 512
NEGS = 320
REL_DEV = 528
PIECES = 4
PIECE = 104
MAIN = 512
REST = REL_DEV - MAIN
TABLE = 4 * REL_DEV
LIST = 16
CHUNK1 = 7
CHUNK2 = 13
GIVEN_CHUNK = 12
FIRST = 4 * D - 128 * GIVEN_CHUNK
F32 = jnp.float32
BF16 = jnp.bfloat16
MIB = 1024 * 1024


def split2(x):
    hi = x.astype(BF16)
    return hi, (x - hi.astype(F32)).astype(BF16)


def split3(x):
    hi = x.astype(BF16)
    rest = x - hi.astype(F32)
    mid = rest.astype(BF16)
    return hi, mid, (rest - mid.astype(F32)).astype(BF16)


def dot_nn(a, b):
    return lax.dot_general(a, b, (((1,), (0,)), ((), ())), preferred_element_type=F32)


def dot_nt(a, b):
    return lax.dot_general(a, b, (((1,), (1,)), ((), ())), preferred_element_type=F32)


def iota(shape, dim):
    return lax.broadcasted_iota(jnp.int32, shape, dim)


def place():
    return lax.axis_index("zh"), lax.axis_index("core")


def read_rows(ref, chunks):
    return jnp.concatenate([ref[pl.ds(k, 128, stride=chunks), :] for k in range(chunks)], axis=1)


def write_rows(ref, value, chunks):
    for k in range(chunks):
        ref[pl.ds(k, 128, stride=chunks), :] = value[:, 128 * k : 128 * (k + 1)]


def onehot_cols(lists, first, count, columns):
    blocks = [(lists[:, first + j : first + j + 1] == columns) for j in range(count)]
    return jnp.concatenate([jnp.where(b, 1.0, 0.0).astype(BF16) for b in blocks], axis=0)


def pack_kernel(
    entity_hbm, head_hbm, rel_hbm, tail_hbm, neg_hbm, count_hbm, out_ref, cols_ref, give_ref,
    rows_ref, entity_ref, head_ref, rel_ref, tail_ref, neg_ref, count_ref, sems,
):
    zh, core = place()
    pairs = (
        (head_hbm, head_ref), (rel_hbm, rel_ref), (tail_hbm, tail_ref), (neg_hbm, neg_ref), (count_hbm, count_ref),
        (entity_hbm, entity_ref),
    )
    copies = [pltpu.make_async_copy(a, b, sems.at[i]) for i, (a, b) in enumerate(pairs)]
    for copy in copies:
        copy.start()
    rows_ref[...] = jnp.full((128, 128), -1.0, F32)
    lane = iota((1, 128), 1)
    for copy in copies[:-1]:
        copy.wait()
    for bucket in range(2):
        at = bucket * LIST
        live = count_ref[0, :, bucket : bucket + 1]
        for j in range(4):
            span = pl.ds(128 * j, 128)
            head = jnp.where(lane + 128 * j < live, head_ref[bucket, 0, 0:1, span], -1)
            rows_ref[at + j : at + j + 1, :] = head.astype(F32)
            rows_ref[at + 4 + j : at + 5 + j, :] = rel_ref[bucket, 0, 0:1, span].astype(F32)
            rows_ref[at + 8 + j : at + 9 + j, :] = tail_ref[bucket, 0, 0:1, span].astype(F32)
        rows_ref[at + 12 : at + 13, :] = neg_ref[bucket, 0, 0:1, 0:128].astype(F32)
        rows_ref[at + 13 : at + 14, :] = neg_ref[bucket, 0, 0:1, 128:256].astype(F32)
        rows_ref[at + 14 : at + 15, 0:64] = neg_ref[bucket, 0, 0:1, 256:320].astype(F32)
    one, two = rows_ref[0:LIST, :], rows_ref[LIST : 2 * LIST, :]
    keep = jnp.where(zh == 0, one, two)
    give = jnp.where(zh == 0, two, one)
    both = jnp.concatenate([keep, give, rows_ref[2 * LIST :, :]], axis=0).T
    cols_ref[...] = both
    give_ref[...] = give
    copies[-1].wait()
    half = jnp.where(core == 0, entity_ref[:, 0:HALF], entity_ref[:, HALF:ROWS]).T
    payload = jnp.concatenate([half[0:128, :], half[128:HALF, :], both[:, 0 : 128 * CHUNK1 - 2 * D]], axis=1)
    write_rows(out_ref, payload, CHUNK1)


def route_kernel(x_ref, matching_ref, out_ref):
    zh, _ = place()
    parts = split3(read_rows(x_ref, CHUNK1))
    rows = iota((128, 128), 0)
    marks = [jnp.where(matching_ref[b : b + 1, :] == rows, 1.0, 0.0) for b in range(2)]
    back_keep = jnp.where(zh == 0, marks[0], marks[1])
    back_give = jnp.where(zh == 0, marks[1], marks[0])
    fore = back_keep.T.astype(BF16)
    back_keep, back_give = back_keep.astype(BF16), back_give.astype(BF16)
    partner = sum(dot_nn(fore, p) for p in reversed(parts))
    source = sum(dot_nn(back_keep, p) for p in reversed(parts))
    given = sum(dot_nn(back_give, p[:, 768 : 128 * CHUNK1]) for p in reversed(parts))
    fill = jnp.zeros((128, 128 * CHUNK2 - 4 * D - 2 * LIST), F32)
    routed = jnp.concatenate([partner[:, 0 : 2 * D], source[:, 0 : 2 * D + LIST], given[:, 48:64], fill], axis=1)
    write_rows(out_ref, routed, CHUNK2)


def table_row(rel, zh, core):
    owner = (rel >= REL_DEV).astype(jnp.int32) + (rel >= 2 * REL_DEV).astype(jnp.int32)
    owner = owner + (rel >= 3 * REL_DEV).astype(jnp.int32)
    off = rel - REL_DEV * owner
    owner_zh = (owner >= 2).astype(jnp.int32)
    other_core = (owner - 2 * owner_zh) != core
    return jnp.where(owner_zh == zh, 0, 2 * REL_DEV) + jnp.where(other_core, REL_DEV, 0) + off


def piece_start(spot):
    return min(PIECE * spot, D - PIECE)


def bundle_kernel(relation_ref, give_ref, out_ref):
    spot = lax.axis_index("x")
    start = pl.multiple_of(jnp.minimum(PIECE * spot, D - PIECE), 8)
    piece = relation_ref[pl.ds(start, PIECE), :]
    out_ref[0:PIECE, :] = piece[:, 0:MAIN]
    rest = jnp.concatenate([piece[:, MAIN:REL_DEV], jnp.zeros((PIECE, 128 - REST), F32)], axis=1)
    rest = jnp.concatenate([rest, jnp.zeros((128 - PIECE, 128), F32)], axis=0).T
    for g in range(4):
        out_ref[PIECE : PIECE + 4, 128 * g : 128 * (g + 1)] = rest[4 * g : 4 * g + 4, :]
        out_ref[PIECE + 4 : PIECE + 8, 128 * g : 128 * (g + 1)] = give_ref[4 * g : 4 * g + 4, :]


def unfold(rows):
    return jnp.concatenate([rows[:, 128 * g : 128 * (g + 1)] for g in range(4)], axis=0)


def store_relations(table_ref, first, rows):
    padded = jnp.concatenate([rows, jnp.zeros((rows.shape[0], 512 - D), F32)], axis=1)
    for k in range(4):
        table_ref[pl.ds(4 * first + k, rows.shape[0], stride=4), :] = padded[:, 128 * k : 128 * (k + 1)]


def load_indices(rels, zh, core, index_vmem, index_smem, sem):
    rels = jnp.concatenate([rels, jnp.zeros((16 - rels.shape[0], 128), F32)], axis=0)
    index_vmem[...] = table_row(rels.astype(jnp.int32), zh, core)
    copy = pltpu.make_async_copy(index_vmem, index_smem, sem)
    copy.start()
    return copy


def gather_relations(table_ref, index_smem, first, out_ref):
    def body(step, _):
        for j in range(4):
            for u in range(8):
                lane = step * 8 + u
                at = pl.multiple_of(4 * index_smem[first + j, lane], 4)
                to = pl.multiple_of(512 * j + 4 * lane, 4)
                out_ref[pl.ds(to, 4), :] = table_ref[pl.ds(at, 4), :]
        return 0

    lax.fori_loop(0, 16, body, 0)
    return jnp.concatenate([out_ref[pl.ds(k, SLOTS, stride=4), :] for k in range(4)], axis=1)[:, 0:D]


def gather_heads(lists, hi, lo):
    heads = onehot_cols(lists, 0, 4, iota((128, ROWS), 1).astype(F32))
    return dot_nn(heads, hi) + dot_nn(heads, lo)


def relations_kernel(
    entity_ref, cols_ref, bundle_ref, near_ref, near2_hbm, far_hbm, far2_hbm, fetched_ref,
    rel_out, left_hi, left_lo, first_out, table_ref, entity_hi, entity_lo, cols_out,
    near2_ref, far_ref, far2_ref, far_table, gathered, index_vmem, index_smem, sem, sems,
):
    zh, core = place()
    pairs = ((near2_hbm, near2_ref), (far_hbm, far_ref), (far2_hbm, far2_ref))
    copies = [pltpu.make_async_copy(a, b, sems.at[i]) for i, (a, b) in enumerate(pairs)]
    for copy in copies:
        copy.start()
    theirs = unfold(bundle_ref[PIECE + 4 : PIECE + 8, :])
    chunk = fetched_ref[pl.ds(GIVEN_CHUNK, 128, stride=CHUNK2), :].T
    rels = jnp.concatenate([cols_ref[...].T[4:8, :], theirs[4:8, :], chunk[FIRST + 4 : FIRST + 8, :]], axis=0)
    indices = load_indices(rels, zh, core, index_vmem, index_smem, sem)
    theirs = jnp.concatenate([theirs, jnp.zeros((128 - LIST, 128), F32)], axis=0).T
    cols_out[...] = theirs
    hi, lo = split2(entity_ref[...].T)
    entity_hi[...] = hi
    entity_lo[...] = lo
    head_rows = [gather_heads(lists[:, 0:LIST], hi, lo) for lists in (cols_ref, theirs)]
    store_relations(table_ref, 0, near_ref[...].T)
    copies[0].wait()
    store_relations(table_ref, REL_DEV, near2_ref[...].T)
    for k, ref in enumerate((far_ref, far2_ref)):
        copies[1 + k].wait()
        for spot in range(PIECES):
            far_table[k, piece_start(spot) : piece_start(spot) + PIECE, :] = ref[spot, 0:PIECE, :]
        store_relations(table_ref, (2 + k) * REL_DEV, far_table[k].T)
        rest = [unfold(ref[spot, PIECE : PIECE + 4, :]) for spot in range(PIECES)]
        rest = [rest[spot][:, 0:PIECE] for spot in range(PIECES - 1)] + [rest[-1][:, PIECES * PIECE - D : PIECE]]
        store_relations(table_ref, (2 + k) * REL_DEV + MAIN, jnp.concatenate(rest, axis=1))
    indices.wait()
    for k in range(2):
        rel_rows = gather_relations(table_ref, index_smem, 4 * k, gathered)
        l_hi, l_lo = split2(head_rows[k] * rel_rows)
        span = pl.ds(k * SLOTS, SLOTS)
        rel_out[span, :] = rel_rows
        left_hi[span, :] = l_hi
        left_lo[span, :] = l_lo
    first_out[...] = gather_relations(table_ref, index_smem, 8, gathered)


def fill_block(hi_ref, lo_ref, mine, theirs, first):
    for k, (rows, lane) in enumerate(((mine, 0), (mine, D), (theirs, 0), (theirs, D))):
        hi, lo = split2(rows[:, first + lane : first + lane + D])
        hi_ref[128 * k : 128 * (k + 1), :] = hi
        lo_ref[128 * k : 128 * (k + 1), :] = lo


def lists_rows(lists):
    return jnp.concatenate([lists, jnp.zeros((128, 128 - LIST), F32)], axis=1).T


def given_kernel(fetched_ref, out_ref):
    out_ref[...] = fetched_ref[pl.ds(GIVEN_CHUNK, 128, stride=CHUNK2), :].T[FIRST + LIST : FIRST + 2 * LIST, :]


def softmax_weights(scores, times, tails, axis):
    scores = jnp.where(times > 0.0, scores, -3.0e38)
    weights = times * jnp.exp(scores - jnp.max(scores, axis=axis, keepdims=True))
    return split2(weights / jnp.sum(weights, axis=axis, keepdims=True) - tails)


def weights_kernel(
    mine_ref, theirs_ref, given_ref, cols_mine, cols_theirs, left_hi, left_lo, rel_ref, entity_hi, entity_lo, table_ref,
    head_hi, head_lo, tail_hi, tail_lo, source_hi, source_lo, block_hi, block_lo,
    other_hi, other_lo, gathered, index_vmem, index_smem, sem,
):
    zh, core = place()
    indices = load_indices(given_ref[4:8, :], zh, core, index_vmem, index_smem, sem)
    mine, theirs = read_rows(mine_ref, CHUNK2), read_rows(theirs_ref, CHUNK2)
    fill_block(block_hi, block_lo, mine, theirs, 0)
    fill_block(other_hi, other_lo, mine, theirs, 2 * D)
    numbers = jnp.bitwise_xor(iota((128, ROWS), 1), core * HALF).astype(F32)
    rows_at = iota((ROWS, 128), 0).astype(F32)
    b_hi, b_lo = block_hi[...], block_lo[...]
    e_hi, e_lo = entity_hi[...], entity_lo[...]
    for k in range(2):
        lists = (cols_mine, cols_theirs)[k][:, 0:LIST]
        span = pl.ds(k * SLOTS, SLOTS)
        hi, lo = left_hi[span, :], left_lo[span, :]
        scores = dot_nt(hi, b_lo) + dot_nt(lo, b_hi) + dot_nt(hi, b_hi)
        tails = jnp.concatenate(
            [jnp.where(lists[:, 8 + j : 9 + j] == numbers, 1.0, 0.0) for j in range(4)], axis=0
        )
        drawn = sum(jnp.where(lists[:, 12 + j : 13 + j] == numbers, 1.0, 0.0) for j in range(3))
        times = jnp.sum(drawn, axis=0, keepdims=True) + tails
        w_hi, w_lo = softmax_weights(scores, times, tails, 1)
        head_hi[span, :] = w_hi
        head_lo[span, :] = w_lo
    for k in range(2):
        span = pl.ds(k * SLOTS, SLOTS)
        if k == 0:
            lists = mine[:, 4 * D : 4 * D + LIST]
            rel_rows = rel_ref[...]
        else:
            lists = jnp.concatenate([given_ref[...], jnp.zeros((128 - LIST, 128), F32)], axis=0).T[:, 0:LIST]
            indices.wait()
            rel_rows = gather_relations(table_ref, index_smem, 0, gathered)
        heads = onehot_cols(lists, 0, 4, numbers)
        hi, lo = split2((dot_nn(heads, other_hi[...]) + dot_nn(heads, other_lo[...])) * rel_rows)
        source_hi[span, :] = hi
        source_lo[span, :] = lo
        scores = dot_nt(e_lo, hi) + dot_nt(e_hi, lo) + dot_nt(e_hi, hi)
        rows = lists_rows(lists)
        tails = jnp.concatenate(
            [jnp.where(rows[8 + j : 9 + j, :] == rows_at, 1.0, 0.0) for j in range(4)], axis=1
        )
        drawn = sum(jnp.where(rows[12 + j : 13 + j, :] == rows_at, 1.0, 0.0) for j in range(3))
        times = jnp.sum(drawn, axis=1, keepdims=True) + tails
        w_hi, w_lo = softmax_weights(scores, times, tails, 0)
        tail_hi[span, :] = w_hi
        tail_lo[span, :] = w_lo


def gradient_kernel(
    first, last, cols_mine, cols_theirs, rel_ref, head_hi, head_lo, tail_hi, tail_lo, source_hi, source_lo, block_hi, block_lo,
    keep_ref, send_ref,
):
    _, core = place()
    heads_at = iota((ROWS, 128), 0).astype(F32)
    b_hi, b_lo = block_hi[:, first:last], block_lo[:, first:last]
    total = None
    for k in range(2):
        span = pl.ds(k * SLOTS, SLOTS)
        w_hi, w_lo = head_hi[span, :], head_lo[span, :]
        grad_left = dot_nn(w_hi, b_lo) + dot_nn(w_lo, b_hi) + dot_nn(w_hi, b_hi)
        g_hi, g_lo = split2(grad_left * rel_ref[span, first:last])
        rows = lists_rows((cols_mine, cols_theirs)[k][:, 0:LIST])
        marks = jnp.concatenate(
            [jnp.where(rows[j : j + 1, :] == heads_at, 1.0, 0.0).astype(BF16) for j in range(4)], axis=1
        )
        part = dot_nn(marks, g_lo) + dot_nn(marks, g_hi)
        hi, lo = source_hi[span, first:last], source_lo[span, first:last]
        w_hi, w_lo = tail_hi[span, :], tail_lo[span, :]
        part = part + (dot_nn(w_lo, hi) + dot_nn(w_hi, lo) + dot_nn(w_hi, hi))
        total = part if total is None else total + part
    one, two = total[0:HALF, :].T, total[HALF:ROWS, :].T
    keep_ref[...] = jnp.where(core == 0, one, two)
    send_ref[...] = jnp.where(core == 0, two, one)


def update_kernel(mine0_ref, mine1_ref, theirs0_ref, theirs1_ref, entity_ref, state_ref, updated_ref, accum_ref):
    _, core = place()
    mine = jnp.concatenate([mine0_ref[...], mine1_ref[...]], axis=0)
    theirs = jnp.concatenate([theirs0_ref[...], theirs1_ref[...]], axis=0)
    for j, gradient in enumerate((jnp.where(core == 0, mine, theirs), jnp.where(core == 0, theirs, mine))):
        span = slice(HALF * j, HALF * (j + 1))
        accum = state_ref[:, span] + jnp.sum(gradient * gradient, axis=0, keepdims=True) / float(D)
        accum_ref[:, span] = accum
        updated_ref[:, span] = entity_ref[:, span] - LEARN_RATE * gradient / jnp.sqrt(accum)


def call(kernel, out_shape, args, vmem, scratch=(), cost=None, space=pltpu.VMEM, in_hbm=()):
    out_shape = jax.tree.map(lambda s: jax.ShapeDtypeStruct(*s), out_shape, is_leaf=lambda s: isinstance(s, tuple))
    return pl.pallas_call(
        kernel,
        out_shape=out_shape,
        in_specs=[pl.BlockSpec(memory_space=pltpu.HBM if i in in_hbm else space) for i in range(len(args))],
        out_specs=jax.tree.map(lambda _: pl.BlockSpec(memory_space=pltpu.VMEM), out_shape),
        scratch_shapes=list(scratch),
        compiler_params=pltpu.CompilerParams(vmem_limit_bytes=vmem * MIB),
        cost_estimate=cost,
        name=getattr(kernel, "func", kernel).__name__,
    )(*args)


def flops(us):
    return pl.CostEstimate(flops=int(us * 1.0e9), bytes_accessed=4_000_000, transcendentals=0)


def shards(entity, state, relation, edge_head, edge_rel, edge_tail, negatives, counts, matching):
    swap_core = functools.partial(lax.ppermute, axis_name="core", perm=[(0, 1), (1, 0)])
    swap_zh = functools.partial(lax.ppermute, axis_name="zh", perm=[(0, 1), (1, 0)])
    exchange = functools.partial(lax.all_to_all, axis_name=("x", "yz"), split_axis=0, concat_axis=0, tiled=True)
    entity_t, relation_t = entity.T, relation.T

    payload, cols, give = call(
        pack_kernel,
        [((128 * CHUNK1, 128), F32), ((128, 128), F32), ((LIST, 128), F32)],
        (entity_t, edge_head, edge_rel, edge_tail, negatives, counts.transpose(1, 2, 0)),
        vmem=60,
        scratch=[pltpu.VMEM((128, 128), F32), pltpu.VMEM((D, ROWS), F32)]
        + [pltpu.VMEM((2, 1, 1, n), jnp.int32) for n in (SLOTS, SLOTS, SLOTS, NEGS)]
        + [pltpu.VMEM((1, 1, 2), jnp.int32), pltpu.SemaphoreType.DMA((6,))],
        space=pltpu.HBM,
    )
    spread = exchange(payload.reshape(128, 1, 128 * CHUNK1)).reshape(128 * CHUNK1, 128)

    bundle = swap_zh(call(bundle_kernel, ((PIECE + 8, MAIN), F32), (relation_t, give), vmem=8))
    near2 = swap_core(relation_t)
    spread, bundle = lax.optimization_barrier((spread, bundle))

    routed = call(route_kernel, ((128 * CHUNK2, 128), F32), (spread, matching), vmem=16)
    fetched = exchange(routed.reshape(128, 1, 128 * CHUNK2)).reshape(128 * CHUNK2, 128)
    bundle, _ = lax.optimization_barrier((bundle, routed))
    far = lax.all_gather(bundle, "x", axis=0)
    far2 = swap_core(far)
    fetched_other = swap_core(fetched)
    given = swap_zh(call(given_kernel, ((LIST, 128), F32), (fetched,), vmem=4))
    gather = [
        pltpu.VMEM((4 * SLOTS, 128), F32),
        pltpu.VMEM((16, 128), jnp.int32),
        pltpu.SMEM((16, 128), jnp.int32),
        pltpu.SemaphoreType.DMA,
    ]
    wide, square = (2 * SLOTS, D), (2 * SLOTS, ROWS)
    rel_rows, left_hi, left_lo, first_rel, table, entity_hi, entity_lo, cols_other = call(
        relations_kernel,
        [
            (wide, F32),
            (wide, BF16),
            (wide, BF16),
            ((SLOTS, D), F32),
            ((4 * TABLE, 128), F32),
            ((ROWS, D), BF16),
            ((ROWS, D), BF16),
            ((128, 128), F32),
        ],
        (entity_t, cols, bundle, relation_t, near2, far, far2, fetched),
        vmem=32,
        scratch=[pltpu.VMEM((D, REL_DEV), F32)]
        + [pltpu.VMEM((PIECES, PIECE + 8, MAIN), F32)] * 2
        + [pltpu.VMEM((2, D, MAIN), F32)]
        + gather
        + [pltpu.SemaphoreType.DMA((3,))],
        cost=flops(8),
        in_hbm=(4, 5, 6),
    )
    weights = call(
        weights_kernel,
        [(square, BF16)] * 4 + [(wide, BF16)] * 2 + [((ROWS, D), BF16)] * 2,
        (fetched, fetched_other, given, cols, cols_other, left_hi, left_lo, first_rel, entity_hi, entity_lo, table),
        vmem=32,
        scratch=[pltpu.VMEM((ROWS, D), BF16)] * 2 + gather,
        cost=flops(8),
    )
    halves, others = [], []
    for first, last in ((0, 256), (256, D)):
        keep, send = call(
            functools.partial(gradient_kernel, first, last),
            [((last - first, HALF), F32)] * 2,
            (cols, cols_other, rel_rows, *weights),
            vmem=28,
            cost=flops(3),
        )
        recv = swap_core(send)
        if first == 0:
            recv, first_weight = lax.optimization_barrier((recv, weights[0]))
            weights = (first_weight, *weights[1:])
        half = keep + recv
        half = half + swap_zh(half)
        halves.append(half)
        others.append(swap_core(half))
    updated, accum = call(
        update_kernel,
        [((D, ROWS), F32), ((1, ROWS), F32)],
        (*halves, *others, entity_t, state.reshape(1, ROWS)),
        vmem=8,
    )
    return updated.T, accum.reshape(ROWS)


def solution(mesh):
    parts = (PIECES, mesh.shape["dom"] // PIECES, 2, 2)
    fine = jax.sharding.Mesh(mesh.devices.reshape(parts), ("x", "yz", "zh", "core"))
    dom, edge = ("x", "yz"), ("zh", "core")
    return jax.shard_map(
        shards,
        mesh=fine,
        in_specs=(
            P(dom, None),
            P(dom),
            P(edge, None),
            P(None, dom, edge, None),
            P(None, dom, edge, None),
            P(None, dom, edge, None),
            P(None, dom, edge, None),
            P(None, dom, edge),
            P(),
        ),
        out_specs=(P(dom, None), P(dom)),
        check_vma=False,
    )
```

```python
import functools

import jax
import jax.numpy as jnp
from jax import lax
from jax.experimental import pallas as pl
from jax.experimental.pallas import tpu as pltpu
from jax.sharding import PartitionSpec as P


LEARN_RATE = 0.1
D = 400
ROWS = 512
HALF = 256
SLOTS = 512
NEGS = 320
REL_DEV = 528
PIECES = 4
PIECE = 104
MAIN = 512
REST = REL_DEV - MAIN
TABLE = 4 * REL_DEV
LIST = 16
CHUNK1 = 7
CHUNK2 = 13
GIVEN_CHUNK = 12
FIRST = 4 * D - 128 * GIVEN_CHUNK
F32 = jnp.float32
BF16 = jnp.bfloat16
MIB = 1024 * 1024


def split2(x):
    hi = x.astype(BF16)
    return hi, (x - hi.astype(F32)).astype(BF16)


def split3(x):
    hi = x.astype(BF16)
    rest = x - hi.astype(F32)
    mid = rest.astype(BF16)
    return hi, mid, (rest - mid.astype(F32)).astype(BF16)


def dot_nn(a, b):
    return lax.dot_general(a, b, (((1,), (0,)), ((), ())), preferred_element_type=F32)


def dot_nt(a, b):
    return lax.dot_general(a, b, (((1,), (1,)), ((), ())), preferred_element_type=F32)


def iota(shape, dim):
    return lax.broadcasted_iota(jnp.int32, shape, dim)


def place():
    return lax.axis_index("zh"), lax.axis_index("core")


def read_rows(ref, chunks):
    return jnp.concatenate([ref[pl.ds(k, 128, stride=chunks), :] for k in range(chunks)], axis=1)


def write_rows(ref, value, chunks):
    for k in range(chunks):
        ref[pl.ds(k, 128, stride=chunks), :] = value[:, 128 * k : 128 * (k + 1)]


def onehot_cols(lists, first, count, columns):
    blocks = [(lists[:, first + j : first + j + 1] == columns) for j in range(count)]
    return jnp.concatenate([jnp.where(b, 1.0, 0.0).astype(BF16) for b in blocks], axis=0)


def pack_kernel(
    entity_hbm, head_hbm, rel_hbm, tail_hbm, neg_hbm, count_hbm, out_ref, cols_ref, give_ref,
    rows_ref, entity_ref, head_ref, rel_ref, tail_ref, neg_ref, count_ref, sems,
):
    zh, core = place()
    pairs = (
        (head_hbm, head_ref), (rel_hbm, rel_ref), (tail_hbm, tail_ref), (neg_hbm, neg_ref), (count_hbm, count_ref),
        (entity_hbm, entity_ref),
    )
    copies = [pltpu.make_async_copy(a, b, sems.at[i]) for i, (a, b) in enumerate(pairs)]
    for copy in copies:
        copy.start()
    rows_ref[...] = jnp.full((128, 128), -1.0, F32)
    lane = iota((1, 128), 1)
    for copy in copies[:-1]:
        copy.wait()
    for bucket in range(2):
        at = bucket * LIST
        live = count_ref[0, :, bucket : bucket + 1]
        for j in range(4):
            span = pl.ds(128 * j, 128)
            head = jnp.where(lane + 128 * j < live, head_ref[bucket, 0, 0:1, span], -1)
            rows_ref[at + j : at + j + 1, :] = head.astype(F32)
            rows_ref[at + 4 + j : at + 5 + j, :] = rel_ref[bucket, 0, 0:1, span].astype(F32)
            rows_ref[at + 8 + j : at + 9 + j, :] = tail_ref[bucket, 0, 0:1, span].astype(F32)
        rows_ref[at + 12 : at + 13, :] = neg_ref[bucket, 0, 0:1, 0:128].astype(F32)
        rows_ref[at + 13 : at + 14, :] = neg_ref[bucket, 0, 0:1, 128:256].astype(F32)
        rows_ref[at + 14 : at + 15, 0:64] = neg_ref[bucket, 0, 0:1, 256:320].astype(F32)
    one, two = rows_ref[0:LIST, :], rows_ref[LIST : 2 * LIST, :]
    keep = jnp.where(zh == 0, one, two)
    give = jnp.where(zh == 0, two, one)
    both = jnp.concatenate([keep, give, rows_ref[2 * LIST :, :]], axis=0).T
    cols_ref[...] = both
    give_ref[...] = give
    copies[-1].wait()
    half = jnp.where(core == 0, entity_ref[:, 0:HALF], entity_ref[:, HALF:ROWS]).T
    payload = jnp.concatenate([half[0:128, :], half[128:HALF, :], both[:, 0 : 128 * CHUNK1 - 2 * D]], axis=1)
    write_rows(out_ref, payload, CHUNK1)


def route_kernel(x_ref, matching_hbm, out_ref, matching_ref, sem):
    zh, _ = place()
    copy = pltpu.make_async_copy(matching_hbm, matching_ref, sem)
    copy.start()
    parts = split3(read_rows(x_ref, CHUNK1))
    rows = iota((128, 128), 0)
    copy.wait()
    marks = [jnp.where(matching_ref[b : b + 1, :] == rows, 1.0, 0.0) for b in range(2)]
    back_keep = jnp.where(zh == 0, marks[0], marks[1])
    back_give = jnp.where(zh == 0, marks[1], marks[0])
    fore = back_keep.T.astype(BF16)
    back_keep, back_give = back_keep.astype(BF16), back_give.astype(BF16)
    partner = sum(dot_nn(fore, p) for p in reversed(parts))
    source = sum(dot_nn(back_keep, p) for p in reversed(parts))
    given = sum(dot_nn(back_give, p[:, 768 : 128 * CHUNK1]) for p in reversed(parts))
    fill = jnp.zeros((128, 128 * CHUNK2 - 4 * D - 2 * LIST), F32)
    routed = jnp.concatenate([partner[:, 0 : 2 * D], source[:, 0 : 2 * D + LIST], given[:, 48:64], fill], axis=1)
    write_rows(out_ref, routed, CHUNK2)


def table_row(rel, zh, core):
    owner = (rel >= REL_DEV).astype(jnp.int32) + (rel >= 2 * REL_DEV).astype(jnp.int32)
    owner = owner + (rel >= 3 * REL_DEV).astype(jnp.int32)
    off = rel - REL_DEV * owner
    owner_zh = (owner >= 2).astype(jnp.int32)
    other_core = (owner - 2 * owner_zh) != core
    return jnp.where(owner_zh == zh, 0, 2 * REL_DEV) + jnp.where(other_core, REL_DEV, 0) + off


def piece_start(spot):
    return min(PIECE * spot, D - PIECE)


def bundle_kernel(relation_ref, give_ref, out_ref):
    spot = lax.axis_index("x")
    start = pl.multiple_of(jnp.minimum(PIECE * spot, D - PIECE), 8)
    piece = relation_ref[pl.ds(start, PIECE), :]
    out_ref[0:PIECE, :] = piece[:, 0:MAIN]
    rest = jnp.concatenate([piece[:, MAIN:REL_DEV], jnp.zeros((PIECE, 128 - REST), F32)], axis=1)
    rest = jnp.concatenate([rest, jnp.zeros((128 - PIECE, 128), F32)], axis=0).T
    for g in range(4):
        out_ref[PIECE : PIECE + 4, 128 * g : 128 * (g + 1)] = rest[4 * g : 4 * g + 4, :]
        out_ref[PIECE + 4 : PIECE + 8, 128 * g : 128 * (g + 1)] = give_ref[4 * g : 4 * g + 4, :]


def unfold(rows):
    return jnp.concatenate([rows[:, 128 * g : 128 * (g + 1)] for g in range(4)], axis=0)


def store_relations(table_ref, first, rows):
    padded = jnp.concatenate([rows, jnp.zeros((rows.shape[0], 512 - D), F32)], axis=1)
    for k in range(4):
        table_ref[pl.ds(4 * first + k, rows.shape[0], stride=4), :] = padded[:, 128 * k : 128 * (k + 1)]


def load_indices(rels, zh, core, index_vmem, index_smem, sem):
    rels = jnp.concatenate([rels, jnp.zeros((16 - rels.shape[0], 128), F32)], axis=0)
    index_vmem[...] = table_row(rels.astype(jnp.int32), zh, core)
    copy = pltpu.make_async_copy(index_vmem, index_smem, sem)
    copy.start()
    return copy


def gather_relations(table_ref, index_smem, first, out_ref):
    def body(step, _):
        for j in range(4):
            for u in range(8):
                lane = step * 8 + u
                at = pl.multiple_of(4 * index_smem[first + j, lane], 4)
                to = pl.multiple_of(512 * j + 4 * lane, 4)
                out_ref[pl.ds(to, 4), :] = table_ref[pl.ds(at, 4), :]
        return 0

    lax.fori_loop(0, 16, body, 0)
    return jnp.concatenate([out_ref[pl.ds(k, SLOTS, stride=4), :] for k in range(4)], axis=1)[:, 0:D]


def gather_heads(lists, hi, lo):
    heads = onehot_cols(lists, 0, 4, iota((128, ROWS), 1).astype(F32))
    return dot_nn(heads, hi) + dot_nn(heads, lo)


def relations_kernel(
    entity_ref, cols_ref, bundle_ref, near_ref, near2_hbm, far_hbm, far2_hbm, fetched_ref,
    rel_out, left_hi, left_lo, first_out, table_ref, entity_hi, entity_lo, cols_out,
    near2_ref, far_ref, far2_ref, far_table, gathered, index_vmem, index_smem, sem, sems,
):
    zh, core = place()
    pairs = ((near2_hbm, near2_ref), (far_hbm, far_ref), (far2_hbm, far2_ref))
    copies = [pltpu.make_async_copy(a, b, sems.at[i]) for i, (a, b) in enumerate(pairs)]
    for copy in copies:
        copy.start()
    theirs = unfold(bundle_ref[PIECE + 4 : PIECE + 8, :])
    chunk = fetched_ref[pl.ds(GIVEN_CHUNK, 128, stride=CHUNK2), :].T
    rels = jnp.concatenate([cols_ref[...].T[4:8, :], theirs[4:8, :], chunk[FIRST + 4 : FIRST + 8, :]], axis=0)
    indices = load_indices(rels, zh, core, index_vmem, index_smem, sem)
    theirs = jnp.concatenate([theirs, jnp.zeros((128 - LIST, 128), F32)], axis=0).T
    cols_out[...] = theirs
    hi, lo = split2(entity_ref[...].T)
    entity_hi[...] = hi
    entity_lo[...] = lo
    head_rows = [gather_heads(lists[:, 0:LIST], hi, lo) for lists in (cols_ref, theirs)]
    store_relations(table_ref, 0, near_ref[...].T)
    copies[0].wait()
    store_relations(table_ref, REL_DEV, near2_ref[...].T)
    for k, ref in enumerate((far_ref, far2_ref)):
        copies[1 + k].wait()
        for spot in range(PIECES):
            far_table[k, piece_start(spot) : piece_start(spot) + PIECE, :] = ref[spot, 0:PIECE, :]
        store_relations(table_ref, (2 + k) * REL_DEV, far_table[k].T)
        rest = [unfold(ref[spot, PIECE : PIECE + 4, :]) for spot in range(PIECES)]
        rest = [rest[spot][:, 0:PIECE] for spot in range(PIECES - 1)] + [rest[-1][:, PIECES * PIECE - D : PIECE]]
        store_relations(table_ref, (2 + k) * REL_DEV + MAIN, jnp.concatenate(rest, axis=1))
    indices.wait()
    for k in range(2):
        rel_rows = gather_relations(table_ref, index_smem, 4 * k, gathered)
        l_hi, l_lo = split2(head_rows[k] * rel_rows)
        span = pl.ds(k * SLOTS, SLOTS)
        rel_out[span, :] = rel_rows
        left_hi[span, :] = l_hi
        left_lo[span, :] = l_lo
    first_out[...] = gather_relations(table_ref, index_smem, 8, gathered)


def fill_block(hi_ref, lo_ref, mine, theirs, first):
    for k, (rows, lane) in enumerate(((mine, 0), (mine, D), (theirs, 0), (theirs, D))):
        hi, lo = split2(rows[:, first + lane : first + lane + D])
        hi_ref[128 * k : 128 * (k + 1), :] = hi
        lo_ref[128 * k : 128 * (k + 1), :] = lo


def lists_rows(lists):
    return jnp.concatenate([lists, jnp.zeros((128, 128 - LIST), F32)], axis=1).T


def head_kernel(mine_ref, theirs_ref, lists_mine, lists_theirs, rel_ref, left_hi, left_lo, grad_ref, block_hi, block_lo):
    _, core = place()
    fill_block(block_hi, block_lo, read_rows(mine_ref, CHUNK2), read_rows(theirs_ref, CHUNK2), 0)
    numbers = jnp.bitwise_xor(iota((128, ROWS), 1), core * HALF).astype(F32)
    heads_at = iota((ROWS, 128), 0).astype(F32)
    total = None
    for k in range(2):
        lists = (lists_mine, lists_theirs)[k][:, 0:LIST]
        span = pl.ds(k * SLOTS, SLOTS)
        hi, lo = left_hi[span, :], left_lo[span, :]
        b_hi, b_lo = block_hi[...], block_lo[...]
        scores = dot_nt(hi, b_lo) + dot_nt(lo, b_hi) + dot_nt(hi, b_hi)
        tails = jnp.concatenate(
            [jnp.where(lists[:, 8 + j : 9 + j] == numbers, 1.0, 0.0) for j in range(4)], axis=0
        )
        drawn = sum(jnp.where(lists[:, 12 + j : 13 + j] == numbers, 1.0, 0.0) for j in range(3))
        times = jnp.sum(drawn, axis=0, keepdims=True) + tails
        scores = jnp.where(times > 0.0, scores, -3.0e38)
        weights = times * jnp.exp(scores - jnp.max(scores, axis=1, keepdims=True))
        weights = weights / jnp.sum(weights, axis=1, keepdims=True) - tails
        w_hi, w_lo = split2(weights)
        grad_left = dot_nn(w_hi, b_lo) + dot_nn(w_lo, b_hi) + dot_nn(w_hi, b_hi)
        g_hi, g_lo = split2(grad_left * rel_ref[span, :])
        rows = lists_rows(lists)
        marks = jnp.concatenate(
            [jnp.where(rows[j : j + 1, :] == heads_at, 1.0, 0.0) for j in range(4)], axis=1
        ).astype(BF16)
        part = dot_nn(marks, g_lo) + dot_nn(marks, g_hi)
        total = part if total is None else total + part
    grad_ref[...] = total


def given_kernel(fetched_ref, out_ref):
    out_ref[...] = fetched_ref[pl.ds(GIVEN_CHUNK, 128, stride=CHUNK2), :].T[FIRST + LIST : FIRST + 2 * LIST, :]


def tail_kernel(
    mine_ref, theirs_ref, given_ref, rel_ref, entity_hi, entity_lo, table_ref, head_grad,
    keep_ref, send_ref, block_hi, block_lo, gathered, index_vmem, index_smem, sem,
):
    zh, core = place()
    mine = read_rows(mine_ref, CHUNK2)
    fill_block(block_hi, block_lo, mine, read_rows(theirs_ref, CHUNK2), 2 * D)
    indices = load_indices(given_ref[4:8, :], zh, core, index_vmem, index_smem, sem)
    e_hi, e_lo = entity_hi[...], entity_lo[...]
    numbers = jnp.bitwise_xor(iota((128, ROWS), 1), core * HALF).astype(F32)
    rows_at = iota((ROWS, 128), 0).astype(F32)
    total = head_grad[...]
    for k in range(2):
        if k == 0:
            lists = mine[:, 4 * D : 4 * D + LIST]
            rel_rows = rel_ref[...]
        else:
            lists = jnp.concatenate([given_ref[...], jnp.zeros((128 - LIST, 128), F32)], axis=0).T[:, 0:LIST]
            indices.wait()
            rel_rows = gather_relations(table_ref, index_smem, 0, gathered)
        heads = onehot_cols(lists, 0, 4, numbers)
        head_rows = dot_nn(heads, block_hi[...]) + dot_nn(heads, block_lo[...])
        l_hi, l_lo = split2(head_rows * rel_rows)
        scores = dot_nt(e_lo, l_hi) + dot_nt(e_hi, l_lo) + dot_nt(e_hi, l_hi)
        rows = lists_rows(lists)
        tails = jnp.concatenate(
            [jnp.where(rows[8 + j : 9 + j, :] == rows_at, 1.0, 0.0) for j in range(4)], axis=1
        )
        drawn = sum(jnp.where(rows[12 + j : 13 + j, :] == rows_at, 1.0, 0.0) for j in range(3))
        times = jnp.sum(drawn, axis=1, keepdims=True) + tails
        scores = jnp.where(times > 0.0, scores, -3.0e38)
        weights = times * jnp.exp(scores - jnp.max(scores, axis=0, keepdims=True))
        weights = weights / jnp.sum(weights, axis=0, keepdims=True) - tails
        w_hi, w_lo = split2(weights)
        total = total + (dot_nn(w_lo, l_hi) + dot_nn(w_hi, l_lo) + dot_nn(w_hi, l_hi))
    first, second = total[0:HALF, :].T, total[HALF:ROWS, :].T
    keep_ref[...] = jnp.where(core == 0, first, second)
    send_ref[...] = jnp.where(core == 0, second, first)


def combine_kernel(keep_ref, sent_ref, out_ref):
    _, core = place()
    out_ref[...] = keep_ref[...] + sent_ref[1 - core]


def update_kernel(gradient_ref, entity_ref, state_ref, updated_ref, accum_ref):
    for j in range(2):
        gradient = gradient_ref[j]
        span = slice(HALF * j, HALF * (j + 1))
        accum = state_ref[:, span] + jnp.sum(gradient * gradient, axis=0, keepdims=True) / float(D)
        accum_ref[:, span] = accum
        updated_ref[:, span] = entity_ref[:, span] - LEARN_RATE * gradient / jnp.sqrt(accum)


def call(kernel, out_shape, args, vmem, scratch=(), cost=None, space=pltpu.VMEM, in_hbm=()):
    out_shape = jax.tree.map(lambda s: jax.ShapeDtypeStruct(*s), out_shape, is_leaf=lambda s: isinstance(s, tuple))
    return pl.pallas_call(
        kernel,
        out_shape=out_shape,
        in_specs=[pl.BlockSpec(memory_space=pltpu.HBM if i in in_hbm else space) for i in range(len(args))],
        out_specs=jax.tree.map(lambda _: pl.BlockSpec(memory_space=pltpu.VMEM), out_shape),
        scratch_shapes=list(scratch),
        compiler_params=pltpu.CompilerParams(vmem_limit_bytes=vmem * MIB),
        cost_estimate=cost,
        name=getattr(kernel, "func", kernel).__name__,
    )(*args)


def flops(us):
    return pl.CostEstimate(flops=int(us * 1.0e9), bytes_accessed=4_000_000, transcendentals=0)


def shards(entity, state, relation, edge_head, edge_rel, edge_tail, negatives, counts, matching):
    swap_core = functools.partial(lax.ppermute, axis_name="core", perm=[(0, 1), (1, 0)])
    swap_zh = functools.partial(lax.ppermute, axis_name="zh", perm=[(0, 1), (1, 0)])
    exchange = functools.partial(lax.all_to_all, axis_name=("x", "yz"), split_axis=0, concat_axis=0, tiled=True)
    entity_t, relation_t = entity.T, relation.T

    payload, cols, give = call(
        pack_kernel,
        [((128 * CHUNK1, 128), F32), ((128, 128), F32), ((LIST, 128), F32)],
        (entity_t, edge_head, edge_rel, edge_tail, negatives, counts.transpose(1, 2, 0)),
        vmem=60,
        scratch=[pltpu.VMEM((128, 128), F32), pltpu.VMEM((D, ROWS), F32)]
        + [pltpu.VMEM((2, 1, 1, n), jnp.int32) for n in (SLOTS, SLOTS, SLOTS, NEGS)]
        + [pltpu.VMEM((1, 1, 2), jnp.int32), pltpu.SemaphoreType.DMA((6,))],
        space=pltpu.HBM,
    )
    spread = exchange(payload.reshape(128, 1, 128 * CHUNK1)).reshape(128 * CHUNK1, 128)

    bundle = swap_zh(call(bundle_kernel, ((PIECE + 8, MAIN), F32), (relation_t, give), vmem=8))
    near2 = swap_core(relation_t)
    spread, bundle = lax.optimization_barrier((spread, bundle))

    routed = call(
        route_kernel,
        ((128 * CHUNK2, 128), F32),
        (spread, matching),
        vmem=16,
        scratch=[pltpu.VMEM((2, 128), jnp.int32), pltpu.SemaphoreType.DMA],
        in_hbm=(1,),
    )
    fetched = exchange(routed.reshape(128, 1, 128 * CHUNK2)).reshape(128 * CHUNK2, 128)
    bundle, _ = lax.optimization_barrier((bundle, routed))
    far = lax.all_gather(bundle, "x", axis=0)
    far2 = swap_core(far)
    fetched_other = swap_core(fetched)
    given = swap_zh(call(given_kernel, ((LIST, 128), F32), (fetched,), vmem=4))
    gather = [
        pltpu.VMEM((4 * SLOTS, 128), F32),
        pltpu.VMEM((16, 128), jnp.int32),
        pltpu.SMEM((16, 128), jnp.int32),
        pltpu.SemaphoreType.DMA,
    ]
    rel_rows, left_hi, left_lo, first_rel, table, entity_hi, entity_lo, cols_other = call(
        relations_kernel,
        [
            ((2 * SLOTS, D), F32),
            ((2 * SLOTS, D), BF16),
            ((2 * SLOTS, D), BF16),
            ((SLOTS, D), F32),
            ((4 * TABLE, 128), F32),
            ((ROWS, D), BF16),
            ((ROWS, D), BF16),
            ((128, 128), F32),
        ],
        (entity_t, cols, bundle, relation_t, near2, far, far2, fetched),
        vmem=32,
        scratch=[pltpu.VMEM((D, REL_DEV), F32)]
        + [pltpu.VMEM((PIECES, PIECE + 8, MAIN), F32)] * 2
        + [pltpu.VMEM((2, D, MAIN), F32)]
        + gather
        + [pltpu.SemaphoreType.DMA((3,))],
        cost=flops(8),
        in_hbm=(4, 5, 6),
    )
    block = [pltpu.VMEM((ROWS, D), BF16), pltpu.VMEM((ROWS, D), BF16)]
    head_grad = call(
        head_kernel,
        ((ROWS, D), F32),
        (fetched, fetched_other, cols, cols_other, rel_rows, left_hi, left_lo),
        vmem=20,
        scratch=block,
        cost=flops(6),
    )
    keep, send = call(
        tail_kernel,
        [((D, HALF), F32)] * 2,
        (fetched, fetched_other, given, first_rel, entity_hi, entity_lo, table, head_grad),
        vmem=28,
        scratch=block + gather,
        cost=flops(9),
    )
    sent = lax.all_gather(send, "core", axis=0)
    half = call(combine_kernel, ((D, HALF), F32), (keep, sent), vmem=8)
    chips = lax.all_gather(half, "zh", axis=0)
    gradient = lax.all_gather(chips[0] + chips[1], "core", axis=0)
    updated, accum = call(
        update_kernel,
        [((D, ROWS), F32), ((1, ROWS), F32)],
        (gradient, entity_t, state.reshape(1, ROWS)),
        vmem=8,
    )
    return updated.T, accum.reshape(ROWS)


def solution(mesh):
    parts = (PIECES, mesh.shape["dom"] // PIECES, 2, 2)
    fine = jax.sharding.Mesh(mesh.devices.reshape(parts), ("x", "yz", "zh", "core"))
    dom, edge = ("x", "yz"), ("zh", "core")
    return jax.shard_map(
        shards,
        mesh=fine,
        in_specs=(
            P(dom, None),
            P(dom),
            P(edge, None),
            P(None, dom, edge, None),
            P(None, dom, edge, None),
            P(None, dom, edge, None),
            P(None, dom, edge, None),
            P(None, dom, edge),
            P(),
        ),
        out_specs=(P(dom, None), P(dom)),
        check_vma=False,
    )
```

```python
import functools

import jax
import jax.numpy as jnp
from jax import lax
from jax.experimental import pallas as pl
from jax.experimental.pallas import tpu as pltpu
from jax.sharding import PartitionSpec as P


LEARN_RATE = 0.1
D = 400
ROWS = 512
HALF = 256
SLOTS = 512
NEGS = 320
REL_DEV = 528
PIECES = 4
PIECE = 104
MAIN = 512
REST = REL_DEV - MAIN
TABLE = 4 * REL_DEV
LIST = 16
CHUNK1 = 7
CHUNK2 = 13
GIVEN_CHUNK = 12
FIRST = 4 * D - 128 * GIVEN_CHUNK
F32 = jnp.float32
BF16 = jnp.bfloat16
MIB = 1024 * 1024


def split2(x):
    hi = x.astype(BF16)
    return hi, (x - hi.astype(F32)).astype(BF16)


def split3(x):
    hi = x.astype(BF16)
    rest = x - hi.astype(F32)
    mid = rest.astype(BF16)
    return hi, mid, (rest - mid.astype(F32)).astype(BF16)


def dot_nn(a, b):
    return lax.dot_general(a, b, (((1,), (0,)), ((), ())), preferred_element_type=F32)


def dot_nt(a, b):
    return lax.dot_general(a, b, (((1,), (1,)), ((), ())), preferred_element_type=F32)


def dot3_nt(a_hi, a_lo, b_hi, b_lo):
    return dot_nt(jnp.concatenate([a_hi, a_lo, a_hi], axis=1), jnp.concatenate([b_lo, b_hi, b_hi], axis=1))


def iota(shape, dim):
    return lax.broadcasted_iota(jnp.int32, shape, dim)


def place():
    return lax.axis_index("zh"), lax.axis_index("core")


def read_rows(ref, chunks):
    return jnp.concatenate([ref[pl.ds(k, 128, stride=chunks), :] for k in range(chunks)], axis=1)


def write_rows(ref, value, chunks):
    for k in range(chunks):
        ref[pl.ds(k, 128, stride=chunks), :] = value[:, 128 * k : 128 * (k + 1)]


def onehot_cols(lists, first, count, columns):
    blocks = [(lists[:, first + j : first + j + 1] == columns) for j in range(count)]
    return jnp.concatenate([jnp.where(b, 1.0, 0.0).astype(BF16) for b in blocks], axis=0)


def pack_kernel(
    entity_hbm, head_hbm, rel_hbm, tail_hbm, neg_hbm, count_hbm, out_ref, cols_ref, give_ref,
    rows_ref, entity_ref, head_ref, rel_ref, tail_ref, neg_ref, count_ref, sems,
):
    zh, core = place()
    pairs = (
        (head_hbm, head_ref), (rel_hbm, rel_ref), (tail_hbm, tail_ref), (neg_hbm, neg_ref), (count_hbm, count_ref),
        (entity_hbm, entity_ref),
    )
    copies = [pltpu.make_async_copy(a, b, sems.at[i]) for i, (a, b) in enumerate(pairs)]
    for copy in copies:
        copy.start()
    rows_ref[...] = jnp.full((128, 128), -1.0, F32)
    lane = iota((1, 128), 1)
    for copy in copies[:-1]:
        copy.wait()
    for bucket in range(2):
        at = bucket * LIST
        live = count_ref[0, :, bucket : bucket + 1]
        for j in range(4):
            span = pl.ds(128 * j, 128)
            head = jnp.where(lane + 128 * j < live, head_ref[bucket, 0, 0:1, span], -1)
            rows_ref[at + j : at + j + 1, :] = head.astype(F32)
            rows_ref[at + 4 + j : at + 5 + j, :] = rel_ref[bucket, 0, 0:1, span].astype(F32)
            rows_ref[at + 8 + j : at + 9 + j, :] = tail_ref[bucket, 0, 0:1, span].astype(F32)
        rows_ref[at + 12 : at + 13, :] = neg_ref[bucket, 0, 0:1, 0:128].astype(F32)
        rows_ref[at + 13 : at + 14, :] = neg_ref[bucket, 0, 0:1, 128:256].astype(F32)
        rows_ref[at + 14 : at + 15, 0:64] = neg_ref[bucket, 0, 0:1, 256:320].astype(F32)
    one, two = rows_ref[0:LIST, :], rows_ref[LIST : 2 * LIST, :]
    keep = jnp.where(zh == 0, one, two)
    give = jnp.where(zh == 0, two, one)
    both = jnp.concatenate([keep, give, rows_ref[2 * LIST :, :]], axis=0).T
    cols_ref[...] = both
    give_ref[...] = give
    copies[-1].wait()
    half = jnp.where(core == 0, entity_ref[:, 0:HALF], entity_ref[:, HALF:ROWS]).T
    payload = jnp.concatenate([half[0:128, :], half[128:HALF, :], both[:, 0 : 128 * CHUNK1 - 2 * D]], axis=1)
    write_rows(out_ref, payload, CHUNK1)


def route_kernel(x_ref, matching_ref, out_ref):
    zh, _ = place()
    parts = split3(read_rows(x_ref, CHUNK1))
    rows = iota((128, 128), 0)
    marks = [jnp.where(matching_ref[b : b + 1, :] == rows, 1.0, 0.0) for b in range(2)]
    back_keep = jnp.where(zh == 0, marks[0], marks[1])
    back_give = jnp.where(zh == 0, marks[1], marks[0])
    fore = back_keep.T.astype(BF16)
    back_keep, back_give = back_keep.astype(BF16), back_give.astype(BF16)
    partner = sum(dot_nn(fore, p) for p in reversed(parts))
    source = sum(dot_nn(back_keep, p) for p in reversed(parts))
    given = sum(dot_nn(back_give, p[:, 768 : 128 * CHUNK1]) for p in reversed(parts))
    fill = jnp.zeros((128, 128 * CHUNK2 - 4 * D - 2 * LIST), F32)
    routed = jnp.concatenate([partner[:, 0 : 2 * D], source[:, 0 : 2 * D + LIST], given[:, 48:64], fill], axis=1)
    write_rows(out_ref, routed, CHUNK2)


def table_row(rel, zh, core):
    owner = (rel >= REL_DEV).astype(jnp.int32) + (rel >= 2 * REL_DEV).astype(jnp.int32)
    owner = owner + (rel >= 3 * REL_DEV).astype(jnp.int32)
    off = rel - REL_DEV * owner
    owner_zh = (owner >= 2).astype(jnp.int32)
    other_core = (owner - 2 * owner_zh) != core
    return jnp.where(owner_zh == zh, 0, 2 * REL_DEV) + jnp.where(other_core, REL_DEV, 0) + off


def piece_start(spot):
    return min(PIECE * spot, D - PIECE)


def bundle_kernel(relation_ref, matching_ref, out_ref, matching_out):
    spot = lax.axis_index("x")
    start = pl.multiple_of(jnp.minimum(PIECE * spot, D - PIECE), 8)
    piece = relation_ref[pl.ds(start, PIECE), :]
    out_ref[0:PIECE, :] = piece[:, 0:MAIN]
    rest = jnp.concatenate([piece[:, MAIN:REL_DEV], jnp.zeros((PIECE, 128 - REST), F32)], axis=1)
    rest = jnp.concatenate([rest, jnp.zeros((128 - PIECE, 128), F32)], axis=0).T
    for g in range(4):
        out_ref[PIECE : PIECE + 4, 128 * g : 128 * (g + 1)] = rest[4 * g : 4 * g + 4, :]
    out_ref[PIECE + 4 : PIECE + 8, :] = jnp.zeros((4, MAIN), F32)
    matching_out[...] = matching_ref[...]


def unfold(rows):
    return jnp.concatenate([rows[:, 128 * g : 128 * (g + 1)] for g in range(4)], axis=0)


def store_relations(table_ref, first, rows):
    padded = jnp.concatenate([rows, jnp.zeros((rows.shape[0], 512 - D), F32)], axis=1)
    for k in range(4):
        table_ref[pl.ds(4 * first + k, rows.shape[0], stride=4), :] = padded[:, 128 * k : 128 * (k + 1)]


def load_indices(rels, zh, core, index_vmem, index_smem, sem):
    rels = jnp.concatenate([rels, jnp.zeros((16 - rels.shape[0], 128), F32)], axis=0)
    index_vmem[...] = table_row(rels.astype(jnp.int32), zh, core)
    copy = pltpu.make_async_copy(index_vmem, index_smem, sem)
    copy.start()
    return copy


def gather_relations(table_ref, index_smem, first, out_ref):
    def body(step, _):
        for j in range(4):
            for u in range(8):
                lane = step * 8 + u
                at = pl.multiple_of(4 * index_smem[first + j, lane], 4)
                to = pl.multiple_of(512 * j + 4 * lane, 4)
                out_ref[pl.ds(to, 4), :] = table_ref[pl.ds(at, 4), :]
        return 0

    lax.fori_loop(0, 16, body, 0)
    return jnp.concatenate([out_ref[pl.ds(k, SLOTS, stride=4), :] for k in range(4)], axis=1)[:, 0:D]


def gather_heads(lists, hi, lo):
    heads = onehot_cols(lists, 0, 4, iota((128, ROWS), 1).astype(F32))
    return dot_nn(heads, hi) + dot_nn(heads, lo)


def relations_kernel(
    entity_ref, cols_ref, theirs_ref, near_ref, near2_hbm, far_hbm, far2_hbm, fetched_ref,
    rel_out, left_hi, left_lo, first_out, table_ref, entity_hi, entity_lo, cols_out,
    near2_ref, far_ref, far2_ref, far_table, gathered, index_vmem, index_smem, sem, sems,
):
    zh, core = place()
    pairs = ((near2_hbm, near2_ref), (far_hbm, far_ref), (far2_hbm, far2_ref))
    copies = [pltpu.make_async_copy(a, b, sems.at[i]) for i, (a, b) in enumerate(pairs)]
    for copy in copies:
        copy.start()
    theirs = theirs_ref[...]
    chunk = fetched_ref[pl.ds(GIVEN_CHUNK, 128, stride=CHUNK2), :].T
    rels = jnp.concatenate([cols_ref[...].T[4:8, :], theirs[4:8, :], chunk[FIRST + 4 : FIRST + 8, :]], axis=0)
    indices = load_indices(rels, zh, core, index_vmem, index_smem, sem)
    theirs = jnp.concatenate([theirs, jnp.zeros((128 - LIST, 128), F32)], axis=0).T
    cols_out[...] = theirs
    hi, lo = split2(entity_ref[...].T)
    entity_hi[...] = hi
    entity_lo[...] = lo
    head_rows = [gather_heads(lists[:, 0:LIST], hi, lo) for lists in (cols_ref, theirs)]
    store_relations(table_ref, 0, near_ref[...].T)
    copies[0].wait()
    store_relations(table_ref, REL_DEV, near2_ref[...].T)
    for k, ref in enumerate((far_ref, far2_ref)):
        copies[1 + k].wait()
        for spot in range(PIECES):
            far_table[k, piece_start(spot) : piece_start(spot) + PIECE, :] = ref[spot, 0:PIECE, :]
        store_relations(table_ref, (2 + k) * REL_DEV, far_table[k].T)
        rest = [unfold(ref[spot, PIECE : PIECE + 4, :]) for spot in range(PIECES)]
        rest = [rest[spot][:, 0:PIECE] for spot in range(PIECES - 1)] + [rest[-1][:, PIECES * PIECE - D : PIECE]]
        store_relations(table_ref, (2 + k) * REL_DEV + MAIN, jnp.concatenate(rest, axis=1))
    indices.wait()
    for k in range(2):
        rel_rows = gather_relations(table_ref, index_smem, 4 * k, gathered)
        l_hi, l_lo = split2(head_rows[k] * rel_rows)
        span = pl.ds(k * SLOTS, SLOTS)
        rel_out[span, :] = rel_rows
        left_hi[span, :] = l_hi
        left_lo[span, :] = l_lo
    first_out[...] = gather_relations(table_ref, index_smem, 8, gathered)


def fill_block(hi_ref, lo_ref, mine, theirs, first):
    for k, (rows, lane) in enumerate(((mine, 0), (mine, D), (theirs, 0), (theirs, D))):
        hi, lo = split2(rows[:, first + lane : first + lane + D])
        hi_ref[128 * k : 128 * (k + 1), :] = hi
        lo_ref[128 * k : 128 * (k + 1), :] = lo


def lists_rows(lists):
    return jnp.concatenate([lists, jnp.zeros((128, 128 - LIST), F32)], axis=1).T


def head_kernel(mine_ref, theirs_ref, lists_mine, lists_theirs, rel_ref, left_hi, left_lo, grad_ref, block_hi, block_lo):
    _, core = place()
    fill_block(block_hi, block_lo, read_rows(mine_ref, CHUNK2), read_rows(theirs_ref, CHUNK2), 0)
    numbers = jnp.bitwise_xor(iota((128, ROWS), 1), core * HALF).astype(F32)
    heads_at = iota((ROWS, 128), 0).astype(F32)
    total = None
    for k in range(2):
        lists = (lists_mine, lists_theirs)[k][:, 0:LIST]
        span = pl.ds(k * SLOTS, SLOTS)
        hi, lo = left_hi[span, :], left_lo[span, :]
        b_hi, b_lo = block_hi[...], block_lo[...]
        scores = dot3_nt(hi, lo, b_hi, b_lo)
        tails = jnp.concatenate(
            [jnp.where(lists[:, 8 + j : 9 + j] == numbers, 1.0, 0.0) for j in range(4)], axis=0
        )
        drawn = sum(jnp.where(lists[:, 12 + j : 13 + j] == numbers, 1.0, 0.0) for j in range(3))
        times = jnp.sum(drawn, axis=0, keepdims=True) + tails
        scores = jnp.where(times > 0.0, scores, -3.0e38)
        weights = times * jnp.exp(scores - jnp.max(scores, axis=1, keepdims=True))
        weights = weights / jnp.sum(weights, axis=1, keepdims=True) - tails
        w_hi, w_lo = split2(weights)
        grad_left = dot_nn(w_hi, b_lo) + dot_nn(w_lo, b_hi) + dot_nn(w_hi, b_hi)
        g_hi, g_lo = split2(grad_left * rel_ref[span, :])
        rows = lists_rows(lists)
        marks = jnp.concatenate(
            [jnp.where(rows[j : j + 1, :] == heads_at, 1.0, 0.0) for j in range(4)], axis=1
        ).astype(BF16)
        part = dot_nn(marks, g_lo) + dot_nn(marks, g_hi)
        total = part if total is None else total + part
    grad_ref[...] = total


def given_kernel(fetched_ref, out_ref):
    out_ref[...] = fetched_ref[pl.ds(GIVEN_CHUNK, 128, stride=CHUNK2), :].T[FIRST + LIST : FIRST + 2 * LIST, :]


def tail_kernel(
    mine_ref, theirs_ref, given_ref, rel_ref, entity_hi, entity_lo, table_ref, head_grad,
    keep_ref, send_ref, block_hi, block_lo, gathered, index_vmem, index_smem, sem,
):
    zh, core = place()
    mine = read_rows(mine_ref, CHUNK2)
    fill_block(block_hi, block_lo, mine, read_rows(theirs_ref, CHUNK2), 2 * D)
    indices = load_indices(given_ref[4:8, :], zh, core, index_vmem, index_smem, sem)
    e_hi, e_lo = entity_hi[...], entity_lo[...]
    numbers = jnp.bitwise_xor(iota((128, ROWS), 1), core * HALF).astype(F32)
    rows_at = iota((ROWS, 128), 0).astype(F32)
    total = head_grad[...]
    for k in range(2):
        if k == 0:
            lists = mine[:, 4 * D : 4 * D + LIST]
            rel_rows = rel_ref[...]
        else:
            lists = jnp.concatenate([given_ref[...], jnp.zeros((128 - LIST, 128), F32)], axis=0).T[:, 0:LIST]
            indices.wait()
            rel_rows = gather_relations(table_ref, index_smem, 0, gathered)
        heads = onehot_cols(lists, 0, 4, numbers)
        head_rows = dot_nn(heads, block_hi[...]) + dot_nn(heads, block_lo[...])
        l_hi, l_lo = split2(head_rows * rel_rows)
        scores = dot3_nt(e_hi, e_lo, l_hi, l_lo)
        rows = lists_rows(lists)
        tails = jnp.concatenate(
            [jnp.where(rows[8 + j : 9 + j, :] == rows_at, 1.0, 0.0) for j in range(4)], axis=1
        )
        drawn = sum(jnp.where(rows[12 + j : 13 + j, :] == rows_at, 1.0, 0.0) for j in range(3))
        times = jnp.sum(drawn, axis=1, keepdims=True) + tails
        scores = jnp.where(times > 0.0, scores, -3.0e38)
        weights = times * jnp.exp(scores - jnp.max(scores, axis=0, keepdims=True))
        weights = weights / jnp.sum(weights, axis=0, keepdims=True) - tails
        w_hi, w_lo = split2(weights)
        total = total + (dot_nn(w_lo, l_hi) + dot_nn(w_hi, l_lo) + dot_nn(w_hi, l_hi))
    first, second = total[0:HALF, :].T, total[HALF:ROWS, :].T
    keep_ref[...] = jnp.where(core == 0, first, second)
    send_ref[...] = jnp.where(core == 0, second, first)


def combine_kernel(keep_ref, sent_ref, out_ref):
    _, core = place()
    out_ref[...] = keep_ref[...] + sent_ref[1 - core]


def update_kernel(gradient_ref, entity_ref, state_ref, updated_ref, accum_ref):
    for j in range(2):
        gradient = gradient_ref[j]
        span = slice(HALF * j, HALF * (j + 1))
        accum = state_ref[:, span] + jnp.sum(gradient * gradient, axis=0, keepdims=True) / float(D)
        accum_ref[:, span] = accum
        updated_ref[:, span] = entity_ref[:, span] - LEARN_RATE * gradient / jnp.sqrt(accum)


def call(kernel, out_shape, args, vmem, scratch=(), cost=None, space=pltpu.VMEM, in_hbm=()):
    out_shape = jax.tree.map(lambda s: jax.ShapeDtypeStruct(*s), out_shape, is_leaf=lambda s: isinstance(s, tuple))
    return pl.pallas_call(
        kernel,
        out_shape=out_shape,
        in_specs=[pl.BlockSpec(memory_space=pltpu.HBM if i in in_hbm else space) for i in range(len(args))],
        out_specs=jax.tree.map(lambda _: pl.BlockSpec(memory_space=pltpu.VMEM), out_shape),
        scratch_shapes=list(scratch),
        compiler_params=pltpu.CompilerParams(vmem_limit_bytes=vmem * MIB),
        cost_estimate=cost,
        name=getattr(kernel, "func", kernel).__name__,
    )(*args)


def flops(us):
    return pl.CostEstimate(flops=int(us * 1.0e9), bytes_accessed=4_000_000, transcendentals=0)


def shards(entity, state, relation, edge_head, edge_rel, edge_tail, negatives, counts, matching):
    swap_core = functools.partial(lax.ppermute, axis_name="core", perm=[(0, 1), (1, 0)])
    swap_zh = functools.partial(lax.ppermute, axis_name="zh", perm=[(0, 1), (1, 0)])
    exchange = functools.partial(lax.all_to_all, axis_name=("x", "yz"), split_axis=0, concat_axis=0, tiled=True)
    entity_t, relation_t = entity.T, relation.T

    payload, cols, give = call(
        pack_kernel,
        [((128 * CHUNK1, 128), F32), ((128, 128), F32), ((LIST, 128), F32)],
        (entity_t, edge_head, edge_rel, edge_tail, negatives, counts.transpose(1, 2, 0)),
        vmem=60,
        scratch=[pltpu.VMEM((128, 128), F32), pltpu.VMEM((D, ROWS), F32)]
        + [pltpu.VMEM((2, 1, 1, n), jnp.int32) for n in (SLOTS, SLOTS, SLOTS, NEGS)]
        + [pltpu.VMEM((1, 1, 2), jnp.int32), pltpu.SemaphoreType.DMA((6,))],
        space=pltpu.HBM,
    )
    spread = exchange(payload.reshape(128, 1, 128 * CHUNK1)).reshape(128 * CHUNK1, 128)

    bundle, matching = call(
        bundle_kernel,
        [((PIECE + 8, MAIN), F32), ((2, 128), jnp.int32)],
        (relation_t, matching),
        vmem=8,
    )
    lines = lax.axis_size("yz") // 4
    mirror = [((4 * y + z) * 2 + h, (4 * y + 3 - z) * 2 + 1 - h) for y in range(lines) for z in range(4) for h in range(2)]
    bundle = lax.ppermute(bundle, ("yz", "zh"), perm=mirror)
    theirs = swap_zh(give)
    near2 = swap_core(relation_t)
    spread, bundle, theirs = lax.optimization_barrier((spread, bundle, theirs))

    routed = call(
        route_kernel,
        ((128 * CHUNK2, 128), F32),
        (spread, matching),
        vmem=16,
    )
    fetched = exchange(routed.reshape(128, 1, 128 * CHUNK2)).reshape(128 * CHUNK2, 128)
    bundle, _ = lax.optimization_barrier((bundle, routed))
    far = lax.all_gather(bundle, "x", axis=0)
    far2 = swap_core(far)
    fetched_other = swap_core(fetched)
    given = swap_zh(call(given_kernel, ((LIST, 128), F32), (fetched,), vmem=4))
    gather = [
        pltpu.VMEM((4 * SLOTS, 128), F32),
        pltpu.VMEM((16, 128), jnp.int32),
        pltpu.SMEM((16, 128), jnp.int32),
        pltpu.SemaphoreType.DMA,
    ]
    rel_rows, left_hi, left_lo, first_rel, table, entity_hi, entity_lo, cols_other = call(
        relations_kernel,
        [
            ((2 * SLOTS, D), F32),
            ((2 * SLOTS, D), BF16),
            ((2 * SLOTS, D), BF16),
            ((SLOTS, D), F32),
            ((4 * TABLE, 128), F32),
            ((ROWS, D), BF16),
            ((ROWS, D), BF16),
            ((128, 128), F32),
        ],
        (entity_t, cols, theirs, relation_t, near2, far, far2, fetched),
        vmem=32,
        scratch=[pltpu.VMEM((D, REL_DEV), F32)]
        + [pltpu.VMEM((PIECES, PIECE + 8, MAIN), F32)] * 2
        + [pltpu.VMEM((2, D, MAIN), F32)]
        + gather
        + [pltpu.SemaphoreType.DMA((3,))],
        cost=flops(8),
        in_hbm=(4, 5, 6),
    )
    block = [pltpu.VMEM((ROWS, D), BF16), pltpu.VMEM((ROWS, D), BF16)]
    head_grad = call(
        head_kernel,
        ((ROWS, D), F32),
        (fetched, fetched_other, cols, cols_other, rel_rows, left_hi, left_lo),
        vmem=20,
        scratch=block,
        cost=flops(6),
    )
    keep, send = call(
        tail_kernel,
        [((D, HALF), F32)] * 2,
        (fetched, fetched_other, given, first_rel, entity_hi, entity_lo, table, head_grad),
        vmem=28,
        scratch=block + gather,
        cost=flops(9),
    )
    sent = lax.all_gather(send, "core", axis=0)
    half = call(combine_kernel, ((D, HALF), F32), (keep, sent), vmem=8)
    chips = lax.all_gather(half, "zh", axis=0)
    gradient = lax.all_gather(chips[0] + chips[1], "core", axis=0)
    updated, accum = call(
        update_kernel,
        [((D, ROWS), F32), ((1, ROWS), F32)],
        (gradient, entity_t, state.reshape(1, ROWS)),
        vmem=8,
    )
    return updated.T, accum.reshape(ROWS)


def solution(mesh):
    parts = (PIECES, mesh.shape["dom"] // PIECES, 2, 2)
    fine = jax.sharding.Mesh(mesh.devices.reshape(parts), ("x", "yz", "zh", "core"))
    dom, edge = ("x", "yz"), ("zh", "core")
    return jax.shard_map(
        shards,
        mesh=fine,
        in_specs=(
            P(dom, None),
            P(dom),
            P(edge, None),
            P(None, dom, edge, None),
            P(None, dom, edge, None),
            P(None, dom, edge, None),
            P(None, dom, edge, None),
            P(None, dom, edge),
            P(),
        ),
        out_specs=(P(dom, None), P(dom)),
        check_vma=False,
    )
```

```python
import functools

import jax
import jax.numpy as jnp
from jax import lax
from jax.experimental import pallas as pl
from jax.experimental.pallas import tpu as pltpu
from jax.sharding import PartitionSpec as P


LEARN_RATE = 0.1
D = 400
ROWS = 512
HALF = 256
SLOTS = 512
NEGS = 320
REL_DEV = 528
PIECES = 4
PIECE = 104
MAIN = 512
REST = REL_DEV - MAIN
TABLE = 4 * REL_DEV
LIST = 16
CHUNK1 = 7
CHUNK2 = 13
GIVEN_CHUNK = 12
FIRST = 4 * D - 128 * GIVEN_CHUNK
F32 = jnp.float32
BF16 = jnp.bfloat16
MIB = 1024 * 1024


def split2(x):
    hi = x.astype(BF16)
    return hi, (x - hi.astype(F32)).astype(BF16)


def split3(x):
    hi = x.astype(BF16)
    rest = x - hi.astype(F32)
    mid = rest.astype(BF16)
    return hi, mid, (rest - mid.astype(F32)).astype(BF16)


def dot_nn(a, b):
    return lax.dot_general(a, b, (((1,), (0,)), ((), ())), preferred_element_type=F32)


def dot_nt(a, b):
    return lax.dot_general(a, b, (((1,), (1,)), ((), ())), preferred_element_type=F32)


def dot3_nt(a_hi, a_lo, b_hi, b_lo):
    return dot_nt(jnp.concatenate([a_hi, a_lo, a_hi], axis=1), jnp.concatenate([b_lo, b_hi, b_hi], axis=1))


def iota(shape, dim):
    return lax.broadcasted_iota(jnp.int32, shape, dim)


def place():
    return lax.axis_index("zh"), lax.axis_index("core")


def read_rows(ref, chunks):
    return jnp.concatenate([ref[pl.ds(k, 128, stride=chunks), :] for k in range(chunks)], axis=1)


def write_rows(ref, value, chunks):
    for k in range(chunks):
        ref[pl.ds(k, 128, stride=chunks), :] = value[:, 128 * k : 128 * (k + 1)]


def onehot_cols(lists, first, count, columns):
    blocks = [(lists[:, first + j : first + j + 1] == columns) for j in range(count)]
    return jnp.concatenate([jnp.where(b, 1.0, 0.0).astype(BF16) for b in blocks], axis=0)


def pack_kernel(
    entity_hbm, head_hbm, rel_hbm, tail_hbm, neg_hbm, count_hbm, out_ref, cols_ref, give_ref,
    rows_ref, entity_ref, head_ref, rel_ref, tail_ref, neg_ref, count_ref, sems,
):
    zh, core = place()
    pairs = (
        (head_hbm, head_ref), (rel_hbm, rel_ref), (tail_hbm, tail_ref), (neg_hbm, neg_ref), (count_hbm, count_ref),
        (entity_hbm, entity_ref),
    )
    copies = [pltpu.make_async_copy(a, b, sems.at[i]) for i, (a, b) in enumerate(pairs)]
    for copy in copies:
        copy.start()
    rows_ref[...] = jnp.full((128, 128), -1.0, F32)
    lane = iota((1, 128), 1)
    for copy in copies[:-1]:
        copy.wait()
    for bucket in range(2):
        at = bucket * LIST
        live = count_ref[0, :, bucket : bucket + 1]
        for j in range(4):
            span = pl.ds(128 * j, 128)
            head = jnp.where(lane + 128 * j < live, head_ref[bucket, 0, 0:1, span], -1)
            rows_ref[at + j : at + j + 1, :] = head.astype(F32)
            rows_ref[at + 4 + j : at + 5 + j, :] = rel_ref[bucket, 0, 0:1, span].astype(F32)
            rows_ref[at + 8 + j : at + 9 + j, :] = tail_ref[bucket, 0, 0:1, span].astype(F32)
        rows_ref[at + 12 : at + 13, :] = neg_ref[bucket, 0, 0:1, 0:128].astype(F32)
        rows_ref[at + 13 : at + 14, :] = neg_ref[bucket, 0, 0:1, 128:256].astype(F32)
        rows_ref[at + 14 : at + 15, 0:64] = neg_ref[bucket, 0, 0:1, 256:320].astype(F32)
    one, two = rows_ref[0:LIST, :], rows_ref[LIST : 2 * LIST, :]
    keep = jnp.where(zh == 0, one, two)
    give = jnp.where(zh == 0, two, one)
    both = jnp.concatenate([keep, give, rows_ref[2 * LIST :, :]], axis=0).T
    cols_ref[...] = both
    give_ref[...] = give
    copies[-1].wait()
    half = jnp.where(core == 0, entity_ref[:, 0:HALF], entity_ref[:, HALF:ROWS]).T
    payload = jnp.concatenate([half[0:128, :], half[128:HALF, :], both[:, 0 : 128 * CHUNK1 - 2 * D]], axis=1)
    write_rows(out_ref, payload, CHUNK1)


def route_kernel(x_ref, matching_ref, out_ref):
    zh, _ = place()
    parts = split3(read_rows(x_ref, CHUNK1))
    rows = iota((128, 128), 0)
    marks = [jnp.where(matching_ref[b : b + 1, :] == rows, 1.0, 0.0) for b in range(2)]
    back_keep = jnp.where(zh == 0, marks[0], marks[1])
    back_give = jnp.where(zh == 0, marks[1], marks[0])
    fore = back_keep.T.astype(BF16)
    back_keep, back_give = back_keep.astype(BF16), back_give.astype(BF16)
    partner = sum(dot_nn(fore, p) for p in reversed(parts))
    source = sum(dot_nn(back_keep, p) for p in reversed(parts))
    given = sum(dot_nn(back_give, p[:, 768 : 128 * CHUNK1]) for p in reversed(parts))
    fill = jnp.zeros((128, 128 * CHUNK2 - 4 * D - 2 * LIST), F32)
    routed = jnp.concatenate([partner[:, 0 : 2 * D], source[:, 0 : 2 * D + LIST], given[:, 48:64], fill], axis=1)
    write_rows(out_ref, routed, CHUNK2)


def table_row(rel, zh, core):
    owner = (rel >= REL_DEV).astype(jnp.int32) + (rel >= 2 * REL_DEV).astype(jnp.int32)
    owner = owner + (rel >= 3 * REL_DEV).astype(jnp.int32)
    off = rel - REL_DEV * owner
    owner_zh = (owner >= 2).astype(jnp.int32)
    other_core = (owner - 2 * owner_zh) != core
    return jnp.where(owner_zh == zh, 0, 2 * REL_DEV) + jnp.where(other_core, REL_DEV, 0) + off


def piece_start(spot):
    return min(PIECE * spot, D - PIECE)


def bundle_kernel(relation_hbm, out_ref, piece_ref, sem):
    spot = lax.axis_index("x")
    start = pl.multiple_of(jnp.minimum(PIECE * spot, D - PIECE), 8)
    copy = pltpu.make_async_copy(relation_hbm.at[pl.ds(start, PIECE), :], piece_ref, sem)
    copy.start()
    copy.wait()
    piece = piece_ref[...]
    out_ref[0:PIECE, :] = piece[:, 0:MAIN]
    rest = jnp.concatenate([piece[:, MAIN:REL_DEV], jnp.zeros((PIECE, 128 - REST), F32)], axis=1)
    rest = jnp.concatenate([rest, jnp.zeros((128 - PIECE, 128), F32)], axis=0).T
    for g in range(4):
        out_ref[PIECE : PIECE + 4, 128 * g : 128 * (g + 1)] = rest[4 * g : 4 * g + 4, :]
    out_ref[PIECE + 4 : PIECE + 8, :] = jnp.zeros((4, MAIN), F32)


def lists_kernel(give_ref, matching_ref, give_out, matching_out):
    give_out[...] = give_ref[...]
    matching_out[...] = matching_ref[...]


def unfold(rows):
    return jnp.concatenate([rows[:, 128 * g : 128 * (g + 1)] for g in range(4)], axis=0)


def store_relations(table_ref, first, rows):
    padded = jnp.concatenate([rows, jnp.zeros((rows.shape[0], 512 - D), F32)], axis=1)
    for k in range(4):
        table_ref[pl.ds(4 * first + k, rows.shape[0], stride=4), :] = padded[:, 128 * k : 128 * (k + 1)]


def load_indices(rels, zh, core, index_vmem, index_smem, sem):
    rels = jnp.concatenate([rels, jnp.zeros((16 - rels.shape[0], 128), F32)], axis=0)
    index_vmem[...] = 4 * table_row(rels.astype(jnp.int32), zh, core)
    copy = pltpu.make_async_copy(index_vmem, index_smem, sem)
    copy.start()
    return copy


def gather_relations(table_ref, index_smem, first, out_ref):
    def body(step, _):
        for j in range(4):
            for u in range(8):
                lane = step * 8 + u
                at = pl.multiple_of(index_smem[first + j, lane], 4)
                to = pl.multiple_of(512 * j + 4 * lane, 4)
                out_ref[pl.ds(to, 4), :] = table_ref[pl.ds(at, 4), :]
        return 0

    lax.fori_loop(0, 16, body, 0)
    return jnp.concatenate([out_ref[pl.ds(k, SLOTS, stride=4), :] for k in range(4)], axis=1)[:, 0:D]


def gather_heads(lists, hi, lo):
    heads = onehot_cols(lists, 0, 4, iota((128, ROWS), 1).astype(F32))
    return dot_nn(heads, hi) + dot_nn(heads, lo)


def relations_kernel(
    entity_ref, cols_ref, theirs_ref, near_ref, near2_hbm, far_hbm, far2_hbm, fetched_ref,
    rel_out, left_hi, left_lo, first_out, table_ref, entity_hi, entity_lo, cols_out,
    near2_ref, far_ref, far2_ref, far_table, gathered, index_vmem, index_smem, sem, sems,
):
    zh, core = place()
    pairs = ((near2_hbm, near2_ref), (far_hbm, far_ref), (far2_hbm, far2_ref))
    copies = [pltpu.make_async_copy(a, b, sems.at[i]) for i, (a, b) in enumerate(pairs)]
    for copy in copies:
        copy.start()
    theirs = theirs_ref[...]
    chunk = fetched_ref[pl.ds(GIVEN_CHUNK, 128, stride=CHUNK2), :].T
    rels = jnp.concatenate([cols_ref[...].T[4:8, :], theirs[4:8, :], chunk[FIRST + 4 : FIRST + 8, :]], axis=0)
    indices = load_indices(rels, zh, core, index_vmem, index_smem, sem)
    theirs = jnp.concatenate([theirs, jnp.zeros((128 - LIST, 128), F32)], axis=0).T
    cols_out[...] = theirs
    hi, lo = split2(entity_ref[...].T)
    entity_hi[...] = hi
    entity_lo[...] = lo
    head_rows = [gather_heads(lists[:, 0:LIST], hi, lo) for lists in (cols_ref, theirs)]
    store_relations(table_ref, 0, near_ref[...].T)
    copies[0].wait()
    store_relations(table_ref, REL_DEV, near2_ref[...].T)
    for k, ref in enumerate((far_ref, far2_ref)):
        copies[1 + k].wait()
        for spot in range(PIECES):
            far_table[k, piece_start(spot) : piece_start(spot) + PIECE, :] = ref[spot, 0:PIECE, :]
        store_relations(table_ref, (2 + k) * REL_DEV, far_table[k].T)
        rest = [unfold(ref[spot, PIECE : PIECE + 4, :]) for spot in range(PIECES)]
        rest = [rest[spot][:, 0:PIECE] for spot in range(PIECES - 1)] + [rest[-1][:, PIECES * PIECE - D : PIECE]]
        store_relations(table_ref, (2 + k) * REL_DEV + MAIN, jnp.concatenate(rest, axis=1))
    indices.wait()
    for k in range(2):
        rel_rows = gather_relations(table_ref, index_smem, 4 * k, gathered)
        l_hi, l_lo = split2(head_rows[k] * rel_rows)
        span = pl.ds(k * SLOTS, SLOTS)
        rel_out[span, :] = rel_rows
        left_hi[span, :] = l_hi
        left_lo[span, :] = l_lo
    first_out[...] = gather_relations(table_ref, index_smem, 8, gathered)


def fill_block(hi_ref, lo_ref, mine, theirs, first):
    for k, (rows, lane) in enumerate(((mine, 0), (mine, D), (theirs, 0), (theirs, D))):
        hi, lo = split2(rows[:, first + lane : first + lane + D])
        hi_ref[128 * k : 128 * (k + 1), :] = hi
        lo_ref[128 * k : 128 * (k + 1), :] = lo


def lists_rows(lists):
    return jnp.concatenate([lists, jnp.zeros((128, 128 - LIST), F32)], axis=1).T


def head_kernel(mine_ref, theirs_ref, lists_mine, lists_theirs, rel_ref, left_hi, left_lo, grad_ref, block_hi, block_lo):
    _, core = place()
    fill_block(block_hi, block_lo, read_rows(mine_ref, CHUNK2), read_rows(theirs_ref, CHUNK2), 0)
    numbers = jnp.bitwise_xor(iota((128, ROWS), 1), core * HALF).astype(F32)
    heads_at = iota((ROWS, 128), 0).astype(F32)
    total = None
    for k in range(2):
        lists = (lists_mine, lists_theirs)[k][:, 0:LIST]
        span = pl.ds(k * SLOTS, SLOTS)
        hi, lo = left_hi[span, :], left_lo[span, :]
        b_hi, b_lo = block_hi[...], block_lo[...]
        scores = dot3_nt(hi, lo, b_hi, b_lo)
        tails = jnp.concatenate(
            [jnp.where(lists[:, 8 + j : 9 + j] == numbers, 1.0, 0.0) for j in range(4)], axis=0
        )
        drawn = sum(jnp.where(lists[:, 12 + j : 13 + j] == numbers, 1.0, 0.0) for j in range(3))
        times = jnp.sum(drawn, axis=0, keepdims=True) + tails
        scores = jnp.where(times > 0.0, scores, -3.0e38)
        weights = times * jnp.exp(scores - jnp.max(scores, axis=1, keepdims=True))
        weights = weights / jnp.sum(weights, axis=1, keepdims=True) - tails
        w_hi, w_lo = split2(weights)
        grad_left = dot_nn(w_hi, b_lo) + dot_nn(w_lo, b_hi) + dot_nn(w_hi, b_hi)
        g_hi, g_lo = split2(grad_left * rel_ref[span, :])
        rows = lists_rows(lists)
        marks = jnp.concatenate(
            [jnp.where(rows[j : j + 1, :] == heads_at, 1.0, 0.0) for j in range(4)], axis=1
        ).astype(BF16)
        part = dot_nn(marks, g_lo) + dot_nn(marks, g_hi)
        total = part if total is None else total + part
    grad_ref[...] = total


def given_kernel(fetched_ref, out_ref):
    out_ref[...] = fetched_ref[pl.ds(GIVEN_CHUNK, 128, stride=CHUNK2), :].T[FIRST + LIST : FIRST + 2 * LIST, :]


def tail_kernel(
    mine_ref, theirs_ref, given_ref, rel_ref, entity_hi, entity_lo, table_ref, head_grad,
    keep_ref, send_ref, block_hi, block_lo, gathered, index_vmem, index_smem, sem,
):
    zh, core = place()
    mine = read_rows(mine_ref, CHUNK2)
    fill_block(block_hi, block_lo, mine, read_rows(theirs_ref, CHUNK2), 2 * D)
    indices = load_indices(given_ref[4:8, :], zh, core, index_vmem, index_smem, sem)
    e_hi, e_lo = entity_hi[...], entity_lo[...]
    numbers = jnp.bitwise_xor(iota((128, ROWS), 1), core * HALF).astype(F32)
    rows_at = iota((ROWS, 128), 0).astype(F32)
    total = head_grad[...]
    for k in range(2):
        if k == 0:
            lists = mine[:, 4 * D : 4 * D + LIST]
            rel_rows = rel_ref[...]
        else:
            lists = jnp.concatenate([given_ref[...], jnp.zeros((128 - LIST, 128), F32)], axis=0).T[:, 0:LIST]
            indices.wait()
            rel_rows = gather_relations(table_ref, index_smem, 0, gathered)
        heads = onehot_cols(lists, 0, 4, numbers)
        head_rows = dot_nn(heads, block_hi[...]) + dot_nn(heads, block_lo[...])
        l_hi, l_lo = split2(head_rows * rel_rows)
        scores = dot3_nt(e_hi, e_lo, l_hi, l_lo)
        rows = lists_rows(lists)
        tails = jnp.concatenate(
            [jnp.where(rows[8 + j : 9 + j, :] == rows_at, 1.0, 0.0) for j in range(4)], axis=1
        )
        drawn = sum(jnp.where(rows[12 + j : 13 + j, :] == rows_at, 1.0, 0.0) for j in range(3))
        times = jnp.sum(drawn, axis=1, keepdims=True) + tails
        scores = jnp.where(times > 0.0, scores, -3.0e38)
        weights = times * jnp.exp(scores - jnp.max(scores, axis=0, keepdims=True))
        weights = weights / jnp.sum(weights, axis=0, keepdims=True) - tails
        w_hi, w_lo = split2(weights)
        total = total + (dot_nn(w_lo, l_hi) + dot_nn(w_hi, l_lo) + dot_nn(w_hi, l_hi))
    first, second = total[0:HALF, :].T, total[HALF:ROWS, :].T
    keep_ref[...] = jnp.where(core == 0, first, second)
    send_ref[...] = jnp.where(core == 0, second, first)


def combine_kernel(keep_ref, sent_ref, out_ref):
    _, core = place()
    out_ref[...] = keep_ref[...] + sent_ref[1 - core]


def update_kernel(gradient_ref, entity_ref, state_ref, updated_ref, accum_ref):
    for j in range(2):
        gradient = gradient_ref[j]
        span = slice(HALF * j, HALF * (j + 1))
        accum = state_ref[:, span] + jnp.sum(gradient * gradient, axis=0, keepdims=True) / float(D)
        accum_ref[:, span] = accum
        updated_ref[:, span] = entity_ref[:, span] - LEARN_RATE * gradient / jnp.sqrt(accum)


def call(kernel, out_shape, args, vmem, scratch=(), cost=None, space=pltpu.VMEM, in_hbm=()):
    out_shape = jax.tree.map(lambda s: jax.ShapeDtypeStruct(*s), out_shape, is_leaf=lambda s: isinstance(s, tuple))
    return pl.pallas_call(
        kernel,
        out_shape=out_shape,
        in_specs=[pl.BlockSpec(memory_space=pltpu.HBM if i in in_hbm else space) for i in range(len(args))],
        out_specs=jax.tree.map(lambda _: pl.BlockSpec(memory_space=pltpu.VMEM), out_shape),
        scratch_shapes=list(scratch),
        compiler_params=pltpu.CompilerParams(vmem_limit_bytes=vmem * MIB),
        cost_estimate=cost,
        name=getattr(kernel, "func", kernel).__name__,
    )(*args)


def flops(us):
    return pl.CostEstimate(flops=int(us * 1.0e9), bytes_accessed=4_000_000, transcendentals=0)


def shards(entity, state, relation, edge_head, edge_rel, edge_tail, negatives, counts, matching):
    swap_core = functools.partial(lax.ppermute, axis_name="core", perm=[(0, 1), (1, 0)])
    swap_zh = functools.partial(lax.ppermute, axis_name="zh", perm=[(0, 1), (1, 0)])
    exchange = functools.partial(lax.all_to_all, axis_name=("x", "yz"), split_axis=0, concat_axis=0, tiled=True)
    entity_t, relation_t = entity.T, relation.T

    payload, cols, give = call(
        pack_kernel,
        [((128 * CHUNK1, 128), F32), ((128, 128), F32), ((LIST, 128), F32)],
        (entity_t, edge_head, edge_rel, edge_tail, negatives, counts.transpose(1, 2, 0)),
        vmem=60,
        scratch=[pltpu.VMEM((128, 128), F32), pltpu.VMEM((D, ROWS), F32)]
        + [pltpu.VMEM((2, 1, 1, n), jnp.int32) for n in (SLOTS, SLOTS, SLOTS, NEGS)]
        + [pltpu.VMEM((1, 1, 2), jnp.int32), pltpu.SemaphoreType.DMA((6,))],
        space=pltpu.HBM,
    )
    spread = exchange(payload.reshape(128, 1, 128 * CHUNK1)).reshape(128 * CHUNK1, 128)

    bundle = call(
        bundle_kernel,
        ((PIECE + 8, MAIN), F32),
        (relation_t,),
        vmem=60,
        scratch=[pltpu.VMEM((PIECE, REL_DEV), F32), pltpu.SemaphoreType.DMA],
        in_hbm=(0,),
    )
    give, matching = call(lists_kernel, [((LIST, 128), F32), ((2, 128), jnp.int32)], (give, matching), vmem=4)
    lines = lax.axis_size("yz") // 4
    mirror = [((4 * y + z) * 2 + h, (4 * y + 3 - z) * 2 + 1 - h) for y in range(lines) for z in range(4) for h in range(2)]
    bundle = lax.ppermute(bundle, ("yz", "zh"), perm=mirror)
    theirs = swap_zh(give)
    near2 = swap_core(relation_t)
    spread, bundle, theirs = lax.optimization_barrier((spread, bundle, theirs))

    routed = call(
        route_kernel,
        ((128 * CHUNK2, 128), F32),
        (spread, matching),
        vmem=16,
    )
    fetched = exchange(routed.reshape(128, 1, 128 * CHUNK2)).reshape(128 * CHUNK2, 128)
    bundle, _ = lax.optimization_barrier((bundle, routed))
    far = lax.all_gather(bundle, "x", axis=0)
    far2 = swap_core(far)
    fetched_other = swap_core(fetched)
    given = swap_zh(call(given_kernel, ((LIST, 128), F32), (fetched,), vmem=4))
    gather = [
        pltpu.VMEM((4 * SLOTS, 128), F32),
        pltpu.VMEM((16, 128), jnp.int32),
        pltpu.SMEM((16, 128), jnp.int32),
        pltpu.SemaphoreType.DMA,
    ]
    rel_rows, left_hi, left_lo, first_rel, table, entity_hi, entity_lo, cols_other = call(
        relations_kernel,
        [
            ((2 * SLOTS, D), F32),
            ((2 * SLOTS, D), BF16),
            ((2 * SLOTS, D), BF16),
            ((SLOTS, D), F32),
            ((4 * TABLE, 128), F32),
            ((ROWS, D), BF16),
            ((ROWS, D), BF16),
            ((128, 128), F32),
        ],
        (entity_t, cols, theirs, relation_t, near2, far, far2, fetched),
        vmem=32,
        scratch=[pltpu.VMEM((D, REL_DEV), F32)]
        + [pltpu.VMEM((PIECES, PIECE + 8, MAIN), F32)] * 2
        + [pltpu.VMEM((2, D, MAIN), F32)]
        + gather
        + [pltpu.SemaphoreType.DMA((3,))],
        cost=flops(8),
        in_hbm=(4, 5, 6),
    )
    block = [pltpu.VMEM((ROWS, D), BF16), pltpu.VMEM((ROWS, D), BF16)]
    head_grad = call(
        head_kernel,
        ((ROWS, D), F32),
        (fetched, fetched_other, cols, cols_other, rel_rows, left_hi, left_lo),
        vmem=20,
        scratch=block,
        cost=flops(6),
    )
    keep, send = call(
        tail_kernel,
        [((D, HALF), F32)] * 2,
        (fetched, fetched_other, given, first_rel, entity_hi, entity_lo, table, head_grad),
        vmem=28,
        scratch=block + gather,
        cost=flops(9),
    )
    sent = lax.all_gather(send, "core", axis=0)
    half = call(combine_kernel, ((D, HALF), F32), (keep, sent), vmem=8)
    chips = lax.all_gather(half, "zh", axis=0)
    gradient = lax.all_gather(chips[0] + chips[1], "core", axis=0)
    updated, accum = call(
        update_kernel,
        [((D, ROWS), F32), ((1, ROWS), F32)],
        (gradient, entity_t, state.reshape(1, ROWS)),
        vmem=8,
    )
    return updated.T, accum.reshape(ROWS)


def solution(mesh):
    parts = (PIECES, mesh.shape["dom"] // PIECES, 2, 2)
    fine = jax.sharding.Mesh(mesh.devices.reshape(parts), ("x", "yz", "zh", "core"))
    dom, edge = ("x", "yz"), ("zh", "core")
    return jax.shard_map(
        shards,
        mesh=fine,
        in_specs=(
            P(dom, None),
            P(dom),
            P(edge, None),
            P(None, dom, edge, None),
            P(None, dom, edge, None),
            P(None, dom, edge, None),
            P(None, dom, edge, None),
            P(None, dom, edge),
            P(),
        ),
        out_specs=(P(dom, None), P(dom)),
        check_vma=False,
    )
```

```python
import functools

import jax
import jax.numpy as jnp
from jax import lax
from jax.experimental import pallas as pl
from jax.experimental.pallas import tpu as pltpu
from jax.sharding import PartitionSpec as P


LEARN_RATE = 0.1
D = 400
ROWS = 512
HALF = 256
SLOTS = 512
NEGS = 320
REL_DEV = 528
PIECES = 4
PIECE = 104
MAIN = 512
REST = REL_DEV - MAIN
TABLE = 4 * REL_DEV
LIST = 16
CHUNK1 = 7
CHUNK2 = 13
GIVEN_CHUNK = 12
FIRST = 4 * D - 128 * GIVEN_CHUNK
F32 = jnp.float32
BF16 = jnp.bfloat16
MIB = 1024 * 1024


def split2(x):
    hi = x.astype(BF16)
    return hi, (x - hi.astype(F32)).astype(BF16)


def split3(x):
    hi = x.astype(BF16)
    rest = x - hi.astype(F32)
    mid = rest.astype(BF16)
    return hi, mid, (rest - mid.astype(F32)).astype(BF16)


def dot_nn(a, b):
    return lax.dot_general(a, b, (((1,), (0,)), ((), ())), preferred_element_type=F32)


def dot_nt(a, b):
    return lax.dot_general(a, b, (((1,), (1,)), ((), ())), preferred_element_type=F32)


def dot3_nt(a_hi, a_lo, b_hi, b_lo):
    return dot_nt(jnp.concatenate([a_hi, a_lo, a_hi], axis=1), jnp.concatenate([b_lo, b_hi, b_hi], axis=1))


def iota(shape, dim):
    return lax.broadcasted_iota(jnp.int32, shape, dim)


def place():
    return lax.axis_index("zh"), lax.axis_index("core")


def read_rows(ref, chunks):
    return jnp.concatenate([ref[pl.ds(k, 128, stride=chunks), :] for k in range(chunks)], axis=1)


def write_rows(ref, value, chunks):
    for k in range(chunks):
        ref[pl.ds(k, 128, stride=chunks), :] = value[:, 128 * k : 128 * (k + 1)]


def onehot_cols(lists, first, count, columns):
    blocks = [(lists[:, first + j : first + j + 1] == columns) for j in range(count)]
    return jnp.concatenate([jnp.where(b, 1.0, 0.0).astype(BF16) for b in blocks], axis=0)


def pack_kernel(
    entity_hbm, head_hbm, rel_hbm, tail_hbm, neg_hbm, count_hbm, out_ref, cols_ref, give_ref,
    rows_ref, entity_ref, head_ref, rel_ref, tail_ref, neg_ref, count_ref, sems,
):
    zh, core = place()
    pairs = (
        (head_hbm, head_ref), (rel_hbm, rel_ref), (tail_hbm, tail_ref), (neg_hbm, neg_ref), (count_hbm, count_ref),
        (entity_hbm, entity_ref),
    )
    copies = [pltpu.make_async_copy(a, b, sems.at[i]) for i, (a, b) in enumerate(pairs)]
    for copy in copies:
        copy.start()
    rows_ref[...] = jnp.full((128, 128), -1.0, F32)
    lane = iota((1, 128), 1)
    for copy in copies[:-1]:
        copy.wait()
    for bucket in range(2):
        at = bucket * LIST
        live = count_ref[0, :, bucket : bucket + 1]
        for j in range(4):
            span = pl.ds(128 * j, 128)
            head = jnp.where(lane + 128 * j < live, head_ref[bucket, 0, 0:1, span], -1)
            rows_ref[at + j : at + j + 1, :] = head.astype(F32)
            rows_ref[at + 4 + j : at + 5 + j, :] = rel_ref[bucket, 0, 0:1, span].astype(F32)
            rows_ref[at + 8 + j : at + 9 + j, :] = tail_ref[bucket, 0, 0:1, span].astype(F32)
        rows_ref[at + 12 : at + 13, :] = neg_ref[bucket, 0, 0:1, 0:128].astype(F32)
        rows_ref[at + 13 : at + 14, :] = neg_ref[bucket, 0, 0:1, 128:256].astype(F32)
        rows_ref[at + 14 : at + 15, 0:64] = neg_ref[bucket, 0, 0:1, 256:320].astype(F32)
    one, two = rows_ref[0:LIST, :], rows_ref[LIST : 2 * LIST, :]
    keep = jnp.where(zh == 0, one, two)
    give = jnp.where(zh == 0, two, one)
    both = jnp.concatenate([keep, give, rows_ref[2 * LIST :, :]], axis=0).T
    cols_ref[...] = both
    give_ref[...] = give
    copies[-1].wait()
    half = jnp.where(core == 0, entity_ref[:, 0:HALF], entity_ref[:, HALF:ROWS]).T
    payload = jnp.concatenate([half[0:128, :], half[128:HALF, :], both[:, 0 : 128 * CHUNK1 - 2 * D]], axis=1)
    write_rows(out_ref, payload, CHUNK1)


def route_kernel(x_ref, matching_ref, out_ref):
    zh, _ = place()
    parts = split3(read_rows(x_ref, CHUNK1))
    rows = iota((128, 128), 0)
    marks = [jnp.where(matching_ref[b : b + 1, :] == rows, 1.0, 0.0) for b in range(2)]
    back_keep = jnp.where(zh == 0, marks[0], marks[1])
    back_give = jnp.where(zh == 0, marks[1], marks[0])
    fore = back_keep.T.astype(BF16)
    back_keep, back_give = back_keep.astype(BF16), back_give.astype(BF16)
    partner = sum(dot_nn(fore, p) for p in reversed(parts))
    source = sum(dot_nn(back_keep, p) for p in reversed(parts))
    given = sum(dot_nn(back_give, p[:, 768 : 128 * CHUNK1]) for p in reversed(parts))
    fill = jnp.zeros((128, 128 * CHUNK2 - 4 * D - 2 * LIST), F32)
    routed = jnp.concatenate([partner[:, 0 : 2 * D], source[:, 0 : 2 * D + LIST], given[:, 48:64], fill], axis=1)
    write_rows(out_ref, routed, CHUNK2)


def table_row(rel, zh, core):
    owner = (rel >= REL_DEV).astype(jnp.int32) + (rel >= 2 * REL_DEV).astype(jnp.int32)
    owner = owner + (rel >= 3 * REL_DEV).astype(jnp.int32)
    off = rel - REL_DEV * owner
    owner_zh = (owner >= 2).astype(jnp.int32)
    other_core = (owner - 2 * owner_zh) != core
    return jnp.where(owner_zh == zh, 0, 2 * REL_DEV) + jnp.where(other_core, REL_DEV, 0) + off


def piece_start(spot):
    return min(PIECE * spot, D - PIECE)


def bundle_kernel(relation_hbm, out_ref, piece_ref, sem):
    spot = lax.axis_index("x")
    start = pl.multiple_of(jnp.minimum(PIECE * spot, D - PIECE), 8)
    copy = pltpu.make_async_copy(relation_hbm.at[pl.ds(start, PIECE), :], piece_ref, sem)
    copy.start()
    copy.wait()
    piece = piece_ref[...]
    out_ref[0:PIECE, :] = piece[:, 0:MAIN]
    rest = jnp.concatenate([piece[:, MAIN:REL_DEV], jnp.zeros((PIECE, 128 - REST), F32)], axis=1)
    rest = jnp.concatenate([rest, jnp.zeros((128 - PIECE, 128), F32)], axis=0).T
    for g in range(4):
        out_ref[PIECE : PIECE + 4, 128 * g : 128 * (g + 1)] = rest[4 * g : 4 * g + 4, :]
    out_ref[PIECE + 4 : PIECE + 8, :] = jnp.zeros((4, MAIN), F32)


def lists_kernel(give_ref, matching_ref, give_out, matching_out):
    give_out[...] = give_ref[...]
    matching_out[...] = matching_ref[...]


def unfold(rows):
    return jnp.concatenate([rows[:, 128 * g : 128 * (g + 1)] for g in range(4)], axis=0)


def store_relations(table_ref, first, rows):
    padded = jnp.concatenate([rows, jnp.zeros((rows.shape[0], 512 - D), F32)], axis=1)
    for k in range(4):
        table_ref[pl.ds(4 * first + k, rows.shape[0], stride=4), :] = padded[:, 128 * k : 128 * (k + 1)]


def load_indices(rels, zh, core, index_vmem, index_smem, sem):
    rels = jnp.concatenate([rels, jnp.zeros((16 - rels.shape[0], 128), F32)], axis=0)
    index_vmem[...] = 4 * table_row(rels.astype(jnp.int32), zh, core)
    copy = pltpu.make_async_copy(index_vmem, index_smem, sem)
    copy.start()
    return copy


def gather_relations(table_ref, index_smem, first, out_ref):
    def body(step, _):
        for j in range(4):
            for u in range(8):
                lane = step * 8 + u
                at = pl.multiple_of(index_smem[first + j, lane], 4)
                to = pl.multiple_of(512 * j + 4 * lane, 4)
                out_ref[pl.ds(to, 4), :] = table_ref[pl.ds(at, 4), :]
        return 0

    lax.fori_loop(0, 16, body, 0)
    return jnp.concatenate([out_ref[pl.ds(k, SLOTS, stride=4), :] for k in range(4)], axis=1)[:, 0:D]


def gather_heads(lists, hi, lo):
    heads = onehot_cols(lists, 0, 4, iota((128, ROWS), 1).astype(F32))
    return dot_nn(heads, hi) + dot_nn(heads, lo)


def relations_kernel(
    entity_ref, cols_ref, theirs_ref, near_ref, near2_hbm, far_hbm, far2_hbm, fetched_ref,
    rel_out, left_hi, left_lo, first_out, table_ref, entity_hi, entity_lo, cols_out,
    near2_ref, far_ref, far2_ref, far_table, gathered, index_vmem, index_smem, sem, sems,
):
    zh, core = place()
    pairs = ((near2_hbm, near2_ref), (far_hbm, far_ref), (far2_hbm, far2_ref))
    copies = [pltpu.make_async_copy(a, b, sems.at[i]) for i, (a, b) in enumerate(pairs)]
    for copy in copies:
        copy.start()
    theirs = theirs_ref[...]
    chunk = fetched_ref[pl.ds(GIVEN_CHUNK, 128, stride=CHUNK2), :].T
    rels = jnp.concatenate([cols_ref[...].T[4:8, :], theirs[4:8, :], chunk[FIRST + 4 : FIRST + 8, :]], axis=0)
    indices = load_indices(rels, zh, core, index_vmem, index_smem, sem)
    theirs = jnp.concatenate([theirs, jnp.zeros((128 - LIST, 128), F32)], axis=0).T
    cols_out[...] = theirs
    hi, lo = split2(entity_ref[...].T)
    entity_hi[...] = hi
    entity_lo[...] = lo
    head_rows = [gather_heads(lists[:, 0:LIST], hi, lo) for lists in (cols_ref, theirs)]
    store_relations(table_ref, 0, near_ref[...].T)
    copies[0].wait()
    store_relations(table_ref, REL_DEV, near2_ref[...].T)
    for k, ref in enumerate((far_ref, far2_ref)):
        copies[1 + k].wait()
        for spot in range(PIECES):
            far_table[k, piece_start(spot) : piece_start(spot) + PIECE, :] = ref[spot, 0:PIECE, :]
        store_relations(table_ref, (2 + k) * REL_DEV, far_table[k].T)
        rest = [unfold(ref[spot, PIECE : PIECE + 4, :]) for spot in range(PIECES)]
        rest = [rest[spot][:, 0:PIECE] for spot in range(PIECES - 1)] + [rest[-1][:, PIECES * PIECE - D : PIECE]]
        store_relations(table_ref, (2 + k) * REL_DEV + MAIN, jnp.concatenate(rest, axis=1))
    indices.wait()
    for k in range(2):
        rel_rows = gather_relations(table_ref, index_smem, 4 * k, gathered)
        l_hi, l_lo = split2(head_rows[k] * rel_rows)
        span = pl.ds(k * SLOTS, SLOTS)
        rel_out[span, :] = rel_rows
        left_hi[span, :] = l_hi
        left_lo[span, :] = l_lo
    first_out[...] = gather_relations(table_ref, index_smem, 8, gathered)


def fill_block(hi_ref, lo_ref, mine, theirs, first):
    for k, (rows, lane) in enumerate(((mine, 0), (mine, D), (theirs, 0), (theirs, D))):
        hi, lo = split2(rows[:, first + lane : first + lane + D])
        hi_ref[128 * k : 128 * (k + 1), :] = hi
        lo_ref[128 * k : 128 * (k + 1), :] = lo


def lists_rows(lists):
    return jnp.concatenate([lists, jnp.zeros((128, 128 - LIST), F32)], axis=1).T


def head_kernel(mine_ref, theirs_ref, lists_mine, lists_theirs, rel_ref, left_hi, left_lo, grad_ref, block_hi, block_lo):
    _, core = place()
    fill_block(block_hi, block_lo, read_rows(mine_ref, CHUNK2), read_rows(theirs_ref, CHUNK2), 0)
    numbers = jnp.bitwise_xor(iota((128, ROWS), 1), core * HALF).astype(F32)
    heads_at = iota((ROWS, 128), 0).astype(F32)
    total = None
    for k in range(2):
        lists = (lists_mine, lists_theirs)[k][:, 0:LIST]
        span = pl.ds(k * SLOTS, SLOTS)
        hi, lo = left_hi[span, :], left_lo[span, :]
        b_hi, b_lo = block_hi[...], block_lo[...]
        scores = dot3_nt(hi, lo, b_hi, b_lo)
        tails = jnp.concatenate(
            [jnp.where(lists[:, 8 + j : 9 + j] == numbers, 1.0, 0.0) for j in range(4)], axis=0
        )
        drawn = sum(jnp.where(lists[:, 12 + j : 13 + j] == numbers, 1.0, 0.0) for j in range(3))
        times = jnp.sum(drawn, axis=0, keepdims=True) + tails
        scores = jnp.where(times > 0.0, scores, -3.0e38)
        weights = times * jnp.exp(scores - jnp.max(scores, axis=1, keepdims=True))
        weights = weights / jnp.sum(weights, axis=1, keepdims=True) - tails
        w_hi, w_lo = split2(weights)
        grad_left = dot_nn(w_hi, b_lo) + dot_nn(w_lo, b_hi) + dot_nn(w_hi, b_hi)
        g_hi, g_lo = split2(grad_left * rel_ref[span, :])
        rows = lists_rows(lists)
        marks = jnp.concatenate(
            [jnp.where(rows[j : j + 1, :] == heads_at, 1.0, 0.0) for j in range(4)], axis=1
        ).astype(BF16)
        part = dot_nn(marks, g_lo) + dot_nn(marks, g_hi)
        total = part if total is None else total + part
    grad_ref[...] = total


def given_kernel(fetched_ref, out_ref):
    out_ref[...] = fetched_ref[pl.ds(GIVEN_CHUNK, 128, stride=CHUNK2), :].T[FIRST + LIST : FIRST + 2 * LIST, :]


def tail_kernel(
    mine_ref, theirs_ref, given_ref, rel_ref, entity_hi, entity_lo, table_ref, head_grad,
    keep_ref, send_ref, block_hi, block_lo, gathered, index_vmem, index_smem, sem,
):
    zh, core = place()
    mine = read_rows(mine_ref, CHUNK2)
    fill_block(block_hi, block_lo, mine, read_rows(theirs_ref, CHUNK2), 2 * D)
    indices = load_indices(given_ref[4:8, :], zh, core, index_vmem, index_smem, sem)
    e_hi, e_lo = entity_hi[...], entity_lo[...]
    numbers = jnp.bitwise_xor(iota((128, ROWS), 1), core * HALF).astype(F32)
    rows_at = iota((ROWS, 128), 0).astype(F32)
    total = head_grad[...]
    for k in range(2):
        if k == 0:
            lists = mine[:, 4 * D : 4 * D + LIST]
            rel_rows = rel_ref[...]
        else:
            lists = jnp.concatenate([given_ref[...], jnp.zeros((128 - LIST, 128), F32)], axis=0).T[:, 0:LIST]
            indices.wait()
            rel_rows = gather_relations(table_ref, index_smem, 0, gathered)
        heads = onehot_cols(lists, 0, 4, numbers)
        head_rows = dot_nn(heads, block_hi[...]) + dot_nn(heads, block_lo[...])
        l_hi, l_lo = split2(head_rows * rel_rows)
        scores = dot3_nt(e_hi, e_lo, l_hi, l_lo)
        rows = lists_rows(lists)
        tails = jnp.concatenate(
            [jnp.where(rows[8 + j : 9 + j, :] == rows_at, 1.0, 0.0) for j in range(4)], axis=1
        )
        drawn = sum(jnp.where(rows[12 + j : 13 + j, :] == rows_at, 1.0, 0.0) for j in range(3))
        times = jnp.sum(drawn, axis=1, keepdims=True) + tails
        scores = jnp.where(times > 0.0, scores, -3.0e38)
        weights = times * jnp.exp(scores - jnp.max(scores, axis=0, keepdims=True))
        weights = weights / jnp.sum(weights, axis=0, keepdims=True) - tails
        w_hi, w_lo = split2(weights)
        total = total + (dot_nn(w_lo, l_hi) + dot_nn(w_hi, l_lo) + dot_nn(w_hi, l_hi))
    first, second = total[0:HALF, :].T, total[HALF:ROWS, :].T
    keep_ref[...] = jnp.where(core == 0, first, second)
    send_ref[...] = jnp.where(core == 0, second, first)


def combine_kernel(keep_ref, sent_ref, out_ref):
    _, core = place()
    out_ref[...] = keep_ref[...] + sent_ref[1 - core]


def update_kernel(gradient_ref, entity_ref, state_ref, updated_ref, accum_ref):
    for j in range(2):
        gradient = gradient_ref[j]
        span = slice(HALF * j, HALF * (j + 1))
        accum = state_ref[:, span] + jnp.sum(gradient * gradient, axis=0, keepdims=True) / float(D)
        accum_ref[:, span] = accum
        updated_ref[:, span] = entity_ref[:, span] - LEARN_RATE * gradient / jnp.sqrt(accum)


def call(kernel, out_shape, args, vmem, scratch=(), cost=None, space=pltpu.VMEM, in_hbm=()):
    out_shape = jax.tree.map(lambda s: jax.ShapeDtypeStruct(*s), out_shape, is_leaf=lambda s: isinstance(s, tuple))
    return pl.pallas_call(
        kernel,
        out_shape=out_shape,
        in_specs=[pl.BlockSpec(memory_space=pltpu.HBM if i in in_hbm else space) for i in range(len(args))],
        out_specs=jax.tree.map(lambda _: pl.BlockSpec(memory_space=pltpu.VMEM), out_shape),
        scratch_shapes=list(scratch),
        compiler_params=pltpu.CompilerParams(vmem_limit_bytes=vmem * MIB),
        cost_estimate=cost,
        name=getattr(kernel, "func", kernel).__name__,
    )(*args)


def flops(us):
    return pl.CostEstimate(flops=int(us * 1.0e9), bytes_accessed=4_000_000, transcendentals=0)


def shards(entity, state, relation, edge_head, edge_rel, edge_tail, negatives, counts, matching):
    swap_core = functools.partial(lax.ppermute, axis_name="core", perm=[(0, 1), (1, 0)])
    swap_zh = functools.partial(lax.ppermute, axis_name="zh", perm=[(0, 1), (1, 0)])
    exchange = functools.partial(lax.all_to_all, axis_name=("x", "yz"), split_axis=0, concat_axis=0, tiled=True)
    entity_t, relation_t = entity.T, relation.T

    payload, cols, give = call(
        pack_kernel,
        [((128 * CHUNK1, 128), F32), ((128, 128), F32), ((LIST, 128), F32)],
        (entity_t, edge_head, edge_rel, edge_tail, negatives, counts.transpose(1, 2, 0)),
        vmem=60,
        scratch=[pltpu.VMEM((128, 128), F32), pltpu.VMEM((D, ROWS), F32)]
        + [pltpu.VMEM((2, 1, 1, n), jnp.int32) for n in (SLOTS, SLOTS, SLOTS, NEGS)]
        + [pltpu.VMEM((1, 1, 2), jnp.int32), pltpu.SemaphoreType.DMA((6,))],
        space=pltpu.HBM,
    )
    spread = exchange(payload.reshape(128, 1, 128 * CHUNK1)).reshape(128 * CHUNK1, 128)

    bundle = call(
        bundle_kernel,
        ((PIECE + 8, MAIN), F32),
        (relation_t,),
        vmem=60,
        scratch=[pltpu.VMEM((PIECE, REL_DEV), F32), pltpu.SemaphoreType.DMA],
        in_hbm=(0,),
    )
    give, matching = call(lists_kernel, [((LIST, 128), F32), ((2, 128), jnp.int32)], (give, matching), vmem=4)
    lines = lax.axis_size("yz") // 4
    mirror = [((4 * y + z) * 2 + h, (4 * y + 3 - z) * 2 + 1 - h) for y in range(lines) for z in range(4) for h in range(2)]
    bundle = lax.ppermute(bundle, ("yz", "zh"), perm=mirror)
    theirs = swap_zh(give)
    near2 = swap_core(relation_t)

    routed = call(
        route_kernel,
        ((128 * CHUNK2, 128), F32),
        (spread, matching),
        vmem=16,
    )
    routed, bundle, theirs = lax.optimization_barrier((routed, bundle, theirs))
    fetched = exchange(routed.reshape(128, 1, 128 * CHUNK2)).reshape(128 * CHUNK2, 128)
    far = lax.all_gather(bundle, "x", axis=0)
    far2 = swap_core(far)
    fetched_other = swap_core(fetched)
    given = swap_zh(call(given_kernel, ((LIST, 128), F32), (fetched,), vmem=4))
    gather = [
        pltpu.VMEM((4 * SLOTS, 128), F32),
        pltpu.VMEM((16, 128), jnp.int32),
        pltpu.SMEM((16, 128), jnp.int32),
        pltpu.SemaphoreType.DMA,
    ]
    rel_rows, left_hi, left_lo, first_rel, table, entity_hi, entity_lo, cols_other = call(
        relations_kernel,
        [
            ((2 * SLOTS, D), F32),
            ((2 * SLOTS, D), BF16),
            ((2 * SLOTS, D), BF16),
            ((SLOTS, D), F32),
            ((4 * TABLE, 128), F32),
            ((ROWS, D), BF16),
            ((ROWS, D), BF16),
            ((128, 128), F32),
        ],
        (entity_t, cols, theirs, relation_t, near2, far, far2, fetched),
        vmem=32,
        scratch=[pltpu.VMEM((D, REL_DEV), F32)]
        + [pltpu.VMEM((PIECES, PIECE + 8, MAIN), F32)] * 2
        + [pltpu.VMEM((2, D, MAIN), F32)]
        + gather
        + [pltpu.SemaphoreType.DMA((3,))],
        cost=flops(8),
        in_hbm=(4, 5, 6),
    )
    block = [pltpu.VMEM((ROWS, D), BF16), pltpu.VMEM((ROWS, D), BF16)]
    head_grad = call(
        head_kernel,
        ((ROWS, D), F32),
        (fetched, fetched_other, cols, cols_other, rel_rows, left_hi, left_lo),
        vmem=20,
        scratch=block,
        cost=flops(6),
    )
    keep, send = call(
        tail_kernel,
        [((D, HALF), F32)] * 2,
        (fetched, fetched_other, given, first_rel, entity_hi, entity_lo, table, head_grad),
        vmem=28,
        scratch=block + gather,
        cost=flops(9),
    )
    sent = lax.all_gather(send, "core", axis=0)
    half = call(combine_kernel, ((D, HALF), F32), (keep, sent), vmem=8)
    chips = lax.all_gather(half, "zh", axis=0)
    gradient = lax.all_gather(chips[0] + chips[1], "core", axis=0)
    updated, accum = call(
        update_kernel,
        [((D, ROWS), F32), ((1, ROWS), F32)],
        (gradient, entity_t, state.reshape(1, ROWS)),
        vmem=8,
    )
    return updated.T, accum.reshape(ROWS)


def solution(mesh):
    parts = (PIECES, mesh.shape["dom"] // PIECES, 2, 2)
    fine = jax.sharding.Mesh(mesh.devices.reshape(parts), ("x", "yz", "zh", "core"))
    dom, edge = ("x", "yz"), ("zh", "core")
    return jax.shard_map(
        shards,
        mesh=fine,
        in_specs=(
            P(dom, None),
            P(dom),
            P(edge, None),
            P(None, dom, edge, None),
            P(None, dom, edge, None),
            P(None, dom, edge, None),
            P(None, dom, edge, None),
            P(None, dom, edge),
            P(),
        ),
        out_specs=(P(dom, None), P(dom)),
        check_vma=False,
    )
```

```python
import functools

import jax
import jax.numpy as jnp
from jax import lax
from jax.experimental import pallas as pl
from jax.experimental.pallas import tpu as pltpu
from jax.sharding import PartitionSpec as P


LEARN_RATE = 0.1
D = 400
ROWS = 512
HALF = 256
SLOTS = 512
NEGS = 320
REL_DEV = 528
PIECES = 4
PIECE = 104
MAIN = 512
REST = REL_DEV - MAIN
TABLE = 4 * REL_DEV
LIST = 16
CHUNK1 = 7
CHUNK2 = 13
GIVEN_CHUNK = 12
FIRST = 4 * D - 128 * GIVEN_CHUNK
F32 = jnp.float32
BF16 = jnp.bfloat16
MIB = 1024 * 1024


def split2(x):
    hi = x.astype(BF16)
    return hi, (x - hi.astype(F32)).astype(BF16)


def split3(x):
    hi = x.astype(BF16)
    rest = x - hi.astype(F32)
    mid = rest.astype(BF16)
    return hi, mid, (rest - mid.astype(F32)).astype(BF16)


def dot_nn(a, b):
    return lax.dot_general(a, b, (((1,), (0,)), ((), ())), preferred_element_type=F32)


def dot_nt(a, b):
    return lax.dot_general(a, b, (((1,), (1,)), ((), ())), preferred_element_type=F32)


def dot3_nt(a_hi, a_lo, b_hi, b_lo):
    return dot_nt(jnp.concatenate([a_hi, a_lo, a_hi], axis=1), jnp.concatenate([b_lo, b_hi, b_hi], axis=1))


def dot3_nn(a_hi, a_lo, b_hi, b_lo):
    return dot_nn(jnp.concatenate([a_hi, a_lo, a_hi], axis=1), jnp.concatenate([b_lo, b_hi, b_hi], axis=0))


def iota(shape, dim):
    return lax.broadcasted_iota(jnp.int32, shape, dim)


def place():
    return lax.axis_index("zh"), lax.axis_index("core")


def read_rows(ref, chunks):
    return jnp.concatenate([ref[pl.ds(k, 128, stride=chunks), :] for k in range(chunks)], axis=1)


def write_rows(ref, value, chunks):
    for k in range(chunks):
        ref[pl.ds(k, 128, stride=chunks), :] = value[:, 128 * k : 128 * (k + 1)]


def onehot_cols(lists, first, count, columns):
    blocks = [(lists[:, first + j : first + j + 1] == columns) for j in range(count)]
    return jnp.concatenate([jnp.where(b, 1.0, 0.0).astype(BF16) for b in blocks], axis=0)


def pack_kernel(
    entity_hbm, head_hbm, rel_hbm, tail_hbm, neg_hbm, count_hbm, out_ref, cols_ref, give_ref,
    rows_ref, entity_ref, head_ref, rel_ref, tail_ref, neg_ref, count_ref, sems,
):
    zh, core = place()
    pairs = (
        (head_hbm, head_ref), (rel_hbm, rel_ref), (tail_hbm, tail_ref), (neg_hbm, neg_ref), (count_hbm, count_ref),
        (entity_hbm.at[:, pl.ds(pl.multiple_of(core * HALF, HALF), HALF)], entity_ref),
    )
    copies = [pltpu.make_async_copy(a, b, sems.at[i]) for i, (a, b) in enumerate(pairs)]
    for copy in copies:
        copy.start()
    rows_ref[...] = jnp.full((128, 128), -1.0, F32)
    lane = iota((1, 128), 1)
    for copy in copies[:-1]:
        copy.wait()
    for bucket in range(2):
        at = bucket * LIST
        live = count_ref[0, :, bucket : bucket + 1]
        for j in range(4):
            span = pl.ds(128 * j, 128)
            head = jnp.where(lane + 128 * j < live, head_ref[bucket, 0, 0:1, span], -1)
            rows_ref[at + j : at + j + 1, :] = head.astype(F32)
            rows_ref[at + 4 + j : at + 5 + j, :] = rel_ref[bucket, 0, 0:1, span].astype(F32)
            rows_ref[at + 8 + j : at + 9 + j, :] = tail_ref[bucket, 0, 0:1, span].astype(F32)
        rows_ref[at + 12 : at + 13, :] = neg_ref[bucket, 0, 0:1, 0:128].astype(F32)
        rows_ref[at + 13 : at + 14, :] = neg_ref[bucket, 0, 0:1, 128:256].astype(F32)
        rows_ref[at + 14 : at + 15, 0:64] = neg_ref[bucket, 0, 0:1, 256:320].astype(F32)
    one, two = rows_ref[0:LIST, :], rows_ref[LIST : 2 * LIST, :]
    keep = jnp.where(zh == 0, one, two)
    give = jnp.where(zh == 0, two, one)
    both = jnp.concatenate([keep, give, rows_ref[2 * LIST :, :]], axis=0).T
    cols_ref[...] = both
    give_ref[...] = give
    copies[-1].wait()
    half = entity_ref[...].T
    payload = jnp.concatenate([half[0:128, :], half[128:HALF, :], both[:, 0 : 128 * CHUNK1 - 2 * D]], axis=1)
    write_rows(out_ref, payload, CHUNK1)


def route_kernel(x_ref, matching_ref, out_ref):
    zh, _ = place()
    parts = split3(read_rows(x_ref, CHUNK1))
    rows = iota((128, 128), 0)
    marks = [jnp.where(matching_ref[b : b + 1, :] == rows, 1.0, 0.0) for b in range(2)]
    back_keep = jnp.where(zh == 0, marks[0], marks[1])
    back_give = jnp.where(zh == 0, marks[1], marks[0])
    marks = jnp.concatenate([back_keep.T, back_keep, back_give], axis=0).astype(BF16)
    picked = dot_nn(jnp.concatenate([marks] * 3, axis=1), jnp.concatenate(parts[::-1], axis=0))
    partner, source, given = picked[0:128], picked[128:256], picked[256:384, 768 : 128 * CHUNK1]
    fill = jnp.zeros((128, 128 * CHUNK2 - 4 * D - 2 * LIST), F32)
    routed = jnp.concatenate([partner[:, 0 : 2 * D], source[:, 0 : 2 * D + LIST], given[:, 48:64], fill], axis=1)
    write_rows(out_ref, routed, CHUNK2)


def table_row(rel, zh, core):
    owner = (rel >= REL_DEV).astype(jnp.int32) + (rel >= 2 * REL_DEV).astype(jnp.int32)
    owner = owner + (rel >= 3 * REL_DEV).astype(jnp.int32)
    off = rel - REL_DEV * owner
    owner_zh = (owner >= 2).astype(jnp.int32)
    other_core = (owner - 2 * owner_zh) != core
    return jnp.where(owner_zh == zh, 0, 2 * REL_DEV) + jnp.where(other_core, REL_DEV, 0) + off


def piece_start(spot):
    return min(PIECE * spot, D - PIECE)


def bundle_kernel(relation_hbm, out_ref, piece_ref, sem):
    spot = lax.axis_index("x")
    start = pl.multiple_of(jnp.minimum(PIECE * spot, D - PIECE), 8)
    copy = pltpu.make_async_copy(relation_hbm.at[pl.ds(start, PIECE), :], piece_ref, sem)
    copy.start()
    copy.wait()
    piece = piece_ref[...]
    out_ref[0:PIECE, :] = piece[:, 0:MAIN]
    rest = jnp.concatenate([piece[:, MAIN:REL_DEV], jnp.zeros((PIECE, 128 - REST), F32)], axis=1)
    rest = jnp.concatenate([rest, jnp.zeros((128 - PIECE, 128), F32)], axis=0).T
    for g in range(4):
        out_ref[PIECE : PIECE + 4, 128 * g : 128 * (g + 1)] = rest[4 * g : 4 * g + 4, :]
    out_ref[PIECE + 4 : PIECE + 8, :] = jnp.zeros((4, MAIN), F32)


def lists_kernel(give_ref, matching_ref, give_out, matching_out):
    give_out[...] = give_ref[...]
    matching_out[...] = matching_ref[...]


def unfold(rows):
    return jnp.concatenate([rows[:, 128 * g : 128 * (g + 1)] for g in range(4)], axis=0)


def store_relations(table_ref, first, rows):
    padded = jnp.concatenate([rows, jnp.zeros((rows.shape[0], 512 - D), F32)], axis=1)
    for k in range(4):
        table_ref[pl.ds(4 * first + k, rows.shape[0], stride=4), :] = padded[:, 128 * k : 128 * (k + 1)]


def load_indices(rels, zh, core, index_vmem, index_smem, sem):
    rels = jnp.concatenate([rels, jnp.zeros((16 - rels.shape[0], 128), F32)], axis=0)
    index_vmem[...] = 4 * table_row(rels.astype(jnp.int32), zh, core)
    copy = pltpu.make_async_copy(index_vmem, index_smem, sem)
    copy.start()
    return copy


def gather_relations(table_ref, index_smem, first, out_ref):
    def body(step, _):
        for j in range(4):
            for u in range(8):
                lane = step * 8 + u
                at = pl.multiple_of(index_smem[first + j, lane], 4)
                to = pl.multiple_of(512 * j + 4 * lane, 4)
                out_ref[pl.ds(to, 4), :] = table_ref[pl.ds(at, 4), :]
        return 0

    lax.fori_loop(0, 16, body, 0)
    return jnp.concatenate([out_ref[pl.ds(k, SLOTS, stride=4), :] for k in range(4)], axis=1)[:, 0:D]


def gather_heads(lists, hi, lo):
    heads = onehot_cols(lists, 0, 4, iota((128, ROWS), 1).astype(F32))
    return dot_nn(heads, hi) + dot_nn(heads, lo)


def relations_kernel(
    entity_ref, cols_ref, theirs_ref, near_ref, near2_hbm, far_hbm, far2_hbm, fetched_ref,
    rel_out, left_hi, left_lo, first_out, table_ref, entity_hi, entity_lo, cols_out,
    near2_ref, far_ref, far2_ref, far_table, gathered, index_vmem, index_smem, sem, sems,
):
    zh, core = place()
    pairs = ((near2_hbm, near2_ref), (far_hbm, far_ref), (far2_hbm, far2_ref))
    copies = [pltpu.make_async_copy(a, b, sems.at[i]) for i, (a, b) in enumerate(pairs)]
    for copy in copies:
        copy.start()
    theirs = theirs_ref[...]
    chunk = fetched_ref[pl.ds(GIVEN_CHUNK, 128, stride=CHUNK2), :].T
    rels = jnp.concatenate([cols_ref[...].T[4:8, :], theirs[4:8, :], chunk[FIRST + 4 : FIRST + 8, :]], axis=0)
    indices = load_indices(rels, zh, core, index_vmem, index_smem, sem)
    theirs = jnp.concatenate([theirs, jnp.zeros((128 - LIST, 128), F32)], axis=0).T
    cols_out[...] = theirs
    hi, lo = split2(entity_ref[...].T)
    entity_hi[...] = hi
    entity_lo[...] = lo
    head_rows = [gather_heads(lists[:, 0:LIST], hi, lo) for lists in (cols_ref, theirs)]
    store_relations(table_ref, 0, near_ref[...].T)
    copies[0].wait()
    store_relations(table_ref, REL_DEV, near2_ref[...].T)
    for k, ref in enumerate((far_ref, far2_ref)):
        copies[1 + k].wait()
        for spot in range(PIECES):
            far_table[k, piece_start(spot) : piece_start(spot) + PIECE, :] = ref[spot, 0:PIECE, :]
        store_relations(table_ref, (2 + k) * REL_DEV, far_table[k].T)
        rest = [unfold(ref[spot, PIECE : PIECE + 4, :]) for spot in range(PIECES)]
        rest = [rest[spot][:, 0:PIECE] for spot in range(PIECES - 1)] + [rest[-1][:, PIECES * PIECE - D : PIECE]]
        store_relations(table_ref, (2 + k) * REL_DEV + MAIN, jnp.concatenate(rest, axis=1))
    indices.wait()
    for k in range(2):
        rel_rows = gather_relations(table_ref, index_smem, 4 * k, gathered)
        l_hi, l_lo = split2(head_rows[k] * rel_rows)
        span = pl.ds(k * SLOTS, SLOTS)
        rel_out[span, :] = rel_rows
        left_hi[span, :] = l_hi
        left_lo[span, :] = l_lo
    first_out[...] = gather_relations(table_ref, index_smem, 8, gathered)


def fill_block(hi_ref, lo_ref, mine, theirs, first):
    for k, (rows, lane) in enumerate(((mine, 0), (mine, D), (theirs, 0), (theirs, D))):
        hi, lo = split2(rows[:, first + lane : first + lane + D])
        hi_ref[128 * k : 128 * (k + 1), :] = hi
        lo_ref[128 * k : 128 * (k + 1), :] = lo


def lists_rows(lists):
    return jnp.concatenate([lists, jnp.zeros((128, 128 - LIST), F32)], axis=1).T


def head_kernel(mine_ref, theirs_ref, lists_mine, lists_theirs, rel_ref, left_hi, left_lo, grad_ref, block_hi, block_lo):
    _, core = place()
    fill_block(block_hi, block_lo, read_rows(mine_ref, CHUNK2), read_rows(theirs_ref, CHUNK2), 0)
    numbers = jnp.bitwise_xor(iota((128, ROWS), 1), core * HALF).astype(F32)
    heads_at = iota((ROWS, 128), 0).astype(F32)
    total = None
    for k in range(2):
        lists = (lists_mine, lists_theirs)[k][:, 0:LIST]
        span = pl.ds(k * SLOTS, SLOTS)
        hi, lo = left_hi[span, :], left_lo[span, :]
        b_hi, b_lo = block_hi[...], block_lo[...]
        scores = dot3_nt(hi, lo, b_hi, b_lo)
        tails = jnp.concatenate(
            [jnp.where(lists[:, 8 + j : 9 + j] == numbers, 1.0, 0.0) for j in range(4)], axis=0
        )
        drawn = sum(jnp.where(lists[:, 12 + j : 13 + j] == numbers, 1.0, 0.0) for j in range(3))
        times = jnp.sum(drawn, axis=0, keepdims=True) + tails
        scores = jnp.where(times > 0.0, scores, -3.0e38)
        weights = times * jnp.exp(scores - jnp.max(scores, axis=1, keepdims=True))
        weights = weights / jnp.sum(weights, axis=1, keepdims=True) - tails
        w_hi, w_lo = split2(weights)
        grad_left = dot3_nn(w_hi, w_lo, b_hi, b_lo)
        g_hi, g_lo = split2(grad_left * rel_ref[span, :])
        rows = lists_rows(lists)
        marks = jnp.concatenate(
            [jnp.where(rows[j : j + 1, :] == heads_at, 1.0, 0.0) for j in range(4)], axis=1
        ).astype(BF16)
        part = dot_nn(marks, g_lo) + dot_nn(marks, g_hi)
        total = part if total is None else total + part
    grad_ref[...] = total


def given_kernel(fetched_ref, out_ref):
    out_ref[...] = fetched_ref[pl.ds(GIVEN_CHUNK, 128, stride=CHUNK2), :].T[FIRST + LIST : FIRST + 2 * LIST, :]


def tail_kernel(
    mine_ref, theirs_ref, given_ref, rel_ref, entity_hi, entity_lo, table_ref, head_grad,
    keep_ref, send_ref, block_hi, block_lo, gathered, index_vmem, index_smem, sem,
):
    zh, core = place()
    mine = read_rows(mine_ref, CHUNK2)
    fill_block(block_hi, block_lo, mine, read_rows(theirs_ref, CHUNK2), 2 * D)
    indices = load_indices(given_ref[4:8, :], zh, core, index_vmem, index_smem, sem)
    e_hi, e_lo = entity_hi[...], entity_lo[...]
    numbers = jnp.bitwise_xor(iota((128, ROWS), 1), core * HALF).astype(F32)
    rows_at = iota((ROWS, 128), 0).astype(F32)
    total = head_grad[...]
    for k in range(2):
        if k == 0:
            lists = mine[:, 4 * D : 4 * D + LIST]
            rel_rows = rel_ref[...]
        else:
            lists = jnp.concatenate([given_ref[...], jnp.zeros((128 - LIST, 128), F32)], axis=0).T[:, 0:LIST]
            indices.wait()
            rel_rows = gather_relations(table_ref, index_smem, 0, gathered)
        heads = onehot_cols(lists, 0, 4, numbers)
        head_rows = dot_nn(heads, block_hi[...]) + dot_nn(heads, block_lo[...])
        l_hi, l_lo = split2(head_rows * rel_rows)
        scores = dot3_nt(e_hi, e_lo, l_hi, l_lo)
        rows = lists_rows(lists)
        tails = jnp.concatenate(
            [jnp.where(rows[8 + j : 9 + j, :] == rows_at, 1.0, 0.0) for j in range(4)], axis=1
        )
        drawn = sum(jnp.where(rows[12 + j : 13 + j, :] == rows_at, 1.0, 0.0) for j in range(3))
        times = jnp.sum(drawn, axis=1, keepdims=True) + tails
        scores = jnp.where(times > 0.0, scores, -3.0e38)
        weights = times * jnp.exp(scores - jnp.max(scores, axis=0, keepdims=True))
        weights = weights / jnp.sum(weights, axis=0, keepdims=True) - tails
        w_hi, w_lo = split2(weights)
        total = total + dot3_nn(w_hi, w_lo, l_hi, l_lo)
    first, second = total[0:HALF, :].T, total[HALF:ROWS, :].T
    keep_ref[...] = jnp.where(core == 0, first, second)
    send_ref[...] = jnp.where(core == 0, second, first)


def combine_kernel(keep_ref, sent_ref, out_ref):
    _, core = place()
    out_ref[...] = keep_ref[...] + sent_ref[1 - core]


def update_kernel(gradient_ref, entity_ref, state_ref, updated_ref, accum_ref):
    for j in range(2):
        gradient = gradient_ref[j]
        span = slice(HALF * j, HALF * (j + 1))
        accum = state_ref[:, span] + jnp.sum(gradient * gradient, axis=0, keepdims=True) / float(D)
        accum_ref[:, span] = accum
        updated_ref[:, span] = entity_ref[:, span] - LEARN_RATE * gradient / jnp.sqrt(accum)


def call(kernel, out_shape, args, vmem, scratch=(), cost=None, space=pltpu.VMEM, in_hbm=()):
    out_shape = jax.tree.map(lambda s: jax.ShapeDtypeStruct(*s), out_shape, is_leaf=lambda s: isinstance(s, tuple))
    return pl.pallas_call(
        kernel,
        out_shape=out_shape,
        in_specs=[pl.BlockSpec(memory_space=pltpu.HBM if i in in_hbm else space) for i in range(len(args))],
        out_specs=jax.tree.map(lambda _: pl.BlockSpec(memory_space=pltpu.VMEM), out_shape),
        scratch_shapes=list(scratch),
        compiler_params=pltpu.CompilerParams(vmem_limit_bytes=vmem * MIB),
        cost_estimate=cost,
        name=getattr(kernel, "func", kernel).__name__,
    )(*args)


def flops(us):
    return pl.CostEstimate(flops=int(us * 1.0e9), bytes_accessed=4_000_000, transcendentals=0)


def shards(entity, state, relation, edge_head, edge_rel, edge_tail, negatives, counts, matching):
    swap_core = functools.partial(lax.ppermute, axis_name="core", perm=[(0, 1), (1, 0)])
    swap_zh = functools.partial(lax.ppermute, axis_name="zh", perm=[(0, 1), (1, 0)])
    exchange = functools.partial(lax.all_to_all, axis_name=("x", "yz"), split_axis=0, concat_axis=0, tiled=True)
    entity_t, relation_t = entity.T, relation.T

    payload, cols, give = call(
        pack_kernel,
        [((128 * CHUNK1, 128), F32), ((128, 128), F32), ((LIST, 128), F32)],
        (entity_t, edge_head, edge_rel, edge_tail, negatives, counts.transpose(1, 2, 0)),
        vmem=60,
        scratch=[pltpu.VMEM((128, 128), F32), pltpu.VMEM((D, HALF), F32)]
        + [pltpu.VMEM((2, 1, 1, n), jnp.int32) for n in (SLOTS, SLOTS, SLOTS, NEGS)]
        + [pltpu.VMEM((1, 1, 2), jnp.int32), pltpu.SemaphoreType.DMA((6,))],
        space=pltpu.HBM,
    )
    spread = exchange(payload.reshape(128, 1, 128 * CHUNK1)).reshape(128 * CHUNK1, 128)

    bundle = call(
        bundle_kernel,
        ((PIECE + 8, MAIN), F32),
        (relation_t,),
        vmem=60,
        scratch=[pltpu.VMEM((PIECE, REL_DEV), F32), pltpu.SemaphoreType.DMA],
        in_hbm=(0,),
    )
    give, matching = call(lists_kernel, [((LIST, 128), F32), ((2, 128), jnp.int32)], (give, matching), vmem=4)
    lines = lax.axis_size("yz") // 4
    mirror = [((4 * y + z) * 2 + h, (4 * y + 3 - z) * 2 + 1 - h) for y in range(lines) for z in range(4) for h in range(2)]
    bundle = lax.ppermute(bundle, ("yz", "zh"), perm=mirror)
    theirs = swap_zh(give)
    near2 = swap_core(relation_t)

    routed = call(
        route_kernel,
        ((128 * CHUNK2, 128), F32),
        (spread, matching),
        vmem=16,
    )
    routed, bundle, theirs = lax.optimization_barrier((routed, bundle, theirs))
    fetched = exchange(routed.reshape(128, 1, 128 * CHUNK2)).reshape(128 * CHUNK2, 128)
    far = lax.all_gather(bundle, "x", axis=0)
    far2 = swap_core(far)
    fetched_other = swap_core(fetched)
    given = swap_zh(call(given_kernel, ((LIST, 128), F32), (fetched,), vmem=4))
    gather = [
        pltpu.VMEM((4 * SLOTS, 128), F32),
        pltpu.VMEM((16, 128), jnp.int32),
        pltpu.SMEM((16, 128), jnp.int32),
        pltpu.SemaphoreType.DMA,
    ]
    rel_rows, left_hi, left_lo, first_rel, table, entity_hi, entity_lo, cols_other = call(
        relations_kernel,
        [
            ((2 * SLOTS, D), F32),
            ((2 * SLOTS, D), BF16),
            ((2 * SLOTS, D), BF16),
            ((SLOTS, D), F32),
            ((4 * TABLE, 128), F32),
            ((ROWS, D), BF16),
            ((ROWS, D), BF16),
            ((128, 128), F32),
        ],
        (entity_t, cols, theirs, relation_t, near2, far, far2, fetched),
        vmem=32,
        scratch=[pltpu.VMEM((D, REL_DEV), F32)]
        + [pltpu.VMEM((PIECES, PIECE + 8, MAIN), F32)] * 2
        + [pltpu.VMEM((2, D, MAIN), F32)]
        + gather
        + [pltpu.SemaphoreType.DMA((3,))],
        cost=flops(8),
        in_hbm=(4, 5, 6),
    )
    block = [pltpu.VMEM((ROWS, D), BF16), pltpu.VMEM((ROWS, D), BF16)]
    head_grad = call(
        head_kernel,
        ((ROWS, D), F32),
        (fetched, fetched_other, cols, cols_other, rel_rows, left_hi, left_lo),
        vmem=20,
        scratch=block,
        cost=flops(6),
    )
    keep, send = call(
        tail_kernel,
        [((D, HALF), F32)] * 2,
        (fetched, fetched_other, given, first_rel, entity_hi, entity_lo, table, head_grad),
        vmem=28,
        scratch=block + gather,
        cost=flops(9),
    )
    sent = lax.all_gather(send, "core", axis=0)
    half = call(combine_kernel, ((D, HALF), F32), (keep, sent), vmem=8)
    chips = lax.all_gather(half, "zh", axis=0)
    gradient = lax.all_gather(chips[0] + chips[1], "core", axis=0)
    updated, accum = call(
        update_kernel,
        [((D, ROWS), F32), ((1, ROWS), F32)],
        (gradient, entity_t, state.reshape(1, ROWS)),
        vmem=8,
    )
    return updated.T, accum.reshape(ROWS)


def solution(mesh):
    parts = (PIECES, mesh.shape["dom"] // PIECES, 2, 2)
    fine = jax.sharding.Mesh(mesh.devices.reshape(parts), ("x", "yz", "zh", "core"))
    dom, edge = ("x", "yz"), ("zh", "core")
    return jax.shard_map(
        shards,
        mesh=fine,
        in_specs=(
            P(dom, None),
            P(dom),
            P(edge, None),
            P(None, dom, edge, None),
            P(None, dom, edge, None),
            P(None, dom, edge, None),
            P(None, dom, edge, None),
            P(None, dom, edge),
            P(),
        ),
        out_specs=(P(dom, None), P(dom)),
        check_vma=False,
    )
```
